256 devices in a mesh: gx: 8 (over x, z_hi), gy: 8 (over z_lo, core), gz: 4 (over y).
Axes of the slice: x: 4, y: 4, z: 8 (z_hi: 2, z_lo: 4; z = z_hi * 4 + z_lo), core: 2. Of those that a mesh axis runs over, the one named last changes fastest.
Arguments:
- cell_index: int32 [3, 8, 8, 4, 1024], P(None, 'gx', 'gy', 'gz'), may hold values from 0 to 127, as said below
- cell_offset: float32 [3, 8, 8, 4, 1024], P(None, 'gx', 'gy', 'gz'), may hold values from 0 to 1
- radius: float32 [8, 8, 4, 1024], P('gx', 'gy', 'gz'), may hold values from 0.3 to 0.7
- forcing: float32 [3, 8, 8, 4, 1024], P(None, 'gx', 'gy', 'gz'), may hold values from -6 to 6
- viscosity: float32 [8, 8, 4, 1024], P('gx', 'gy', 'gz'), may hold values from 0.2 to 2
- occupied: int32 [8, 8, 4, 1024], P('gx', 'gy', 'gz'), may hold values 0 or 1
- base_viscosity: float32 [128, 256, 512], P('gx', 'gy', 'gz'), may hold values from 0.5 to 2
- pair_local: int32 [8, 8, 4, 4096], P('gx', 'gy', 'gz'), may hold values from 0 to 1023
- pair_owner: int32 [8, 8, 4, 4096], P('gx', 'gy', 'gz'), may hold values from 0 to 26
- pair_partner: int32 [8, 8, 4, 4096], P('gx', 'gy', 'gz'), may hold values from 0 to 1023
- pair_slot_mask: int32 [8, 8, 4, 4096], P('gx', 'gy', 'gz'), may hold values 0 or 1
Outputs:
- velocity_field: float32 [3, 128, 256, 512], P(None, 'gx', 'gy', 'gz')
- sphere_velocity: float32 [3, 8, 8, 4, 1024], P(None, 'gx', 'gy', 'gz')
The draws below stay inside these ranges and needn't reach their ends.
Inputs may be any that keep to these rules, and one draw needn't show every extreme that they name: `cell_index`: row 0 is below 16, row 1 below 32, row 2 below 128.
All inputs are finite; a program needn't handle non-finite values. No bound on the sum of `occupied` or of `pair_slot_mask` on one device may be relied on, other than what follows from the above.
Results may differ from the reference program's by a relative error of at most 0.0003.
Values sent between devices are 32-bit elements; how exact they have to be, the bound alone decides.
A program may use at most 128 MiB of HBM per device.

```python
import math
import jax
import jax.numpy as jnp
from jax import lax

CX = 16
CY = 32
CZ = 128
P_DEV = 1024
Q_DEV = 4096
SWEEPS = 4
NBX = 8
NBY = 8
NBZ = 4
NX = 128
NY = 256
NZ = 512


def draw_cell_index(key, part):
    key = jax.random.fold_in(key, 7)
    keys = jax.random.split(key, 3)
    shape = (NBX, NBY, NBZ, P_DEV)
    rows_x = jax.random.randint(keys[0], shape, 0, CX)
    rows_y = jax.random.randint(keys[1], shape, 0, CY)
    rows_z = jax.random.randint(keys[2], shape, 0, CZ)
    return jnp.stack([rows_x, rows_y, rows_z]).astype(jnp.int32)


def set_ends(values, key, smallest, top_value):
    spot = [jax.random.randint(jax.random.fold_in(key, axis), (), 0, length) for axis, length in enumerate(values.shape)]
    main_axis = values.shape.index(max(values.shape))
    neighbour = spot[:main_axis] + [(spot[main_axis] + 1) % values.shape[main_axis]] + spot[main_axis + 1:]
    return values.at[tuple(spot)].set(smallest).at[tuple(neighbour)].set(top_value)


def levels(own_key, extent, cuts, smallest, high):
    def one(dim, shards_of):
        steps = jax.random.uniform(jax.random.fold_in(jax.random.fold_in(own_key, 6), dim), (shards_of,), jnp.float32, smallest / len(cuts), high / len(cuts))
        return jnp.repeat(jnp.exp(steps), extent[dim] // shards_of).reshape((-1,) + (1,) * (len(extent) - dim - 1))

    level = one(*cuts[0])
    for cut in cuts[1:]:
        level = level * one(*cut)
    return level


def noise(stream_key, dims, scale, bound, shards=(), kind=jnp.bfloat16):
    loudness = levels(stream_key, dims, shards, -0.22, 0.18) if shards else 1.0
    values = jax.random.normal(stream_key, dims, jnp.float32) * scale * loudness
    return jnp.minimum(jnp.maximum(values, -bound), bound).astype(kind)


def setup_inputs(seed: int = 0) -> dict:
    splits = jax.random.split(jax.random.key(seed), 12)
    return {
        "cell_index": draw_cell_index(jax.random.fold_in(splits[11], 71), 0),
        "cell_offset": jnp.clip(1.0 * jax.random.uniform(splits[1], (3, NBX, NBY, NBZ, P_DEV), jnp.float32) ** levels(splits[1], (3, NBX, NBY, NBZ, P_DEV), ((1, 8), (2, 8), (3, 4)), -0.2, 0.2), 0.0, 1.0),
        "radius": jnp.clip(0.3 + 0.39999998 * jax.random.uniform(splits[2], (NBX, NBY, NBZ, P_DEV), jnp.float32) ** levels(splits[2], (NBX, NBY, NBZ, P_DEV), ((0, 8), (1, 8), (2, 4)), -0.2, 0.2), 0.3, 0.7),
        "forcing": noise(splits[3], (3, NBX, NBY, NBZ, P_DEV), 1.0, 6.0, ((1, 8), (2, 8), (3, 4)), jnp.float32),
        "viscosity": jnp.clip(jnp.exp(math.log(2.0) - 2.3025851 * jax.random.uniform(splits[4], (NBX, NBY, NBZ, P_DEV), jnp.float32) ** levels(splits[4], (NBX, NBY, NBZ, P_DEV), ((0, 8), (1, 8), (2, 4)), -0.2, 0.2)), 0.2, 2.0),
        "occupied": set_ends((jax.random.randint(splits[5], (NBX, NBY, NBZ, P_DEV), 0, 8) < 7).astype(jnp.int32), jax.random.fold_in(splits[5], 1), 0, 1),
        "base_viscosity": jnp.clip(jnp.exp(math.log(2.0) - 1.3862944 * jax.random.uniform(splits[6], (NX, NY, NZ), jnp.float32) ** levels(splits[6], (NX, NY, NZ), ((0, 8), (1, 8), (2, 4)), -0.2, 0.2)), 0.5, 2.0),
        "pair_local": set_ends(jax.random.randint(splits[7], (NBX, NBY, NBZ, Q_DEV), 0, P_DEV), jax.random.fold_in(splits[7], 1), 0, P_DEV - 1).astype(jnp.int32),
        "pair_owner": set_ends(jax.random.randint(splits[8], (NBX, NBY, NBZ, Q_DEV), 0, 27), jax.random.fold_in(splits[8], 1), 0, 26).astype(jnp.int32),
        "pair_partner": set_ends(jax.random.randint(splits[9], (NBX, NBY, NBZ, Q_DEV), 0, P_DEV), jax.random.fold_in(splits[9], 1), 0, P_DEV - 1).astype(jnp.int32),
        "pair_slot_mask": set_ends((jax.random.randint(splits[10], (NBX, NBY, NBZ, Q_DEV), 0, 4) < 3).astype(jnp.int32), jax.random.fold_in(splits[10], 1), 0, 1),
    }


spread_sigma = 0.8
damping = 0.5
lubrication_strength = 8.0
minimum_gap = 4.0

def envelope(offset):
    shifts = jnp.arange(5, dtype=jnp.float32) - 1.5
    grid_spacing = shifts.reshape((5,) + (1,) * offset.ndim) - offset[None]
    weights = jnp.exp(-grid_spacing * grid_spacing / (2.0 * spread_sigma * spread_sigma))
    return weights / lax.optimization_barrier(jnp.sum(weights, axis=0, keepdims=True))

def reference(cell_index, cell_offset, radius, forcing, viscosity, occupied, base_viscosity, pair_local, pair_owner, pair_partner, pair_slot_mask):
    brick_blocks = NBX * NBY * NBZ
    pair_count = P_DEV
    index = cell_index.reshape(3, brick_blocks, pair_count)
    offset = cell_offset.reshape(3, brick_blocks, pair_count)
    active_flags = occupied.reshape(brick_blocks * pair_count).astype(jnp.float32)
    sphere_positions = (index.astype(jnp.float32) + offset).reshape(3, brick_blocks * pair_count)
    sides = jnp.array([CX, CY, CZ], jnp.float32)
    brick_ids = jnp.arange(brick_blocks, dtype=jnp.int32)
    brick_x = brick_ids // (NBY * NBZ)
    brick_y = brick_ids // NBZ % NBY
    brick_z = brick_ids % NBZ
    owner_code = pair_owner.reshape(brick_blocks, -1)
    step_x = owner_code // 9 - 1
    step_y = owner_code // 3 % 3 - 1
    step_z = owner_code % 3 - 1
    target = ((brick_x[:, None] + step_x) % NBX * NBY + (brick_y[:, None] + step_y) % NBY) * NBZ + (brick_z[:, None] + step_z) % NBZ
    self_slot = (brick_ids[:, None] * pair_count + pair_local.reshape(brick_blocks, -1)).reshape(-1)
    distant_slot = (target * pair_count + pair_partner.reshape(brick_blocks, -1)).reshape(-1)
    flat_radius = radius.reshape(-1)
    offsets = jnp.stack([step_x, step_y, step_z]).reshape(3, -1).astype(jnp.float32)
    apart = sphere_positions[:, distant_slot] + offsets * sides[:, None] - sphere_positions[:, self_slot]
    grid_spacing = jnp.sqrt(lax.optimization_barrier(jnp.sum(apart * apart, axis=0)))
    surface_clearance = grid_spacing - flat_radius[self_slot] - flat_radius[distant_slot]
    kernel_weight = pair_slot_mask.reshape(-1).astype(jnp.float32) * active_flags[self_slot] * active_flags[distant_slot] * lubrication_strength / (jnp.maximum(grid_spacing, 1.0) * jnp.maximum(surface_clearance, minimum_gap))
    push = apart * kernel_weight[None]
    zeros = jnp.zeros((3, brick_blocks * pair_count), jnp.float32)
    total_sum = forcing.reshape(3, -1) + zeros.at[:, self_slot].add(push)
    total_sum = total_sum + zeros.at[:, distant_slot].add(-push)
    applied_loads = jnp.concatenate([total_sum * active_flags[None], (viscosity.reshape(-1) * active_flags)[None]], 0).reshape(4, brick_blocks, pair_count)
    window = jnp.arange(5, dtype=jnp.int32) - 2

    def stencil(brick):
        cells = lax.dynamic_index_in_dim(index, brick, 1, keepdims=False)
        fracs = lax.dynamic_index_in_dim(offset, brick, 1, keepdims=False)
        corner_x = brick // (NBY * NBZ) * CX
        corner_y = brick // NBZ % NBY * CY
        corner_z = brick % NBZ * CZ
        along_x = (corner_x + cells[0][:, None] + window[None]) % NX
        along_y = (corner_y + cells[1][:, None] + window[None]) % NY
        along_z = (corner_z + cells[2][:, None] + window[None]) % NZ
        flat = ((along_x[:, :, None, None] * NY + along_y[:, None, :, None]) * NZ + along_z[:, None, None, :]).reshape(-1)
        weight_x = envelope(fracs[0]).T
        weight_y = envelope(fracs[1]).T
        weight_z = envelope(fracs[2]).T
        weights = weight_x[:, :, None, None] * weight_y[:, None, :, None] * weight_z[:, None, None, :]
        return (flat, weights)

    def spread_brick(brick, grid):
        flat, weights = stencil(brick)
        load = lax.dynamic_index_in_dim(applied_loads, brick, 1, keepdims=False)
        values = (load[:, :, None, None, None] * weights[None]).reshape(4, -1)
        return grid.at[:, flat].add(values)
    grid = lax.fori_loop(0, brick_blocks, spread_brick, jnp.zeros((4, NX * NY * NZ), jnp.float32))
    drive = grid[:3].reshape(3, NX, NY, NZ)
    visco = base_viscosity + grid[3].reshape(NX, NY, NZ)
    diag = damping + 6.0 * visco
    field = jnp.zeros((3, NX, NY, NZ), jnp.float32)
    for repeat in range(SWEEPS):
        beside_all = jnp.roll(field, -1, axis=1) + jnp.roll(field, 1, axis=1)
        beside_all = beside_all + jnp.roll(field, -1, axis=2) + jnp.roll(field, 1, axis=2)
        beside_all = beside_all + jnp.roll(field, -1, axis=3) + jnp.roll(field, 1, axis=3)
        field = (drive + visco[None] * beside_all) / diag[None]
    field_flat = field.reshape(3, -1)
    active_blocks = active_flags.reshape(brick_blocks, pair_count)

    def sample_brick(brick):
        flat, weights = stencil(brick)
        picked = field_flat[:, flat].reshape(3, pair_count, 5, 5, 5)
        displaced = lax.optimization_barrier(jnp.sum(picked * weights[None], axis=(2, 3, 4)))
        return displaced * lax.dynamic_index_in_dim(active_blocks, brick, 0, keepdims=False)[None]
    displaced = lax.map(sample_brick, brick_ids)
    sphere_velocity = jnp.transpose(displaced, (1, 0, 2)).reshape(3, NBX, NBY, NBZ, pair_count)
    return (field, sphere_velocity)
```

```python
import functools
import jax
import jax.numpy as jnp
from jax import lax
from jax.experimental import pallas as pl
from jax.experimental.pallas import tpu as pltpu
from jax.sharding import PartitionSpec as P

spread_sigma = 0.8
damping = 0.5
lubrication_strength = 8.0
minimum_gap = 4.0
sharpness = 1.0 / (2.0 * spread_sigma * spread_sigma)

CX, CY, CZ = 16, 32, 128
SLOTS = 1024
PAIRS = 4096
QB = 512
REACH = 5
PLANES = 28
ROWS = 48
ROW0 = 6
BF = jnp.bfloat16
F32 = jnp.float32
NT = (((1,), (1,)), ((), ()))
NN = (((1,), (0,)), ((), ()))


def halves(value):
    high = value.astype(BF)
    return high, (value - high.astype(F32)).astype(BF)


def dot(a, b, dims):
    return lax.dot_general(a, b, dims, preferred_element_type=F32)


def iota(shape, dim):
    return lax.broadcasted_iota(jnp.int32, shape, dim)


def pairs_kernel(s_ref, zs_ref, q_ref, bucket_ref, self_ref, tab, mtab, acc):
    def parts(v):
        high = v.astype(BF).astype(F32)
        return jnp.concatenate([high, v - high], axis=0).astype(BF)

    for b in range(9):
        t = parts(s_ref[b, 0:8, :])
        for h in range(4):
            tab[pl.ds((b * 4 + h) * 16, 16), :] = t[:, h * 256:(h + 1) * 256]
    for l in range(3):
        t = parts(s_ref[4, 0:8, :] if l == 0 else zs_ref[l - 1, 0:8, :])
        for h in range(4):
            mtab[l, pl.ds(h * 16, 16), :] = t[:, h * 256:(h + 1) * 256]
    acc[...] = jnp.zeros_like(acc)
    self_ref[...] = jnp.zeros_like(self_ref)

    def step(it, carry):
        l = it // (PAIRS // QB)
        ch = it % (PAIRS // QB)
        loc = q_ref[l, 0, pl.ds(ch, 1), :]
        own = q_ref[l, 1, pl.ds(ch, 1), :]
        par = q_ref[l, 2, pl.ds(ch, 1), :]
        live = q_ref[l, 3, pl.ds(ch, 1), :]
        one = lambda c: jnp.where(c, 1, 0)
        dx = one(own >= 9) + one(own >= 18)
        rest = own - 9 * dx
        dy = one(rest >= 3) + one(rest >= 6)
        dz = rest - 3 * dy
        want = jnp.where(l == 0, 1, jnp.where(l == 1, 2, 0))
        brick = dx * 3 + dy
        high_p, low_p = par // 256, par % 256
        high_a, low_a = loc // 256, loc % 256
        rows = iota((256, QB), 0)
        hot_p = jnp.where(rows == low_p, 1.0, 0.0).astype(BF)
        hot_a = jnp.where(rows == low_a, 1.0, 0.0).astype(BF)
        found = dot(tab[...], hot_p, NN)
        slab = jnp.broadcast_to(brick * 4 + high_p, (16, QB))
        other = jnp.zeros((16, QB), F32)
        for k in range(36):
            other = other + jnp.where(slab == k, found[k * 16:(k + 1) * 16], 0.0)
        found_a = dot(mtab[l], hot_a, NN)
        slab_a = jnp.broadcast_to(high_a, (16, QB))
        mine = jnp.zeros((16, QB), F32)
        for k in range(4):
            mine = mine + jnp.where(slab_a == k, found_a[k * 16:(k + 1) * 16], 0.0)
        other = other[0:8] + other[8:16]
        mine = mine[0:8] + mine[8:16]
        diff = other - mine
        r = [
            diff[c:c + 1] + diff[3 + c:4 + c] + (code - 1).astype(F32) * float(side)
            for c, (code, side) in enumerate(((dx, CX), (dy, CY), (dz, CZ)))
        ]
        spacing = jnp.sqrt(r[0] * r[0] + r[1] * r[1] + r[2] * r[2])
        clearance = spacing - mine[6:7] - other[6:7]
        weight = (
            jnp.where(dz == want, live, 0).astype(F32) * mine[7:8] * other[7:8] * lubrication_strength
            / (jnp.maximum(spacing, 1.0) * jnp.maximum(clearance, minimum_gap))
        )
        push = [v * weight for v in r]

        def spread_rows(key, count):
            index = iota((count, QB), 0)
            out = jnp.where(index == key, push[0], 0.0)
            out = jnp.where(index == key + 4, push[1], out)
            out = jnp.where(index == key + 8, push[2], out)
            return halves(out)

        high, low = spread_rows(brick * 12 + high_p, 112)
        acc[...] -= dot(high, hot_p, NT) + dot(low, hot_p, NT)
        high, low = spread_rows(high_a, 16)
        both = dot(high, hot_a, NT) + dot(low, hot_a, NT)
        self_ref[l] += both
        return carry

    lax.fori_loop(0, 3 * (PAIRS // QB), step, 0)
    for b in range(9):
        bucket_ref[b] = acc[b * 12:(b + 1) * 12, :]


def run_pairs(spheres, z_spheres, pairs):
    return pl.pallas_call(
        pairs_kernel,
        out_shape=(
            jax.ShapeDtypeStruct((9, 12, 256), F32),
            jax.ShapeDtypeStruct((3, 16, 256), F32),
        ),
        in_specs=[pl.BlockSpec(memory_space=pltpu.VMEM)] * 3,
        out_specs=(pl.BlockSpec(memory_space=pltpu.VMEM),) * 2,
        scratch_shapes=[
            pltpu.VMEM((576, 256), BF),
            pltpu.VMEM((3, 64, 256), BF),
            pltpu.VMEM((112, 256), F32),
        ],
        compiler_params=pltpu.CompilerParams(vmem_limit_bytes=40 * 2**20),
        name="pairs",
    )(spheres, z_spheres, pairs)


def gauss(shift, offset):
    t = shift + 0.5 - offset
    return jnp.exp(-(t * t) * sharpness)


def norm(offset):
    total = gauss(-2.0, offset)
    for k in range(-1, 3):
        total = total + gauss(float(k), offset)
    return total


def window(cells, target, offset):
    shift = target.astype(F32) - cells
    return jnp.where(jnp.abs(shift) <= 2.0, gauss(shift, offset), 0.0)


X_PARTS = {-1: (0, 7), 0: (3, 20), 1: (19, 7)}
Y_PARTS = {-1: (0, 8), 0: (0, 40), 1: (32, 16)}


def spread_kernel(s_ref, load_ref, main_ref, edge_ref, send_ref, p_high, p_low):
    main_ref[...] = jnp.zeros_like(main_ref)
    edge_ref[...] = jnp.zeros_like(edge_ref)
    line = iota((128, 1), 0)
    code = line % 64
    side = code // 32
    comp = code // 8 % 4
    k = code % 8
    edge_z = jnp.where(
        line < 64,
        jnp.where(side == 0, -5 + k, 125 + k),
        jnp.where(side == 0, -3 + k, 123 + k),
    )

    def brick(dx, dy, x0, nx):
        r0, ny = Y_PARTS[dy]

        def chunk(kc, carry):
            b = (dx + 1) * 3 + (dy + 1)
            s = s_ref[b, kc]
            offs = [s[3 + c:4 + c] for c in range(3)]
            dx_cells = jnp.asarray(dx * CX, jnp.int32).astype(F32)
            wx = window(s[0:1] + dx_cells, iota((nx, 256), 0) + (x0 - REACH), offs[0])
            wy = window(s[1:2] + float(dy * CY), iota((ny, 256), 0) + (r0 - ROW0), offs[1])
            scale = s[7:8] / (norm(offs[0]) * norm(offs[1]) * norm(offs[2]))
            load = [load_ref[b, pl.ds(c * 4 + kc, 1), :] * scale for c in range(3)]
            load.append(s[8:9] * scale)
            for x in range(nx):
                high, low = halves(wx[x:x + 1] * wy)
                p_high[x * ny:(x + 1) * ny] = high
                p_low[x * ny:(x + 1) * ny] = low
            ph, pw = p_high[0:nx * ny], p_low[0:nx * ny]
            wz = window(s[2:3], iota((128, 256), 0), offs[2])
            wedge = window(s[2:3], edge_z, offs[2])
            for c in range(5):
                if c < 4:
                    d = wz * load[c]
                else:
                    d = wedge * jnp.where(
                        comp == 0, load[0], jnp.where(comp == 1, load[1], jnp.where(comp == 2, load[2], load[3]))
                    )
                dh, dl = halves(d)
                res = dot(ph, dh, NT) + dot(pw, dh, NT) + dot(ph, dl, NT)
                res = res.reshape(nx, ny, 128)
                if c < 4:
                    main_ref[c, pl.ds(x0, nx), r0:r0 + ny, :] += res
                else:
                    edge_ref[pl.ds(x0, nx), r0:r0 + ny, :] += res
            return carry

        lax.fori_loop(0, 4, chunk, 0)

    def sided(it, carry):
        dx = 2 * it - 1
        x0 = it * 19
        for dy in (-1, 0, 1):
            brick(dx, dy, x0, 7)
        return carry

    for dy in (-1, 0, 1):
        brick(0, dy, 3, 20)
    lax.fori_loop(0, 2, sided, 0)

    lane = iota((ROWS, 128), 1)

    def pack(g, carry):
        for s in range(2):
            out = jnp.zeros((ROWS, 128), F32)
            for j in range(4):
                rolled = pltpu.roll(edge_ref[g * 4 + j], (32 * j - 64 - 32 * s) % 128, 1) if (32 * j - 64 - 32 * s) % 128 else edge_ref[g * 4 + j]
                out = jnp.where(lane // 32 == j, rolled, out)
            send_ref[s, g] = out
        return carry

    lax.fori_loop(0, PLANES // 4, pack, 0)


def run_spread(spheres, loads):
    return pl.pallas_call(
        spread_kernel,
        out_shape=(
            jax.ShapeDtypeStruct((4, PLANES, ROWS, 128), F32),
            jax.ShapeDtypeStruct((PLANES, ROWS, 128), F32),
            jax.ShapeDtypeStruct((2, PLANES // 4, ROWS, 128), F32),
        ),
        in_specs=[pl.BlockSpec(memory_space=pltpu.VMEM)] * 2,
        out_specs=(pl.BlockSpec(memory_space=pltpu.VMEM),) * 3,
        scratch_shapes=[pltpu.VMEM((800, 256), BF), pltpu.VMEM((800, 256), BF)],
        compiler_params=pltpu.CompilerParams(vmem_limit_bytes=48 * 2**20),
        name="spread",
    )(spheres, loads)


def roll(value, shift, axis):
    shift = shift % value.shape[axis]
    return pltpu.roll(value, shift, axis) if shift else value


def sweep_kernel(
    main_ref, edge_ref, low_ref, high_ref, base_ref, base_edge_ref, s_ref,
    out_ref, vel_ref,
    ua, ub, ha, hb, drive, visco, inv, hdrive, hvisco, hinv, lh, ll,
):
    lane = iota((ROWS, 128), 1)
    comp = lane // 8 % 4

    def start(g, carry):
        from_low, from_high = low_ref[g], high_ref[g]
        for j in range(4):
            i = g * 4 + j
            got = jnp.where(lane < 32, roll(from_low, -32 * j, 1), 0.0)
            got = jnp.where(lane // 32 == 1, roll(from_high, 32 - 32 * j, 1), got)
            total = jnp.where(lane < 64, edge_ref[i], 0.0) + got
            v = total + base_edge_ref[i]
            v = jnp.where(
                comp == 3, v, jnp.where(comp == 2, roll(v, -8, 1), jnp.where(comp == 1, roll(v, -16, 1), roll(v, -24, 1)))
            )
            hvisco[i] = v
            r = 1.0 / (damping + 6.0 * v)
            hinv[i] = r
            hdrive[i] = total
            ha[i] = total * r
            m = []
            for c in range(4):
                near = jnp.where(lane < 2, roll(got, -(c * 8 + 5), 1), 0.0)
                near = jnp.where(lane >= 126, roll(got, 93 - 8 * c, 1), near)
                m.append(main_ref[c, i] + near)
            v = m[3] + base_ref[i]
            visco[i] = v
            r = 1.0 / (damping + 6.0 * v)
            inv[i] = r
            for c in range(3):
                drive[c, i] = m[c]
                ua[c, i] = m[c] * r
        return carry

    lax.fori_loop(0, PLANES // 4, start, 0)

    def sweep(src, dst, hsrc, hdst, first):
        def plane(i, carry):
            h = hsrc[i]
            beside = hsrc[i - 1] + hsrc[i + 1] + roll(h, 1, 0) + roll(h, -1, 0) + roll(h, 1, 1) + roll(h, -1, 1)
            hdst[i] = (hdrive[i] + hvisco[i] * beside) * hinv[i]
            v, r = visco[i], inv[i]
            for c in range(3):
                u = src[c, i]
                before = jnp.where(lane == 0, roll(h, -(c * 8 + 4), 1), roll(u, 1, 1))
                after = jnp.where(lane == 127, roll(h, 92 - 8 * c, 1), roll(u, -1, 1))
                beside = src[c, i - 1] + src[c, i + 1] + roll(u, 1, 0) + roll(u, -1, 0) + before + after
                dst[c, i] = (drive[c, i] + v * beside) * r
            return carry

        lax.fori_loop(first, 26 - first, plane, 0)

    sweep(ua, ub, ha, hb, 1)
    sweep(ub, ua, hb, ha, 2)
    sweep(ua, ub, ha, hb, 3)

    def finish(x, carry):
        for c in range(3):
            out_ref[c, x] = ub[c, x + REACH, ROW0:ROW0 + CY, :]
        return carry

    lax.fori_loop(0, CX, finish, 0)

    comp40 = comp[0:40]

    def gather_rows(x, carry):
        h = hb[x + 3, 0:40, :]
        at = pl.multiple_of(x * 40, 40)
        for c in range(3):
            row = jnp.concatenate([ub[c, x + 3, 0:40, :], jnp.where(comp40 == c, h, 0.0)], axis=1)
            high, low = halves(row)
            lh[c, x] = high.reshape(40, 256)
            ll[c, x] = low.reshape(40, 256)
        return carry

    lax.fori_loop(0, 20, gather_rows, 0)
    line = iota((256, 1), 0)
    code = line - 128
    zed = jnp.where(code < 32, -5 + code % 8, 125 + code % 8)
    zed = jnp.where((zed >= 0) & (zed < CZ) | (code >= 64), -1000, zed)
    zed = jnp.where(line < 128, line, zed)

    for pc in range(4):
        s = s_ref[:, pc * 256:(pc + 1) * 256]
        offs = [s[3 + c:4 + c] for c in range(3)]
        wx = window(s[0:1], iota((20, 256), 0) - 2, offs[0])
        wy = window(s[1:2], iota((40, 256), 0) - ROW0, offs[1])
        wh, wl = halves(window(s[2:3], zed, offs[2]))
        scale = s[7:8] / (norm(offs[0]) * norm(offs[1]) * norm(offs[2]))
        for c in range(3):
            a, b = lh[c].reshape(800, 256), ll[c].reshape(800, 256)
            g = dot(a, wh, NN) + dot(b, wh, NN) + dot(a, wl, NN)
            t = jnp.zeros((40, 256), F32)
            for x in range(20):
                t = t + wx[x:x + 1] * g[x * 40:(x + 1) * 40]
            vel_ref[c:c + 1, pc * 256:(pc + 1) * 256] = jnp.sum(t * wy, axis=0, keepdims=True) * scale


def run_sweeps(main, edge, low, high, base, base_edge, sphere):
    field = lambda *lead: pltpu.VMEM(lead + (PLANES, ROWS, 128), F32)
    return pl.pallas_call(
        sweep_kernel,
        out_shape=(
            jax.ShapeDtypeStruct((3, CX, CY, CZ), F32),
            jax.ShapeDtypeStruct((3, SLOTS), F32),
        ),
        in_specs=[pl.BlockSpec(memory_space=pltpu.VMEM)] * 7,
        out_specs=(pl.BlockSpec(memory_space=pltpu.VMEM),) * 2,
        scratch_shapes=[
            field(3), field(3), field(), field(), field(3), field(), field(), field(), field(), field(),
            pltpu.VMEM((3, 20, 40, 256), BF), pltpu.VMEM((3, 20, 40, 256), BF),
        ],
        compiler_params=pltpu.CompilerParams(vmem_limit_bytes=56 * 2**20),
        name="sweeps",
    )(main, edge, low, high, base, base_edge, sphere)


def shift(value, axis, step):
    size = lax.axis_size(axis)
    return lax.ppermute(value, axis, [(i, (i + step) % size) for i in range(size)])


def around(value, axis, dim):
    return jnp.concatenate([shift(value, axis, 1), value, shift(value, axis, -1)], axis=dim)


def halo(array, axis, dim, width):
    n = array.shape[dim]
    before = shift(lax.slice_in_dim(array, n - width, n, axis=dim), axis, 1)
    after = shift(lax.slice_in_dim(array, 0, width, axis=dim), axis, -1)
    return before, after


def body(
    cell_index, cell_offset, radius, forcing, viscosity, occupied, base_viscosity,
    pair_local, pair_owner, pair_partner, pair_slot_mask,
):
    row = lambda a: a.reshape(-1, SLOTS)
    sphere = jnp.concatenate(
        [
            row(cell_index).astype(F32), row(cell_offset), row(radius),
            row(occupied).astype(F32), row(viscosity),
        ],
        0,
    )
    pairs = jnp.stack(
        [a.reshape(PAIRS // QB, QB) for a in (pair_local, pair_owner, pair_partner, pair_slot_mask)]
    )
    spheres = around(around(sphere[None], "gx", 0)[:, None], "gy", 1).reshape(9, 9, SLOTS)
    z_spheres = jnp.stack([shift(sphere[:8], "gz", 1), shift(sphere[:8], "gz", -1)])
    all_pairs = jnp.stack([pairs, shift(pairs, "gz", 1), shift(pairs, "gz", -1)])

    before, after = halo(base_viscosity, "gx", 0, REACH)
    base = jnp.concatenate([before, base_viscosity, after], 0)
    before, after = halo(base, "gy", 1, REACH)
    base = jnp.concatenate([before, base, after], 1)
    base = jnp.pad(base, ((0, PLANES - 26), (ROW0 - REACH, ROWS - ROW0 - REACH - CY), (0, 0)))
    before, after = halo(base, "gz", 2, REACH)
    blank = lambda n: jnp.zeros((PLANES, ROWS, n), F32)
    base_edge = jnp.concatenate(
        [blank(24), before, base[:, :, 0:3], blank(24), base[:, :, CZ - 3:CZ], after, blank(64)], 2
    )

    bucket, selves = run_pairs(spheres, z_spheres, all_pairs)
    selves = selves[:, :12]
    bucket = bucket.reshape(3, 3, 12, 256)
    bucket = bucket[:, 1] + shift(bucket[:, 2], "gy", 1) + shift(bucket[:, 0], "gy", -1)
    total = bucket[1] + shift(bucket[2], "gx", 1) + shift(bucket[0], "gx", -1)
    total = total + forcing.reshape(12, 256) + selves[0] + shift(selves[1], "gz", -1) + shift(selves[2], "gz", 1)
    loads = around(around(total[None], "gx", 0)[:, None], "gy", 1).reshape(9, 12, 256)

    chunked = spheres.reshape(9, 9, 4, 256).transpose(0, 2, 1, 3)
    main, edge, send = run_spread(chunked, loads)
    high = shift(send[0], "gz", -1)
    low = shift(send[1], "gz", 1)
    field, velocity = run_sweeps(main, edge, low, high, base, base_edge, sphere)
    return field, velocity.reshape(3, 1, 1, 1, SLOTS)


def solution(mesh):
    line = P("gx", "gy", "gz", None)
    wide = P(None, "gx", "gy", "gz", None)
    placed = (wide, wide, line, wide, line, line, P("gx", "gy", "gz"), line, line, line, line)
    return jax.shard_map(
        body,
        mesh=mesh,
        in_specs=placed,
        out_specs=(P(None, "gx", "gy", "gz"), wide),
        check_vma=False,
    )
```

```python
import functools
import jax
import jax.numpy as jnp
from jax import lax
from jax.experimental import pallas as pl
from jax.experimental.pallas import tpu as pltpu
from jax.sharding import PartitionSpec as P

spread_sigma = 0.8
damping = 0.5
lubrication_strength = 8.0
minimum_gap = 4.0
sharpness = 1.0 / (2.0 * spread_sigma * spread_sigma)

CX, CY, CZ = 16, 32, 128
SLOTS = 1024
PAIRS = 4096
QB = 512
REACH = 5
PLANES = 28
ROWS = 48
ROW0 = 6
BF = jnp.bfloat16
F32 = jnp.float32
NT = (((1,), (1,)), ((), ()))
NN = (((1,), (0,)), ((), ()))


def halves(value):
    high = value.astype(BF)
    return high, (value - high.astype(F32)).astype(BF)


def dot(a, b, dims):
    return lax.dot_general(a, b, dims, preferred_element_type=F32)


def iota(shape, dim):
    return lax.broadcasted_iota(jnp.int32, shape, dim)


def gauss(shift, offset):
    t = shift + 0.5 - offset
    return jnp.exp(-(t * t) * sharpness)


def norm(offset):
    total = gauss(-2.0, offset)
    for k in range(-1, 3):
        total = total + gauss(float(k), offset)
    return total


def window(cells, target, offset):
    shift = target.astype(F32) - cells
    return jnp.where(jnp.abs(shift) <= 2.0, gauss(shift, offset), 0.0)


def roll(value, shift, axis):
    shift = shift % value.shape[axis]
    return pltpu.roll(value, shift, axis) if shift else value


X_PARTS = {-1: (0, 7), 0: (3, 20), 1: (19, 7)}
Y_PARTS = {-1: (0, 8), 0: (0, 40), 1: (32, 16)}


def pair_forces(s, zs, q, acc, selves, tab, mtab):
    def parts(v):
        high = v.astype(BF).astype(F32)
        return jnp.concatenate([high, v - high], axis=0).astype(BF)

    def fill(n, carry):
        tab[pl.ds(pl.multiple_of(n * 16, 16), 16), :] = parts(s[n // 4, n % 4])
        return carry

    lax.fori_loop(0, 36, fill, 0)
    for h in range(4):
        mtab[0, h * 16:(h + 1) * 16] = parts(s[4, h])
        mtab[1, h * 16:(h + 1) * 16] = parts(zs[0, h])
        mtab[2, h * 16:(h + 1) * 16] = parts(zs[1, h])
    acc[...] = jnp.zeros_like(acc)
    selves[...] = jnp.zeros_like(selves)

    def step(it, carry):
        l = it // (PAIRS // QB)
        ch = it % (PAIRS // QB)
        loc = q[l, 0, pl.ds(ch, 1), :]
        own = q[l, 1, pl.ds(ch, 1), :]
        par = q[l, 2, pl.ds(ch, 1), :]
        live = q[l, 3, pl.ds(ch, 1), :]
        one = lambda c: jnp.where(c, 1, 0)
        dx = one(own >= 9) + one(own >= 18)
        rest = own - 9 * dx
        dy = one(rest >= 3) + one(rest >= 6)
        dz = rest - 3 * dy
        want = jnp.where(l == 0, 1, jnp.where(l == 1, 2, 0))
        brick = dy * 3 + dx
        high_p, low_p = par // 256, par % 256
        high_a, low_a = loc // 256, loc % 256
        rows = iota((256, QB), 0)
        hot_p = jnp.where(rows == low_p, 1.0, 0.0).astype(BF)
        hot_a = jnp.where(rows == low_a, 1.0, 0.0).astype(BF)
        found = dot(tab[...], hot_p, NN)
        slab = jnp.broadcast_to(brick * 4 + high_p, (16, QB))
        other = jnp.zeros((16, QB), F32)
        for k in range(36):
            other = other + jnp.where(slab == k, found[k * 16:(k + 1) * 16], 0.0)
        found_a = dot(mtab[l], hot_a, NN)
        slab_a = jnp.broadcast_to(high_a, (16, QB))
        mine = jnp.zeros((16, QB), F32)
        for k in range(4):
            mine = mine + jnp.where(slab_a == k, found_a[k * 16:(k + 1) * 16], 0.0)
        other = other[0:8] + other[8:16]
        mine = mine[0:8] + mine[8:16]
        diff = other - mine
        r = [
            diff[c:c + 1] + diff[3 + c:4 + c] + (code - 1).astype(F32) * float(side)
            for c, (code, side) in enumerate(((dx, CX), (dy, CY), (dz, CZ)))
        ]
        spacing = jnp.sqrt(r[0] * r[0] + r[1] * r[1] + r[2] * r[2])
        clearance = spacing - mine[6:7] - other[6:7]
        weight = (
            jnp.where(dz == want, live, 0).astype(F32) * mine[7:8] * other[7:8] * lubrication_strength
            / (jnp.maximum(spacing, 1.0) * jnp.maximum(clearance, minimum_gap))
        )
        push = [v * weight for v in r]

        def spread_rows(key, count):
            index = iota((count, QB), 0)
            out = jnp.where(index == key, push[0], 0.0)
            out = jnp.where(index == key + 4, push[1], out)
            out = jnp.where(index == key + 8, push[2], out)
            return halves(out)

        high, low = spread_rows(brick * 12 + high_p, 112)
        acc[...] -= dot(high, hot_p, NT) + dot(low, hot_p, NT)
        high, low = spread_rows(high_a, 16)
        selves[l] += dot(high, hot_a, NT) + dot(low, hot_a, NT)
        return carry

    lax.fori_loop(0, 3 * (PAIRS // QB), step, 0)


def spread_brick(s, loads, main, edge, p_high, p_low, dx, dy, x0, nx):
    r0, ny = Y_PARTS[dy]
    line = iota((128, 1), 0)
    code = line % 64
    side = code // 32
    comp = code // 8 % 4
    k = code % 8
    edge_z = jnp.where(
        line < 64,
        jnp.where(side == 0, -5 + k, 125 + k),
        jnp.where(side == 0, -3 + k, 123 + k),
    )
    b = (dy + 1) * 3 + (dx + 1)

    def chunk(kc, carry):
        v = s[b, kc]
        offs = [v[3 + c:4 + c] for c in range(3)]
        dx_cells = jnp.asarray(dx * CX, jnp.int32).astype(F32)
        wx = window(v[0:1] + dx_cells, iota((nx, 256), 0) + (x0 - REACH), offs[0])
        wy = window(v[1:2] + float(dy * CY), iota((ny, 256), 0) + (r0 - ROW0), offs[1])
        scale = 1.0 / (norm(offs[0]) * norm(offs[1]) * norm(offs[2]))
        load = [loads[b, pl.ds(c * 4 + kc, 1), :] * scale for c in range(4)]
        for x in range(nx):
            high, low = halves(wx[x:x + 1] * wy)
            p_high[x * ny:(x + 1) * ny] = high
            p_low[x * ny:(x + 1) * ny] = low
        ph, pw = p_high[0:nx * ny], p_low[0:nx * ny]
        wz = window(v[2:3], iota((128, 256), 0), offs[2])
        wedge = window(v[2:3], edge_z, offs[2])
        for c in range(5):
            if c < 4:
                d = wz * load[c]
            else:
                d = wedge * jnp.where(
                    comp == 0, load[0], jnp.where(comp == 1, load[1], jnp.where(comp == 2, load[2], load[3]))
                )
            dh, dl = halves(d)
            res = dot(ph, dh, NT) + dot(pw, dh, NT) + dot(ph, dl, NT)
            res = res.reshape(nx, ny, 128)
            if c < 4:
                main[c, pl.ds(x0, nx), r0:r0 + ny, :] += res
            else:
                edge[pl.ds(x0, nx), r0:r0 + ny, :] += res
        return carry

    lax.fori_loop(0, 4, chunk, 0)


def assemble_base(bx, by, i):
    rows = jnp.concatenate([by[0, i], bx[i], by[1, i]], axis=0)
    return pltpu.roll(rows, ROWS - (8 - ROW0), 0)


def exchange_kernel(
    cell_ref, offset_ref, radius_ref, force_ref, visc_ref, live_ref, base_ref,
    local_ref, owner_ref, partner_ref, mask_ref,
    main, edge, rim, bx_out, by_out, own_ref,
    s, zs, q, acc, selves, tab, mtab, ry, rz, xb, rx, loads, pack, force, got, p_high, p_low,
    bx, by, send_sem, recv_sem,
):
    me = {a: lax.axis_index(a) for a in ("gx", "gy", "gz")}

    def near(axis, step):
        n = lax.axis_size(axis)
        return {axis: lax.rem(me[axis] + step + n, n)}

    barrier = pltpu.get_barrier_semaphore()
    for axis in ("gx", "gy", "gz"):
        for step in (1, -1):
            pl.semaphore_signal(barrier, inc=1, device_id=near(axis, step), device_id_type=pl.DeviceIdType.MESH)

    count = [0]

    def copy(src, dst, axis, step):
        n = count[0]
        count[0] += 1
        return pltpu.make_async_remote_copy(
            src_ref=src, dst_ref=dst, send_sem=send_sem.at[n], recv_sem=recv_sem.at[n],
            device_id=near(axis, step), device_id_type=pl.DeviceIdType.MESH,
        )

    rows = [cell_ref[c, 0, 0].astype(F32) for c in range(3)] + [offset_ref[c, 0, 0] for c in range(3)]
    rows += [radius_ref[0, 0], live_ref[0, 0].astype(F32)]
    for r, v in enumerate(rows):
        for h in range(4):
            s[4, h, r:r + 1, :] = v[:, h * 256:(h + 1) * 256]
    for j, ref in enumerate((local_ref, owner_ref, partner_ref, mask_ref)):
        for ch in range(PAIRS // QB):
            q[0, j, ch:ch + 1, :] = ref[0, 0, :, ch * QB:(ch + 1) * QB]
    bx[REACH:REACH + CX] = base_ref[...]
    bx[26:28] = jnp.zeros((2, CY, CZ), F32)

    pl.semaphore_wait(barrier, 6)

    s_x = [copy(s.at[4], s.at[3], "gx", 1), copy(s.at[4], s.at[5], "gx", -1)]
    s_z = [copy(s.at[4], zs.at[0], "gz", 1), copy(s.at[4], zs.at[1], "gz", -1)]
    q_z = [copy(q.at[0], q.at[1], "gz", 1), copy(q.at[0], q.at[2], "gz", -1)]
    b_x = [
        copy(bx.at[pl.ds(CX, REACH)], bx.at[pl.ds(0, REACH)], "gx", 1),
        copy(bx.at[pl.ds(REACH, REACH)], bx.at[pl.ds(CX + REACH, REACH)], "gx", -1),
    ]
    s_y = [copy(s.at[pl.ds(3, 3)], s.at[pl.ds(0, 3)], "gy", 1), copy(s.at[pl.ds(3, 3)], s.at[pl.ds(6, 3)], "gy", -1)]
    b_y = [
        copy(bx.at[:, pl.ds(CY - 8, 8)], by.at[0], "gy", 1),
        copy(bx.at[:, pl.ds(0, 8)], by.at[1], "gy", -1),
    ]
    a_y = [copy(acc.at[pl.ds(72, 40)], ry.at[0], "gy", 1), copy(acc.at[pl.ds(0, 40)], ry.at[1], "gy", -1)]
    a_z = [copy(selves.at[1], rz.at[0], "gz", -1), copy(selves.at[2], rz.at[1], "gz", 1)]
    a_x = [copy(xb.at[1], rx.at[0], "gx", 1), copy(xb.at[0], rx.at[1], "gx", -1)]
    l_x = [copy(loads.at[4], loads.at[3], "gx", 1), copy(loads.at[4], loads.at[5], "gx", -1)]
    l_y = [
        copy(loads.at[pl.ds(3, 3)], loads.at[pl.ds(0, 3)], "gy", 1),
        copy(loads.at[pl.ds(3, 3)], loads.at[pl.ds(6, 3)], "gy", -1),
    ]
    e_z = [copy(pack.at[0], got.at[1], "gz", -1), copy(pack.at[1], got.at[0], "gz", 1)]

    def start(copies):
        for c in copies:
            c.start()

    def arrived(copies):
        for c in copies:
            c.wait_recv()

    start(s_x)
    start(s_z)
    start(q_z)
    start(b_x)

    own_ref[...] = s[4]
    force[...] = jnp.zeros_like(force)
    loads[4] = jnp.zeros((16, 256), F32)
    for c in range(3):
        for h in range(4):
            force[c * 4 + h:c * 4 + h + 1, :] = force_ref[c, 0, 0, :, h * 256:(h + 1) * 256]
    thick = visc_ref[0, 0] * live_ref[0, 0].astype(F32)
    for h in range(4):
        force[12 + h:13 + h, :] = thick[:, h * 256:(h + 1) * 256]
    main[...] = jnp.zeros_like(main)
    edge[...] = jnp.zeros_like(edge)

    arrived(s_x)
    start(s_y)
    arrived(b_x)
    start(b_y)
    arrived(s_z)
    arrived(q_z)
    arrived(s_y)

    pair_forces(s, zs, q, acc, selves, tab, mtab)

    start(a_y)
    start(a_z)
    arrived(a_y)
    middle = acc[36:72] + ry[0, 0:36] + ry[1, 0:36]
    xb[...] = jnp.zeros_like(xb)
    xb[0, 0:12] = middle[0:12]
    xb[1, 0:12] = middle[24:36]
    start(a_x)
    arrived(a_z)
    force[0:12] += middle[12:24] + selves[0, 0:12] + rz[0, 0:12] + rz[1, 0:12]
    arrived(a_x)
    for h in range(4):
        alive = s[4, h, 7:8, :]
        for c in range(3):
            at = c * 4 + h
            loads[4, at:at + 1, :] = alive * (force[at:at + 1] + rx[0, at:at + 1] + rx[1, at:at + 1])
        loads[4, 12 + h:13 + h, :] = force[12 + h:13 + h]
    start(l_x)

    put = functools.partial(spread_brick, s, loads, main, edge, p_high, p_low)
    put(0, 0, 3, 20)
    arrived(l_x)
    start(l_y)
    lax.fori_loop(0, 2, lambda it, carry: (put(2 * it - 1, 0, it * 19, 7), carry)[1], 0)
    arrived(l_y)
    for dy in (-1, 1):
        put(0, dy, 3, 20)
        lax.fori_loop(0, 2, lambda it, carry: (put(2 * it - 1, dy, it * 19, 7), carry)[1], 0)

    arrived(b_y)
    lane = iota((ROWS, 128), 1)

    def wrap(g, carry):
        tiles = []
        for j in range(4):
            i = g * 4 + j
            b = assemble_base(bx, by, i)
            t = edge[i]
            t = t + jnp.where((lane >= 29) & (lane < 32), roll(b, 29, 1), 0.0)
            t = t + jnp.where((lane >= 56) & (lane < 59), roll(b, 56 - 125, 1), 0.0)
            t = t + jnp.where((lane >= 91) & (lane < 96), roll(b, 91, 1), 0.0)
            t = t + jnp.where((lane >= 120) & (lane < 125), roll(b, 120 - 123, 1), 0.0)
            edge[i] = t
            tiles.append(t)
        for side in range(2):
            out = jnp.zeros((ROWS, 128), F32)
            for j in range(4):
                out = jnp.where(lane // 32 == j, roll(tiles[j], 32 * j - 64 - 32 * side, 1), out)
            pack[side, g] = out
        return carry

    lax.fori_loop(0, PLANES // 4, wrap, 0)
    start(e_z)
    arrived(e_z)
    rim[...] = got[...]
    bx_out[...] = bx[...]
    by_out[...] = by[...]
    for group in (s_x, s_z, q_z, b_x, s_y, b_y, a_y, a_z, a_x, l_x, l_y, e_z):
        for c in group:
            c.wait_send()


def run_exchange(*args):
    vmem = pl.BlockSpec(memory_space=pltpu.VMEM)
    shape = lambda *s: jax.ShapeDtypeStruct(s, F32)
    return pl.pallas_call(
        exchange_kernel,
        out_shape=(
            shape(4, PLANES, ROWS, 128),
            shape(PLANES, ROWS, 128),
            shape(2, PLANES // 4, ROWS, 128),
            shape(PLANES, CY, CZ),
            shape(2, PLANES, 8, CZ),
            shape(4, 8, 256),
        ),
        in_specs=[vmem] * 11,
        out_specs=(vmem,) * 6,
        scratch_shapes=[
            pltpu.VMEM((9, 4, 8, 256), F32),
            pltpu.VMEM((2, 4, 8, 256), F32),
            pltpu.VMEM((3, 4, PAIRS // QB, QB), jnp.int32),
            pltpu.VMEM((112, 256), F32),
            pltpu.VMEM((3, 16, 256), F32),
            pltpu.VMEM((576, 256), BF),
            pltpu.VMEM((3, 64, 256), BF),
            pltpu.VMEM((2, 40, 256), F32),
            pltpu.VMEM((2, 16, 256), F32),
            pltpu.VMEM((2, 16, 256), F32),
            pltpu.VMEM((2, 16, 256), F32),
            pltpu.VMEM((9, 16, 256), F32),
            pltpu.VMEM((2, PLANES // 4, ROWS, 128), F32),
            pltpu.VMEM((16, 256), F32),
            pltpu.VMEM((2, PLANES // 4, ROWS, 128), F32),
            pltpu.VMEM((800, 256), BF),
            pltpu.VMEM((800, 256), BF),
            pltpu.VMEM((PLANES, CY, CZ), F32),
            pltpu.VMEM((2, PLANES, 8, CZ), F32),
            pltpu.SemaphoreType.DMA((24,)),
            pltpu.SemaphoreType.DMA((24,)),
        ],
        compiler_params=pltpu.CompilerParams(
            collective_id=0, has_side_effects=True, vmem_limit_bytes=48 * 2**20
        ),
        name="exchange",
    )(*args)


def sweep_kernel(
    main_ref, edge_ref, rim_ref, bx_ref, by_ref, s_ref,
    out_ref, vel_ref,
    ua, ub, ha, hb, drive, visco, inv, hdrive, hvisco, hinv, lh, ll,
):
    lane = iota((ROWS, 128), 1)
    comp = lane // 8 % 4

    def start(g, carry):
        from_low, from_high = rim_ref[0, g], rim_ref[1, g]
        for j in range(4):
            i = g * 4 + j
            got = jnp.where(lane < 32, roll(from_low, -32 * j, 1), 0.0)
            got = jnp.where(lane // 32 == 1, roll(from_high, 32 - 32 * j, 1), got)
            total = jnp.where(lane < 64, edge_ref[i], 0.0) + got
            v = total
            v = jnp.where(
                comp == 3, v, jnp.where(comp == 2, roll(v, -8, 1), jnp.where(comp == 1, roll(v, -16, 1), roll(v, -24, 1)))
            )
            hvisco[i] = v
            r = 1.0 / (damping + 6.0 * v)
            hinv[i] = r
            hdrive[i] = total
            ha[i] = total * r
            m = []
            for c in range(4):
                near = jnp.where(lane < 2, roll(got, -(c * 8 + 5), 1), 0.0)
                near = jnp.where(lane >= 126, roll(got, 93 - 8 * c, 1), near)
                m.append(main_ref[c, i] + near)
            v = m[3] + assemble_base(bx_ref, by_ref, i)
            visco[i] = v
            r = 1.0 / (damping + 6.0 * v)
            inv[i] = r
            for c in range(3):
                drive[c, i] = m[c]
                ua[c, i] = m[c] * r
        return carry

    lax.fori_loop(0, PLANES // 4, start, 0)

    def sweep(src, dst, hsrc, hdst, first):
        def plane(i, carry):
            h = hsrc[i]
            beside = hsrc[i - 1] + hsrc[i + 1] + roll(h, 1, 0) + roll(h, -1, 0) + roll(h, 1, 1) + roll(h, -1, 1)
            hdst[i] = (hdrive[i] + hvisco[i] * beside) * hinv[i]
            v, r = visco[i], inv[i]
            for c in range(3):
                u = src[c, i]
                before = jnp.where(lane == 0, roll(h, -(c * 8 + 4), 1), roll(u, 1, 1))
                after = jnp.where(lane == 127, roll(h, 92 - 8 * c, 1), roll(u, -1, 1))
                beside = src[c, i - 1] + src[c, i + 1] + roll(u, 1, 0) + roll(u, -1, 0) + before + after
                dst[c, i] = (drive[c, i] + v * beside) * r
            return carry

        lax.fori_loop(first, 26 - first, plane, 0)

    sweep(ua, ub, ha, hb, 1)
    sweep(ub, ua, hb, ha, 2)
    sweep(ua, ub, ha, hb, 3)

    def finish(x, carry):
        for c in range(3):
            out_ref[c, x] = ub[c, x + REACH, ROW0:ROW0 + CY, :]
        return carry

    lax.fori_loop(0, CX, finish, 0)

    comp40 = comp[0:40]

    def gather_rows(x, carry):
        h = hb[x + 3, 0:40, :]
        at = pl.multiple_of(x * 40, 40)
        for c in range(3):
            row = jnp.concatenate([ub[c, x + 3, 0:40, :], jnp.where(comp40 == c, h, 0.0)], axis=1)
            high, low = halves(row)
            lh[c, x] = high.reshape(40, 256)
            ll[c, x] = low.reshape(40, 256)
        return carry

    lax.fori_loop(0, 20, gather_rows, 0)
    line = iota((256, 1), 0)
    code = line - 128
    zed = jnp.where(code < 32, -5 + code % 8, 125 + code % 8)
    zed = jnp.where((zed >= 0) & (zed < CZ) | (code >= 64), -1000, zed)
    zed = jnp.where(line < 128, line, zed)

    for pc in range(4):
        s = s_ref[pc]
        offs = [s[3 + c:4 + c] for c in range(3)]
        wx = window(s[0:1], iota((20, 256), 0) - 2, offs[0])
        wy = window(s[1:2], iota((40, 256), 0) - ROW0, offs[1])
        wh, wl = halves(window(s[2:3], zed, offs[2]))
        scale = s[7:8] / (norm(offs[0]) * norm(offs[1]) * norm(offs[2]))
        for c in range(3):
            a, b = lh[c].reshape(800, 256), ll[c].reshape(800, 256)
            g = dot(a, wh, NN) + dot(b, wh, NN) + dot(a, wl, NN)
            t = jnp.zeros((40, 256), F32)
            for x in range(20):
                t = t + wx[x:x + 1] * g[x * 40:(x + 1) * 40]
            vel_ref[c, 0, 0, :, pc * 256:(pc + 1) * 256] = jnp.sum(t * wy, axis=0, keepdims=True) * scale


def run_sweeps(*args):
    field = lambda *lead: pltpu.VMEM(lead + (PLANES, ROWS, 128), F32)
    return pl.pallas_call(
        sweep_kernel,
        out_shape=(
            jax.ShapeDtypeStruct((3, CX, CY, CZ), F32),
            jax.ShapeDtypeStruct((3, 1, 1, 1, SLOTS), F32),
        ),
        in_specs=[pl.BlockSpec(memory_space=pltpu.VMEM)] * 6,
        out_specs=(pl.BlockSpec(memory_space=pltpu.VMEM),) * 2,
        scratch_shapes=[
            field(3), field(3), field(), field(), field(3), field(), field(), field(), field(), field(),
            pltpu.VMEM((3, 20, 40, 256), BF), pltpu.VMEM((3, 20, 40, 256), BF),
        ],
        compiler_params=pltpu.CompilerParams(vmem_limit_bytes=56 * 2**20),
        name="sweeps",
    )(*args)


def body(*args):
    return run_sweeps(*run_exchange(*args))

def solution(mesh):
    line = P("gx", "gy", "gz", None)
    wide = P(None, "gx", "gy", "gz", None)
    placed = (wide, wide, line, wide, line, line, P("gx", "gy", "gz"), line, line, line, line)
    return jax.shard_map(
        body,
        mesh=mesh,
        in_specs=placed,
        out_specs=(P(None, "gx", "gy", "gz"), wide),
        check_vma=False,
    )
```

```python
import functools
import jax
import jax.numpy as jnp
from jax import lax
from jax.experimental import pallas as pl
from jax.experimental.pallas import tpu as pltpu
from jax.sharding import PartitionSpec as P

spread_sigma = 0.8
damping = 0.5
lubrication_strength = 8.0
minimum_gap = 4.0
sharpness = 1.0 / (2.0 * spread_sigma * spread_sigma)

CX, CY, CZ = 16, 32, 128
SLOTS = 1024
PAIRS = 4096
TILES = 3 * PAIRS // 128
QB = 1024
REACH = 5
PLANES = 28
ROWS = 48
ROW0 = 5
BF = jnp.bfloat16
F32 = jnp.float32
NT = (((1,), (1,)), ((), ()))
NN = (((1,), (0,)), ((), ()))
TN = (((0,), (0,)), ((), ()))


def halves(value):
    high = value.astype(BF)
    return high, (value - high.astype(F32)).astype(BF)


def dot(a, b, dims):
    return lax.dot_general(a, b, dims, preferred_element_type=F32)


def dot3(a, b, dims):
    return dot(a[0], b[0], dims) + dot(a[1], b[0], dims) + dot(a[0], b[1], dims)


def iota(shape, dim):
    return lax.broadcasted_iota(jnp.int32, shape, dim)


def roll(value, shift, axis):
    shift = shift % value.shape[axis]
    return pltpu.roll(value, shift, axis) if shift else value


def lanes(value, index):
    return jnp.take_along_axis(value, jnp.broadcast_to(index, value.shape), axis=1)


def gauss(shift, offset):
    t = shift + 0.5 - offset
    return jnp.exp(-(t * t) * sharpness)


def norm(offset):
    total = gauss(-2.0, offset)
    for k in range(-1, 3):
        total = total + gauss(float(k), offset)
    return total


def window(cells, target, offset):
    shift = target.astype(F32) - cells
    return jnp.where(jnp.abs(shift) <= 2.0, gauss(shift, offset), 0.0)


def hot_rows(q, hot_p, hot_a, l):
    rows = iota((256, 128), 0)

    def tile(t, carry):
        for j in range(4):
            n = t * 4 + j
            at = pl.multiple_of(n * 128, 128)
            par = q[l, 2, pl.ds(n, 1), :] % 256
            loc = q[l, 0, pl.ds(n, 1), :] % 256
            hot_p[l, :, pl.ds(at, 128)] = jnp.where(rows == par, 1.0, 0.0).astype(BF)
            hot_a[l, :, pl.ds(at, 128)] = jnp.where(rows == loc, 1.0, 0.0).astype(BF)
        return carry

    lax.fori_loop(0, PAIRS // 512, tile, 0)


def split_rows(v, ref, at):
    high, low = halves(v)
    ref[at, 0:256] = high
    ref[at, 256:512] = low


def row_of(q, l, j, ch):
    n = QB // 128
    return jnp.concatenate([q[l, j, pl.ds(ch * n + t, 1), :] for t in range(n)], axis=1)


def pick(found, slab, count):
    wide = jnp.broadcast_to(slab, (8, QB))
    out = found[0:8]
    for k in range(1, count):
        out = jnp.where(wide == k, found[k * 8:(k + 1) * 8], out)
    return out


def keep(out, ref, l, ch):
    n = QB // 128
    for t in range(n):
        ref[l * (PAIRS // 128) + ch * n + t] = out[:, t * 128:(t + 1) * 128]


def find_mine(src, q, hot_a, mtab, mine, l):
    for h in range(2):
        split_rows(jnp.concatenate([src[2 * h], src[2 * h + 1]], axis=0), mtab, pl.ds(h * 16, 16))

    def step(ch, carry):
        hot = hot_a[l, :, pl.ds(pl.multiple_of(ch * QB, QB), QB)]
        found = dot(mtab[:, 0:256], hot, NN) + dot(mtab[:, 256:512], hot, NN)
        keep(pick(found, row_of(q, l, 0, ch) // 256, 4), mine, l, ch)
        return carry

    lax.fori_loop(0, PAIRS // QB, step, 0)


def codes(own):
    one = lambda c: jnp.where(c, 1, 0)
    dx = one(own >= 9) + one(own >= 18)
    rest = own - 9 * dx
    dy = one(rest >= 3) + one(rest >= 6)
    return dx, dy, rest - 3 * dy


def find_others(s, q, hot_p, tab, other):
    def fill(n, carry):
        v = jnp.concatenate([s[n // 2, n % 2 * 2], s[n // 2, n % 2 * 2 + 1]], axis=0)
        split_rows(v, tab, pl.ds(pl.multiple_of(n * 16, 16), 16))
        return carry

    lax.fori_loop(0, 18, fill, 0)

    def step(it, carry):
        l = it // (PAIRS // QB)
        ch = it % (PAIRS // QB)
        hot = hot_p[l, :, pl.ds(pl.multiple_of(ch * QB, QB), QB)]
        dx, dy, _ = codes(row_of(q, l, 1, ch))
        slab = (dy * 3 + dx) * 4 + row_of(q, l, 2, ch) // 256
        found = dot(tab[:, 0:256], hot, NN) + dot(tab[:, 256:512], hot, NN)
        keep(pick(found, slab, 36), other, l, ch)
        return carry

    lax.fori_loop(0, 3 * PAIRS // QB, step, 0)


def push_forces(q, mine, other, push, keys):
    for l in range(3):
        at = slice(l * (PAIRS // 128), (l + 1) * (PAIRS // 128))
        loc, own, par, live = (q[l, j] for j in range(4))
        dx, dy, dz = codes(own)
        m = [mine[at, r, :] for r in range(8)]
        o = [other[at, r, :] for r in range(8)]
        r = [
            (o[c] - m[c]) + (o[3 + c] - m[3 + c]) + (code - 1).astype(F32) * float(side)
            for c, (code, side) in enumerate(((dx, CX), (dy, CY), (dz, CZ)))
        ]
        spacing = jnp.sqrt(r[0] * r[0] + r[1] * r[1] + r[2] * r[2])
        clearance = spacing - m[6] - o[6]
        want = (1, 2, 0)[l]
        weight = (
            jnp.where(dz == want, live, 0).astype(F32) * m[7] * o[7] * lubrication_strength
            / (jnp.maximum(spacing, 1.0) * jnp.maximum(clearance, minimum_gap))
        )
        for c in range(3):
            v = r[c] * weight
            high = v.astype(BF).astype(F32)
            push[c, at] = high
            push[3 + c, at] = v - high
        keys[0, at] = (dy * 3 + dx) * 4 + par // 256
        keys[1, at] = loc // 256


def sum_forces(push, keys, hot_p, hot_a, acc, selves):
    acc[...] = jnp.zeros_like(acc)
    selves[...] = jnp.zeros_like(selves)
    n = QB // 128

    def step(it, carry):
        l = it // (PAIRS // QB)
        ch = it % (PAIRS // QB)
        at = pl.multiple_of(ch * QB, QB)

        def spread_rows(which, count):
            cols = []
            for t in range(n):
                k = it * n + t
                hit = iota((count, 128), 0) == keys[which, pl.ds(k, 1), :]
                cols.append(jnp.concatenate([jnp.where(hit, push[p, pl.ds(k, 1), :], 0.0) for p in range(6)], axis=0).astype(BF))
            return jnp.concatenate(cols, axis=1)

        sums = dot(spread_rows(0, 40), hot_p[l, :, pl.ds(at, QB)], NT)
        acc[...] -= (sums[0:120] + sums[120:240]).reshape(3, 40, 256)
        sums = dot(spread_rows(1, 8), hot_a[l, :, pl.ds(at, QB)], NT)
        selves[l] += sums[0:24] + sums[24:48]
        return carry

    lax.fori_loop(0, 3 * PAIRS // QB, step, 0)


X0 = (0, 3, 19)
NXS = (7, 20, 7)
R0 = (0, 0, 34)


def edge_rows():
    line = iota((128, 1), 0)
    k = line % 8
    low = line // 32 % 2 == 0
    kept = jnp.where(low, -5 + k, 125 + k)
    sent = jnp.where(low, -3 + k, 123 + k)
    return jnp.where(line < 64, kept, sent), line // 8 % 4


def axis_tables(s, b, kc, dx, dy, x0, nx, r0, ny):
    v = s[b, kc]
    offs = [v[3 + c:4 + c] for c in range(3)]
    dx_cells = jnp.asarray(dx * CX, jnp.int32).astype(F32)
    wx = window(v[0:1] + dx_cells, iota((nx, 256), 0) + (x0 - REACH), offs[0])
    wy = window(v[1:2] + float(dy * CY), iota((ny, 256), 0) + (r0 - ROW0), offs[1])
    wx = wx / (norm(offs[0]) * norm(offs[1]) * norm(offs[2]))
    wz = window(v[2:3], iota((128, 256), 0), offs[2])
    wedge = window(v[2:3], edge_rows()[0], offs[2])
    return wx, wy, jnp.concatenate([wz, wedge], axis=0)


def long_tables(s, b, dx, x0, nx, ph, pw, zt):
    def chunk(kc, carry):
        wx, wy, z = axis_tables(s, b, kc, dx, 0, x0, nx, 0, 40)
        at = pl.ds(pl.multiple_of(kc * 256, 256), 256)
        for x in range(nx):
            high, low = halves(wx[x:x + 1] * wy)
            ph[x * 40:(x + 1) * 40, at] = high
            pw[x * 40:(x + 1) * 40, at] = low
        zt[:, at] = z
        return carry

    lax.fori_loop(0, 4, chunk, 0)


def short_tables(s, b, dx, dy, x0, nx, pf, zh, zl):
    def chunk(kc, carry):
        wx, wy, z = axis_tables(s, b, kc, dx, dy, x0, nx, R0[dy + 1], 8)
        at = pl.ds(pl.multiple_of(kc * 256, 256), 256)
        for x in range(nx):
            pf[x * 8:(x + 1) * 8, at] = wx[x:x + 1] * wy
        high, low = halves(z)
        zh[:, at] = high
        zl[:, at] = low
        return carry

    lax.fori_loop(0, 4, chunk, 0)


def line_of(ref, b, c):
    return jnp.concatenate([ref[b, c * 4 + h:c * 4 + h + 1, :] for h in range(4)], axis=1)


def long_brick(ph, pw, zt, load, parts, main, edge, x0, nx):
    comp = edge_rows()[1]
    cols = []
    for part in parts:
        if part is None:
            v = jnp.zeros((128, SLOTS), F32)
            for c, value in load.items():
                v = jnp.where(comp == c, value, v)
            cols.append(zt[128:256, :] * v)
        else:
            cols.append(zt[0:128, :] * load[part])
    res = dot3((ph[...], pw[...]), halves(jnp.concatenate(cols, axis=0)), NT).reshape(nx, 40, 256)
    for n, part in enumerate(parts):
        here = res[:, :, n * 128:(n + 1) * 128]
        if part is None:
            edge[pl.ds(x0, nx), 0:40, :] += here
        else:
            main[part, pl.ds(x0, nx), 0:40, :] += here


def short_brick(pf, zh, zl, load, main, edge, x0, nx, r0):
    lane = iota((nx, 8, 128), 2)
    value = jnp.concatenate([pf[...] * v for v in load.values()], axis=0)
    res = dot3(halves(value), (zh[...], zl[...]), NT).reshape(len(load), nx, 8, 256)
    rim = jnp.zeros((nx, 8, 128), F32)
    for n, c in enumerate(load):
        main[c, pl.ds(x0, nx), r0:r0 + 8, :] += res[n, :, :, 0:128]
        rim = jnp.where(lane // 8 % 4 == c, res[n, :, :, 128:256], rim)
    edge[pl.ds(x0, nx), r0:r0 + 8, :] += rim


def assemble_base(bx, by, i):
    rows = jnp.concatenate([by[0, i], bx[i], by[1, i]], axis=0)
    return roll(rows, ROW0 - 8, 0)


def wrap_rims(bx, by, main, edge, pack):
    lane = iota((ROWS, 128), 1)
    within = [(29, 32, 0), (56, 59, 125), (91, 96, 0), (120, 125, 123)]
    index = lane
    mask = lane < 0
    for first, last, z in within:
        inside = (lane >= first) & (lane < last)
        index = jnp.where(inside, lane - first + z, index)
        mask = mask | inside

    def wrap(g, carry):
        tiles = []
        for j in range(4):
            i = g * 4 + j
            b = assemble_base(bx, by, i)
            main[3, i] += b
            t = edge[i] + jnp.where(mask, lanes(b, index), 0.0)
            edge[i] = t
            tiles.append(t)
        for side in range(2):
            out = jnp.zeros((ROWS, 128), F32)
            for j in range(4):
                out = jnp.where(lane // 32 == j, roll(tiles[j], 32 * j - 64 - 32 * side, 1), out)
            pack[side, g] = out
        return carry

    lax.fori_loop(0, PLANES // 4, wrap, 0)


def first_sweep(main, edge, rim, ua, ha, inv, hvisco, hinv):
    lane = iota((ROWS, 128), 1)
    thick = lane // 32 * 32 + 24 + lane % 8

    def start(g, carry):
        from_low, from_high = rim[0, g], rim[1, g]
        for j in range(4):
            i = g * 4 + j
            got = jnp.where(lane < 32, roll(from_low, -32 * j, 1), 0.0)
            got = jnp.where(lane // 32 == 1, roll(from_high, 32 - 32 * j, 1), got)
            total = jnp.where(lane < 64, edge[i], 0.0) + got
            v = lanes(total, thick)
            r = 1.0 / (damping + 6.0 * v)
            hvisco[i] = v
            hinv[i] = r
            edge[i] = total
            ha[i] = total * r
            m = []
            for c in range(4):
                near = lanes(got, jnp.where(lane < 64, lane + (c * 8 + 5), lane + (33 + c * 8 - 126)) % 128)
                m.append(main[c, i] + jnp.where((lane < 2) | (lane >= 126), near, 0.0))
            main[3, i] = m[3]
            r = 1.0 / (damping + 6.0 * m[3])
            inv[i] = r
            for c in range(3):
                main[c, i] = m[c]
                ua[c, i] = m[c] * r
        return carry

    lax.fori_loop(0, PLANES // 4, start, 0)


def sweep(src, dst, hsrc, hdst, main, edge, inv, hvisco, hinv, first, rows):
    lane = iota((rows, 128), 1)
    at = slice(0, rows)

    def next_row(value, ref, *lead):
        return ref[(*lead, slice(1, rows + 1))] if rows < ROWS else roll(value, -1, 0)

    def plane(i, carry):
        h = hsrc[i, at]
        beside = hsrc[i - 1, at] + hsrc[i + 1, at] + roll(h, 1, 0) + next_row(h, hsrc, i) + roll(h, 1, 1) + roll(h, -1, 1)
        hdst[i, at] = (edge[i, at] + hvisco[i, at] * beside) * hinv[i, at]
        v, r = main[3, i, at], inv[i, at]
        for c in range(3):
            u = src[c, i, at]
            rim = lanes(h, jnp.where(lane == 0, c * 8 + 4, 35 + c * 8))
            before = jnp.where(lane == 0, rim, roll(u, 1, 1))
            after = jnp.where(lane == 127, rim, roll(u, -1, 1))
            beside = src[c, i - 1, at] + src[c, i + 1, at] + roll(u, 1, 0) + next_row(u, src, c, i) + before + after
            dst[c, i, at] = (main[c, i, at] + v * beside) * r
        return carry

    lax.fori_loop(first, 26 - first, plane, 0, unroll=4)


def interpolate(ub, hb, ph, pw, zt, s, uh, ul, out):
    for x in range(20):
        row = jnp.concatenate([ub[0, x + 3, 0:40], ub[1, x + 3, 0:40], ub[2, x + 3, 0:40], hb[x + 3, 0:40]], axis=1)
        high, low = halves(row)
        uh[x * 40:(x + 1) * 40] = high
        ul[x * 40:(x + 1) * 40] = low
    z, comp = edge_rows()
    line = iota((128, 1), 0)
    outside = ((z < 0) | (z >= CZ)) & (line < 64)

    def chunk(pc, carry):
        at = pl.ds(pl.multiple_of(pc * 256, 256), 256)
        res = dot3((uh[...], ul[...]), (ph[:, at], pw[:, at]), TN)
        wz = zt[0:128, at]
        rim = jnp.where(outside, zt[128:256, at] * res[384:512], 0.0)
        alive = s[4, pc, 7:8, :]
        for c in range(3):
            value = jnp.sum(res[c * 128:(c + 1) * 128] * wz + jnp.where(comp == c, rim, 0.0), axis=0, keepdims=True)
            out[c, pl.ds(2 * pc, 1), :] = (value * alive)[:, 0:128]
            out[c, pl.ds(2 * pc + 1, 1), :] = (value * alive)[:, 128:256]
        return carry

    lax.fori_loop(0, 4, chunk, 0)


def step_kernel(
    cell_in, offset_in, radius_in, force_in, visc_in, live_in, base_in,
    local_in, owner_in, partner_in, mask_in,
    field_out, vel_out,
    cell, offset, radius, force, visc, alive,
    s, thick, zs, q, hot_p, hot_a, tab, mtab, mine, other, push, keys, acc, selves,
    ry, rz, xs, rx1, rx2, loads,
    ph0, pw0, ph1, pw1, zt, pfy, pfd, zh, zl,
    bx, by, main, edge, pack, rim,
    ua, ub, ha, hb, inv, hvisco, hinv, uh, ul, vel,
    in_sem, send_sem, recv_sem, out_sem,
):
    me = {a: lax.axis_index(a) for a in ("gx", "gy", "gz")}

    def near(axis, step):
        n = lax.axis_size(axis)
        return {axis: lax.rem(me[axis] + step + n, n)}

    inputs = [
        (cell_in, cell), (offset_in, offset), (radius_in, radius), (force_in, force), (visc_in, visc),
        (live_in, alive), (base_in, bx.at[pl.ds(REACH, CX)]), (local_in, q.at[0, 0]), (owner_in, q.at[0, 1]),
        (partner_in, q.at[0, 2]), (mask_in, q.at[0, 3]),
    ]
    inputs = [pltpu.make_async_copy(a, b, in_sem.at[n]) for n, (a, b) in enumerate(inputs)]
    for c in inputs:
        c.start()

    barrier = pltpu.get_barrier_semaphore()
    greeted = [("gx", 1), ("gx", -1), ("gx", 2), ("gx", -2), ("gy", 1), ("gy", -1), ("gz", 1), ("gz", -1)]
    for axis, step in greeted:
        pl.semaphore_signal(barrier, inc=1, device_id=near(axis, step), device_id_type=pl.DeviceIdType.MESH)

    count = [0]

    def copy(src, dst, axis, step):
        n = count[0]
        count[0] += 1
        return pltpu.make_async_remote_copy(
            src_ref=src, dst_ref=dst, send_sem=send_sem.at[n], recv_sem=recv_sem.at[n],
            device_id=near(axis, step), device_id_type=pl.DeviceIdType.MESH,
        )

    three, low3, high3 = pl.ds(3, 3), pl.ds(0, 3), pl.ds(6, 3)
    s_x = [copy(s.at[4], s.at[3], "gx", 1), copy(s.at[4], s.at[5], "gx", -1)]
    s_x += [copy(thick.at[4], thick.at[3], "gx", 1), copy(thick.at[4], thick.at[5], "gx", -1)]
    s_y = [copy(s.at[three], s.at[low3], "gy", 1), copy(s.at[three], s.at[high3], "gy", -1)]
    s_y += [copy(thick.at[three], thick.at[low3], "gy", 1), copy(thick.at[three], thick.at[high3], "gy", -1)]
    s_z = [copy(s.at[4], zs.at[0], "gz", 1), copy(s.at[4], zs.at[1], "gz", -1)]
    q_z = [copy(q.at[0], q.at[1], "gz", 1), copy(q.at[0], q.at[2], "gz", -1)]
    b_x = [
        copy(bx.at[pl.ds(CX, REACH)], bx.at[pl.ds(0, REACH)], "gx", 1),
        copy(bx.at[pl.ds(REACH, REACH)], bx.at[pl.ds(CX + REACH, REACH)], "gx", -1),
    ]
    b_y = [
        copy(bx.at[:, pl.ds(CY - 8, 8)], by.at[0], "gy", 1),
        copy(bx.at[:, pl.ds(0, 8)], by.at[1], "gy", -1),
    ]
    a_y = [copy(acc.at[:, pl.ds(24, 16)], ry.at[0], "gy", 1), copy(acc.at[:, pl.ds(0, 16)], ry.at[1], "gy", -1)]
    a_z = [copy(selves.at[1], rz.at[0], "gz", -1), copy(selves.at[2], rz.at[1], "gz", 1)]
    a_x = [
        copy(xs.at[pl.ds(1, 2)], rx1.at[0], "gx", 1), copy(xs.at[pl.ds(0, 2)], rx1.at[1], "gx", -1),
        copy(xs.at[2], rx2.at[0], "gx", 2), copy(xs.at[0], rx2.at[1], "gx", -2),
    ]
    l_y = [copy(loads.at[three], loads.at[low3], "gy", 1), copy(loads.at[three], loads.at[high3], "gy", -1)]
    e_z = [copy(pack.at[0], rim.at[1], "gz", -1), copy(pack.at[1], rim.at[0], "gz", 1)]

    def start(copies):
        for c in copies:
            c.start()

    def arrived(copies):
        for c in copies:
            c.wait_recv()

    for c in inputs:
        c.wait()
    flags = alive[...].astype(F32)
    rows = [cell[c].astype(F32) for c in range(3)] + [offset[c] for c in range(3)] + [radius[...], flags]
    for r, v in enumerate(rows):
        for h in range(4):
            s[4, h, r:r + 1, 0:128] = v[2 * h:2 * h + 1]
            s[4, h, r:r + 1, 128:256] = v[2 * h + 1:2 * h + 2]
    thick[4] = visc[...] * flags
    pl.semaphore_wait(barrier, len(greeted))
    start(s_x)
    start(s_z)
    start(q_z)

    bx[26:28] = jnp.zeros((2, CY, CZ), F32)
    hot_rows(q, hot_p, hot_a, 0)
    find_mine(s.at[4], q, hot_a, mtab, mine, 0)
    arrived(s_z)
    arrived(q_z)
    for l in (1, 2):
        hot_rows(q, hot_p, hot_a, l)
        find_mine(zs.at[l - 1], q, hot_a, mtab, mine, l)
    arrived(s_x)
    start(s_y)
    main[...] = jnp.zeros_like(main)
    edge[...] = jnp.zeros_like(edge)
    long_tables(s, 4, 0, 3, 20, ph0, pw0, zt.at[0])
    arrived(s_y)
    start(b_x)

    find_others(s, q, hot_p, tab, other)
    push_forces(q, mine, other, push, keys)
    sum_forces(push, keys, hot_p, hot_a, acc, selves)

    start(a_y)
    start(a_z)
    def side_tables(it, carry):
        long_tables(s, 3 + 2 * it, 2 * it - 1, it * 19, 7, ph1.at[it], pw1.at[it], zt.at[1 + it])
        return carry

    lax.fori_loop(0, 2, side_tables, 0)
    arrived(a_y)
    arrived(a_z)
    xs[...] = jnp.zeros_like(xs)
    for c in range(3):
        middle = acc[c, 12:24] + ry[0, c, 0:12] + ry[1, c, 0:12]
        f = force[c]
        f = jnp.concatenate(
            [jnp.concatenate([f[2 * h:2 * h + 1], f[2 * h + 1:2 * h + 2]], axis=1) for h in range(4)], axis=0
        )
        at = slice(c * 8, c * 8 + 4)
        f = f + selves[0, at] + rz[0, at] + rz[1, at]
        xs[0, c * 4:c * 4 + 4] = middle[0:4]
        xs[1, c * 4:c * 4 + 4] = middle[4:8] + f
        xs[2, c * 4:c * 4 + 4] = middle[8:12]
    start(a_x)
    for n, dy in enumerate((-1, 1)):
        short_tables(s, 3 * (dy + 1) + 1, 0, dy, 3, 20, pfy.at[n], zh.at[n * 3], zl.at[n * 3])

        def corner(it, carry):
            k = n * 3 + 1 + it
            short_tables(s, 3 * (dy + 1) + 2 * it, 2 * it - 1, dy, it * 19, 7, pfd.at[n * 2 + it], zh.at[k], zl.at[k])
            return carry

        lax.fori_loop(0, 2, corner, 0)

    def thickness(b):
        return {3: jnp.concatenate([thick[b, t:t + 1, :] for t in range(8)], axis=1)}

    def short_all(load):
        for n, dy in enumerate((-1, 1)):
            k = n * 3
            short_brick(pfy[n], zh.at[k], zl.at[k], load(3 * (dy + 1) + 1), main, edge, 3, 20, R0[dy + 1])

            def corner(it, carry):
                k = n * 3 + 1 + it
                b = 3 * (dy + 1) + 2 * it
                short_brick(pfd[n * 2 + it], zh.at[k], zl.at[k], load(b), main, edge, it * 19, 7, R0[dy + 1])
                return carry

            lax.fori_loop(0, 2, corner, 0)

    def long_all(load, parts):
        long_brick(ph0, pw0, zt.at[0], load(4), parts, main, edge, 3, 20)

        def side(it, carry):
            long_brick(ph1.at[it], pw1.at[it], zt.at[1 + it], load(3 + 2 * it), parts, main, edge, it * 19, 7)
            return carry

        lax.fori_loop(0, 2, side, 0)

    long_all(thickness, (3, None))
    short_all(thickness)

    arrived(a_x)
    for n in range(3):
        if n == 0:
            total = rx1[0, 0] + rx2[0] + xs[0]
        elif n == 1:
            total = xs[1] + rx1[0, 1] + rx1[1, 0]
        else:
            total = rx1[1, 1] + rx2[1] + xs[2]
        for h in range(4):
            on = s[3 + n, h, 7:8, :]
            for c in range(3):
                loads[3 + n, c * 4 + h:c * 4 + h + 1, :] = on * total[c * 4 + h:c * 4 + h + 1]
        loads[3 + n, 12:16] = jnp.zeros((4, 256), F32)
    start(l_y)
    arrived(b_x)
    start(b_y)

    def forces(b):
        return {c: line_of(loads, b, c) for c in range(3)}

    long_all(forces, (2, None))
    arrived(l_y)
    short_all(forces)
    arrived(b_y)
    wrap_rims(bx, by, main, edge, pack)
    start(e_z)
    long_all(forces, (0, 1))
    arrived(e_z)

    first_sweep(main, edge, rim, ua, ha, inv, hvisco, hinv)
    rest = (main, edge, inv, hvisco, hinv)
    sweep(ua, ub, ha, hb, *rest, 1, 48)
    sweep(ub, ua, hb, ha, *rest, 2, 40)
    sweep(ua, ub, ha, hb, *rest, 3, 40)

    def finish(x, carry):
        for c in range(3):
            ua[c, x, 0:CY] = ub[c, x + REACH, ROW0:ROW0 + CY, :]
        return carry

    lax.fori_loop(0, CX, finish, 0)
    outputs = [pltpu.make_async_copy(ua.at[:, pl.ds(0, CX), pl.ds(0, CY)], field_out, out_sem.at[0])]
    outputs[0].start()
    interpolate(ub, hb, ph0, pw0, zt.at[0], s, uh, ul, vel)
    outputs.append(pltpu.make_async_copy(vel, vel_out, out_sem.at[1]))
    outputs[1].start()
    for group in (s_x, s_y, s_z, q_z, b_x, b_y, a_y, a_z, a_x, l_y, e_z):
        for c in group:
            c.wait_send()
    for c in outputs:
        c.wait()


def scratch():
    f = lambda *shape: pltpu.VMEM(shape, F32)
    i = lambda *shape: pltpu.VMEM(shape, jnp.int32)
    b = lambda *shape: pltpu.VMEM(shape, BF)
    grid = lambda *lead: pltpu.VMEM(lead + (PLANES, ROWS, 128), F32)
    sem = pltpu.SemaphoreType.DMA
    return [
        i(3, 8, 128), f(3, 8, 128), f(8, 128), f(3, 8, 128), f(8, 128), i(8, 128),
        f(9, 4, 8, 256), f(9, 8, 128), f(2, 4, 8, 256), i(3, 4, 32, 128),
        b(3, 256, PAIRS), b(3, 256, PAIRS), b(288, 512), b(32, 512),
        f(TILES, 8, 128), f(TILES, 8, 128), f(6, TILES, 128), i(2, TILES, 128),
        f(3, 40, 256), f(3, 24, 256),
        f(2, 3, 16, 256), f(2, 24, 256), f(3, 16, 256), f(2, 2, 16, 256), f(2, 16, 256), f(9, 16, 256),
        b(800, SLOTS), b(800, SLOTS), b(2, 280, SLOTS), b(2, 280, SLOTS), f(3, 256, SLOTS),
        f(2, 160, SLOTS), f(4, 56, SLOTS), b(6, 256, SLOTS), b(6, 256, SLOTS),
        f(PLANES, CY, CZ), f(2, PLANES, 8, CZ), grid(4), grid(), f(2, PLANES // 4, ROWS, 128), f(2, PLANES // 4, ROWS, 128),
        grid(3), grid(3), grid(), grid(), grid(), grid(), grid(), b(800, 512), b(800, 512), f(3, 8, 128),
        sem((11,)), sem((28,)), sem((28,)), sem((2,)),
    ]


def body(
    cell_index, cell_offset, radius, forcing, viscosity, occupied, base_viscosity,
    pair_local, pair_owner, pair_partner, pair_slot_mask,
):
    args = [a.reshape(3, 8, 128) if a.shape[0] == 3 else a.reshape(8, 128) for a in (
        cell_index, cell_offset, radius, forcing, viscosity, occupied
    )]
    args += [base_viscosity]
    args += [a.reshape(32, 128) for a in (pair_local, pair_owner, pair_partner, pair_slot_mask)]
    field, velocity = pl.pallas_call(
        step_kernel,
        out_shape=(
            jax.ShapeDtypeStruct((3, CX, CY, CZ), F32),
            jax.ShapeDtypeStruct((3, 8, 128), F32),
        ),
        in_specs=[pl.BlockSpec(memory_space=pltpu.HBM)] * 11,
        out_specs=(pl.BlockSpec(memory_space=pltpu.HBM),) * 2,
        scratch_shapes=scratch(),
        compiler_params=pltpu.CompilerParams(
            collective_id=0, has_side_effects=True, vmem_limit_bytes=62 * 2**20
        ),
        name="coupling",
    )(*args)
    return field, velocity.reshape(3, 1, 1, 1, SLOTS)


def solution(mesh):
    line = P("gx", "gy", "gz", None)
    wide = P(None, "gx", "gy", "gz", None)
    placed = (wide, wide, line, wide, line, line, P("gx", "gy", "gz"), line, line, line, line)
    return jax.shard_map(
        body,
        mesh=mesh,
        in_specs=placed,
        out_specs=(P(None, "gx", "gy", "gz"), wide),
        check_vma=False,
    )
```

```python
import functools
import jax
import jax.numpy as jnp
from jax import lax
from jax.experimental import pallas as pl
from jax.experimental.pallas import tpu as pltpu
from jax.sharding import PartitionSpec as P

spread_sigma = 0.8
damping = 0.5
lubrication_strength = 8.0
minimum_gap = 4.0
sharpness = 1.0 / (2.0 * spread_sigma * spread_sigma)

CX, CY, CZ = 16, 32, 128
SLOTS = 1024
PAIRS = 4096
TILES = 3 * PAIRS // 128
QB = 1024
REACH = 5
PLANES = 28
ROWS = 48
ROW0 = 5
BF = jnp.bfloat16
F32 = jnp.float32
NT = (((1,), (1,)), ((), ()))
NN = (((1,), (0,)), ((), ()))
TN = (((0,), (0,)), ((), ()))


def halves(value):
    high = value.astype(BF)
    return high, (value - high.astype(F32)).astype(BF)


def dot(a, b, dims):
    return lax.dot_general(a, b, dims, preferred_element_type=F32)


def dot3(a, b, dims):
    return dot(a[0], b[0], dims) + dot(a[1], b[0], dims) + dot(a[0], b[1], dims)


def iota(shape, dim):
    return lax.broadcasted_iota(jnp.int32, shape, dim)


def roll(value, shift, axis):
    shift = shift % value.shape[axis]
    return pltpu.roll(value, shift, axis) if shift else value


def lanes(value, index):
    index = jnp.broadcast_to(index, value.shape)
    return jnp.take_along_axis(value, index, axis=1, mode="promise_in_bounds")


def gauss(shift, offset):
    t = shift + 0.5 - offset
    return jnp.exp(-(t * t) * sharpness)


def norm(offset):
    total = gauss(-2.0, offset)
    for k in range(-1, 3):
        total = total + gauss(float(k), offset)
    return total


def window(cells, target, offset):
    shift = target.astype(F32) - cells
    return jnp.where(jnp.abs(shift) <= 2.0, gauss(shift, offset), 0.0)


def hot_rows(q, hot_p, hot_a, l):
    rows = iota((256, 128), 0)

    def tile(t, carry):
        for j in range(4):
            n = t * 4 + j
            at = pl.multiple_of(n * 128, 128)
            par = q[l, 2, pl.ds(n, 1), :] & 255
            loc = q[l, 0, pl.ds(n, 1), :] & 255
            hot_p[l, :, pl.ds(at, 128)] = jnp.where(rows == par, 1.0, 0.0).astype(BF)
            hot_a[l, :, pl.ds(at, 128)] = jnp.where(rows == loc, 1.0, 0.0).astype(BF)
        return carry

    lax.fori_loop(0, PAIRS // 512, tile, 0)


def row_of(q, l, j, ch):
    n = QB // 128
    return jnp.concatenate([q[l, j, pl.ds(ch * n + t, 1), :] for t in range(n)], axis=1)


def pick(found, slab, slabs, out):
    wide = jnp.broadcast_to(slab, (8, QB))
    for n, k in enumerate(slabs):
        out = jnp.where(wide == k, found[n * 8:(n + 1) * 8], out)
    return out


def find_mine(src, q, mine, l):
    def step(t, carry):
        for j in range(4):
            n = t * 4 + j
            loc = jnp.broadcast_to(q[l, 0, pl.ds(n, 1), :], (8, 128))
            index, block = loc & 127, loc >> 7
            out = jnp.zeros((8, 128), F32)
            for k in range(8):
                out = jnp.where(block == k, lanes(src[k // 2, :, k % 2 * 128:k % 2 * 128 + 128], index), out)
            mine[l * (PAIRS // 128) + n] = out
        return carry

    lax.fori_loop(0, PAIRS // 512, step, 0)


def codes(own):
    one = lambda c: jnp.where(c, 1, 0)
    dx = one(own >= 9) + one(own >= 18)
    rest = own - 9 * dx
    dy = one(rest >= 3) + one(rest >= 6)
    return dx, dy, rest - 3 * dy


def find_others(s, q, hot_p, tab, other, bricks, first):
    count = len(bricks)
    def fill(brick, n):
        v = jnp.concatenate([s[brick, 0], s[brick, 1], s[brick, 2], s[brick, 3]], axis=0)
        high, low = halves(v)
        tab[n * 32:(n + 1) * 32, 0:256] = high
        tab[n * 32:(n + 1) * 32, 256:512] = low

    for n, brick in enumerate(bricks):
        fill(brick, n)
    slabs = [b * 4 + h for b in bricks for h in range(4)]
    tiles = QB // 128

    def step(it, carry):
        l = it // (PAIRS // QB)
        ch = it % (PAIRS // QB)
        hot = hot_p[l, :, pl.ds(pl.multiple_of(ch * QB, QB), QB)]
        dx, dy, _ = codes(row_of(q, l, 1, ch))
        slab = (dy * 3 + dx) * 4 + (row_of(q, l, 2, ch) >> 8)
        rows = slice(0, count * 32)
        found = dot(tab[rows, 0:256], hot, NN) + dot(tab[rows, 256:512], hot, NN)
        if first:
            out = jnp.zeros((8, QB), F32)
        else:
            out = jnp.concatenate([other[it * tiles + t] for t in range(tiles)], axis=1)
        out = pick(found, slab, slabs, out)
        for t in range(tiles):
            other[it * tiles + t] = out[:, t * 128:(t + 1) * 128]
        return carry

    lax.fori_loop(0, 3 * PAIRS // QB, step, 0, unroll=2)


def push_forces(q, mine, other, push, keys):
    for l in range(3):
        at = slice(l * (PAIRS // 128), (l + 1) * (PAIRS // 128))
        loc, own, par, live = (q[l, j] for j in range(4))
        dx, dy, dz = codes(own)
        m = [mine[at, r, :] for r in range(8)]
        o = [other[at, r, :] for r in range(8)]
        r = [
            (o[c] - m[c]) + (o[3 + c] - m[3 + c]) + (code - 1).astype(F32) * float(side)
            for c, (code, side) in enumerate(((dx, CX), (dy, CY), (dz, CZ)))
        ]
        spacing = jnp.sqrt(r[0] * r[0] + r[1] * r[1] + r[2] * r[2])
        clearance = spacing - m[6] - o[6]
        want = (1, 2, 0)[l]
        weight = (
            jnp.where(dz == want, live, 0).astype(F32) * m[7] * o[7] * lubrication_strength
            / (jnp.maximum(spacing, 1.0) * jnp.maximum(clearance, minimum_gap))
        )
        for c in range(3):
            v = r[c] * weight
            high = v.astype(BF).astype(F32)
            push[c, at] = high
            push[3 + c, at] = v - high
        keys[0, at] = (dy * 3 + dx) * 4 + (par >> 8)
        keys[1, at] = loc >> 8


def spread_rows(push, keys, it, count):
    cols = []
    for t in range(QB // 128):
        k = it * (QB // 128) + t
        hit = iota((count, 128), 0) == keys[pl.ds(k, 1), :]
        rows = [jnp.where(hit, push[p, pl.ds(k, 1), :], 0.0) for p in range(6)]
        cols.append(jnp.concatenate(rows, axis=0).astype(BF))
    return jnp.concatenate(cols, axis=1)


def sum_others(push, keys, hot_p, acc):
    acc[...] = jnp.zeros_like(acc)

    def step(it, carry):
        l = it // (PAIRS // QB)
        at = pl.multiple_of(it % (PAIRS // QB) * QB, QB)
        sums = dot(spread_rows(push, keys.at[0], it, 40), hot_p[l, :, pl.ds(at, QB)], NT)
        acc[...] -= (sums[0:120] + sums[120:240]).reshape(3, 40, 256)
        return carry

    lax.fori_loop(0, 3 * PAIRS // QB, step, 0, unroll=2)


def sum_mine(push, keys, hot_a, selves, l):
    selves[l] = jnp.zeros((24, 256), F32)

    def step(ch, carry):
        it = l * (PAIRS // QB) + ch
        sums = dot(spread_rows(push, keys.at[1], it, 8), hot_a[l, :, pl.ds(pl.multiple_of(ch * QB, QB), QB)], NT)
        selves[l] += sums[0:24] + sums[24:48]
        return carry

    lax.fori_loop(0, PAIRS // QB, step, 0, unroll=2)


X0 = (0, 3, 19)
NXS = (7, 20, 7)
R0 = (0, 0, 34)


def edge_rows():
    line = iota((128, 1), 0)
    k = line % 8
    low = line // 32 % 2 == 0
    kept = jnp.where(low, -5 + k, 125 + k)
    sent = jnp.where(low, -3 + k, 123 + k)
    return jnp.where(line < 64, kept, sent), line // 8 % 4


def axis_tables(s, b, kc, dx, dy, x0, nx, r0, ny):
    v = s[b, kc]
    offs = [v[3 + c:4 + c] for c in range(3)]
    dx_cells = jnp.asarray(dx * CX, jnp.int32).astype(F32)
    wx = window(v[0:1] + dx_cells, iota((nx, 256), 0) + (x0 - REACH), offs[0])
    wy = window(v[1:2] + float(dy * CY), iota((ny, 256), 0) + (r0 - ROW0), offs[1])
    wz = window(v[2:3], iota((128, 256), 0), offs[2])
    eight = iota((8, 256), 0)
    wedge = [window(v[2:3], eight + z, offs[2]) for z in (-5, 125, -3, 123)]
    return wx, wy, wz, [w for w in wedge for c in range(4)]


def long_tables(s, b, dx, x0, nx, ph, pw, zt):
    def chunk(kc, carry):
        wx, wy, wz, wedge = axis_tables(s, b, kc, dx, 0, x0, nx, 0, 40)
        at = pl.ds(pl.multiple_of(kc * 256, 256), 256)
        for x in range(nx):
            high, low = halves(wx[x:x + 1] * wy)
            ph[x * 40:(x + 1) * 40, at] = high
            pw[x * 40:(x + 1) * 40, at] = low
        zt[0:128, at] = wz
        zt[128:256, at] = jnp.concatenate(wedge, axis=0)
        return carry

    lax.fori_loop(0, 4, chunk, 0)


def short_tables(s, b, dx, dy, x0, nx, pf, zh, zl):
    def chunk(kc, carry):
        wx, wy, wz, wedge = axis_tables(s, b, kc, dx, dy, x0, nx, R0[dy + 1], 8)
        at = pl.ds(pl.multiple_of(kc * 256, 256), 256)
        for x in range(nx):
            pf[x * 8:(x + 1) * 8, at] = wx[x:x + 1] * wy
        high, low = halves(wz)
        zh[0:128, at] = high
        zl[0:128, at] = low
        pairs = [jnp.concatenate(wedge[n:n + 2], axis=0) for n in (0, 4, 8, 12)]
        for n, (high, low) in enumerate(halves(p) for p in pairs):
            for k in range(2):
                rows = slice(128 + n * 32 + k * 16, 128 + n * 32 + k * 16 + 16)
                zh[rows, at] = high
                zl[rows, at] = low
        return carry

    lax.fori_loop(0, 4, chunk, 0)


def envelope_scale(s, b, h):
    total = norm(s[b, h])
    return 1.0 / (total[3:4] * total[4:5] * total[5:6])


def line_of(ref, b, c):
    return jnp.concatenate([ref[b, c * 4 + h:c * 4 + h + 1, :] for h in range(4)], axis=1)


def long_brick(ph, pw, zt, load, parts, main, edge, x0, nx):
    comp = edge_rows()[1]
    cols = []
    for part in parts:
        if part is None:
            v = jnp.zeros((128, SLOTS), F32)
            for c, value in load.items():
                v = jnp.where(comp == c, value, v)
            cols.append(zt[128:256, :] * v)
        else:
            cols.append(zt[0:128, :] * load[part])
    res = dot3((ph[...], pw[...]), halves(jnp.concatenate(cols, axis=0)), NT).reshape(nx, 40, 256)
    for n, part in enumerate(parts):
        here = res[:, :, n * 128:(n + 1) * 128]
        if part is None:
            edge[pl.ds(x0, nx), 0:40, :] += here
        else:
            main[part, pl.ds(x0, nx), 0:40, :] += here


def short_brick(pf, zh, zl, load, main, edge, x0, nx, r0):
    lane = iota((nx, 8, 128), 2)
    value = jnp.concatenate([pf[...] * v for v in load.values()], axis=0)
    res = dot3(halves(value), (zh[...], zl[...]), NT).reshape(len(load), nx, 8, 256)
    rim = jnp.zeros((nx, 8, 128), F32)
    for n, c in enumerate(load):
        main[c, pl.ds(x0, nx), r0:r0 + 8, :] += res[n, :, :, 0:128]
        rim = jnp.where(lane // 8 % 4 == c, res[n, :, :, 128:256], rim)
    edge[pl.ds(x0, nx), r0:r0 + 8, :] += rim


def assemble_base(bx, by, i):
    rows = jnp.concatenate([by[0, i], bx[i], by[1, i]], axis=0)
    return roll(rows, ROW0 - 8, 0)


def wrap_rims(bx, by, edge, pack):
    lane = iota((ROWS, 128), 1)
    within = [(29, 32, 0), (56, 59, 125), (91, 96, 0), (120, 125, 123)]
    index = lane
    mask = lane < 0
    for first, last, z in within:
        inside = (lane >= first) & (lane < last)
        index = jnp.where(inside, lane - first + z, index)
        mask = mask | inside

    def wrap(g, carry):
        tiles = []
        for j in range(4):
            i = g * 4 + j
            b = assemble_base(bx, by, i)
            t = edge[i] + jnp.where(mask, lanes(b, index), 0.0)
            edge[i] = t
            tiles.append(t)
        for side in range(2):
            out = jnp.zeros((ROWS, 128), F32)
            for j in range(4):
                out = jnp.where(lane // 32 == j, roll(tiles[j], 32 * j - 64 - 32 * side, 1), out)
            pack[side, g] = out
        return carry

    lax.fori_loop(0, PLANES // 4, wrap, 0)


def add_base(bx, by, main):
    def plane(g, carry):
        for j in range(4):
            i = g * 4 + j
            main[3, i] += assemble_base(bx, by, i)
        return carry

    lax.fori_loop(0, PLANES // 4, plane, 0)


def first_sweep(main, edge, rim, ua, ha, inv, hvisco, hinv):
    lane = iota((ROWS, 128), 1)
    thick = lane // 32 * 32 + 24 + lane % 8

    def start(g, carry):
        from_low, from_high = rim[0, g], rim[1, g]
        for j in range(4):
            i = g * 4 + j
            got = jnp.where(lane < 32, roll(from_low, -32 * j, 1), 0.0)
            got = jnp.where(lane // 32 == 1, roll(from_high, 32 - 32 * j, 1), got)
            total = jnp.where(lane < 64, edge[i], 0.0) + got
            v = lanes(total, thick)
            r = 1.0 / (damping + 6.0 * v)
            hvisco[i] = v
            hinv[i] = r
            edge[i] = total
            ha[i] = total * r
            m = []
            for c in range(4):
                near = lanes(got, jnp.where(lane < 64, lane + (c * 8 + 5), lane + (33 + c * 8 - 126)) % 128)
                m.append(main[c, i] + jnp.where((lane < 2) | (lane >= 126), near, 0.0))
            main[3, i] = m[3]
            r = 1.0 / (damping + 6.0 * m[3])
            inv[i] = r
            for c in range(3):
                main[c, i] = m[c]
                ua[c, i] = m[c] * r
        return carry

    lax.fori_loop(0, PLANES // 4, start, 0)


def sweep(src, dst, hsrc, hdst, main, edge, inv, hvisco, hinv, first, rows):
    lane = iota((rows, 128), 1)
    at = slice(0, rows)

    def next_row(value, ref, *lead):
        return ref[(*lead, slice(1, rows + 1))] if rows < ROWS else roll(value, -1, 0)

    def plane(i, carry):
        h = hsrc[i, at]
        beside = hsrc[i - 1, at] + hsrc[i + 1, at] + roll(h, 1, 0) + next_row(h, hsrc, i) + roll(h, 1, 1) + roll(h, -1, 1)
        hdst[i, at] = (edge[i, at] + hvisco[i, at] * beside) * hinv[i, at]
        v, r = main[3, i, at], inv[i, at]
        for c in range(3):
            u = src[c, i, at]
            rim = lanes(h, jnp.where(lane == 0, c * 8 + 4, 35 + c * 8))
            before = jnp.where(lane == 0, rim, roll(u, 1, 1))
            after = jnp.where(lane == 127, rim, roll(u, -1, 1))
            beside = src[c, i - 1, at] + src[c, i + 1, at] + roll(u, 1, 0) + next_row(u, src, c, i) + before + after
            dst[c, i, at] = (main[c, i, at] + v * beside) * r
        return carry

    lax.fori_loop(first, 26 - first, plane, 0, unroll=4)


def interpolate(ub, hb, ph, pw, zt, s, scale, uh, ul, out):
    for x in range(20):
        row = jnp.concatenate([ub[0, x + 3, 0:40], ub[1, x + 3, 0:40], ub[2, x + 3, 0:40], hb[x + 3, 0:40]], axis=1)
        high, low = halves(row)
        uh[x * 40:(x + 1) * 40] = high
        ul[x * 40:(x + 1) * 40] = low
    field = uh[...].T[0:448], ul[...].T[0:448]
    z, comp = (v[0:64] for v in edge_rows())
    outside = (z < 0) | (z >= CZ)
    for pc in range(4):
        at = slice(pc * 256, (pc + 1) * 256)
        res = dot3(field, (ph[:, at], pw[:, at]), NN)
        wz = zt[0:128, at]
        rim = jnp.where(outside, zt[128:192, at] * res[384:448], 0.0)
        factor = s[4, pc, 7:8, :] * scale[1, pc:pc + 1, :]
        for c in range(3):
            value = jnp.sum(res[c * 128:(c + 1) * 128] * wz, axis=0, keepdims=True)
            value = (value + jnp.sum(jnp.where(comp == c, rim, 0.0), axis=0, keepdims=True)) * factor
            out[c, 2 * pc:2 * pc + 1, :] = value[:, 0:128]
            out[c, 2 * pc + 1:2 * pc + 2, :] = value[:, 128:256]


def step_kernel(
    cell_in, offset_in, radius_in, force_in, visc_in, live_in, base_in,
    local_in, owner_in, partner_in, mask_in,
    field_out, vel_out,
    cell, offset, radius, force, visc, alive,
    s, thick, scale, zs, q, hot_p, hot_a, tab, mine, other, push, keys, acc, selves,
    ry, rz, xs, rx1, rx2, loads,
    ph0, pw0, ph1, pw1, zt, pfy, pfd, zh, zl,
    bx, by, main, edge, pack, rim,
    ua, ub, ha, hb, inv, hvisco, hinv, uh, ul, vel,
    in_sem, send_sem, recv_sem, out_sem,
):
    me = {a: lax.axis_index(a) for a in ("gx", "gy", "gz")}

    def near(axis, step):
        n = lax.axis_size(axis)
        return {axis: lax.rem(me[axis] + step + n, n)}

    inputs = [
        (cell_in, cell), (offset_in, offset), (radius_in, radius), (force_in, force), (visc_in, visc),
        (live_in, alive), (base_in, bx.at[pl.ds(REACH, CX)]), (local_in, q.at[0, 0]), (owner_in, q.at[0, 1]),
        (partner_in, q.at[0, 2]), (mask_in, q.at[0, 3]),
    ]
    inputs = [pltpu.make_async_copy(a, b, in_sem.at[n]) for n, (a, b) in enumerate(inputs)]
    for c in inputs:
        c.start()

    barrier = pltpu.get_barrier_semaphore()
    greeted = [("gx", 1), ("gx", -1), ("gx", 2), ("gx", -2), ("gy", 1), ("gy", -1), ("gz", 1), ("gz", -1)]
    for axis, step in greeted:
        pl.semaphore_signal(barrier, inc=1, device_id=near(axis, step), device_id_type=pl.DeviceIdType.MESH)

    count = [0]

    def copy(src, dst, axis, step):
        n = count[0]
        count[0] += 1
        return pltpu.make_async_remote_copy(
            src_ref=src, dst_ref=dst, send_sem=send_sem.at[n], recv_sem=recv_sem.at[n],
            device_id=near(axis, step), device_id_type=pl.DeviceIdType.MESH,
        )

    three, low3, high3 = pl.ds(3, 3), pl.ds(0, 3), pl.ds(6, 3)
    s_x = [copy(s.at[4], s.at[3], "gx", 1), copy(s.at[4], s.at[5], "gx", -1)]
    s_x += [copy(thick.at[4], thick.at[3], "gx", 1), copy(thick.at[4], thick.at[5], "gx", -1)]
    s_y = [copy(s.at[three], s.at[low3], "gy", 1), copy(s.at[three], s.at[high3], "gy", -1)]
    s_y += [copy(thick.at[three], thick.at[low3], "gy", 1), copy(thick.at[three], thick.at[high3], "gy", -1)]
    s_z = [copy(s.at[4], zs.at[0], "gz", 1), copy(s.at[4], zs.at[1], "gz", -1)]
    q_z = [copy(q.at[0], q.at[1], "gz", 1), copy(q.at[0], q.at[2], "gz", -1)]
    b_x = [
        copy(bx.at[pl.ds(CX, REACH)], bx.at[pl.ds(0, REACH)], "gx", 1),
        copy(bx.at[pl.ds(REACH, REACH)], bx.at[pl.ds(CX + REACH, REACH)], "gx", -1),
    ]
    b_y = [
        copy(bx.at[:, pl.ds(CY - 8, 8)], by.at[0], "gy", 1),
        copy(bx.at[:, pl.ds(0, 8)], by.at[1], "gy", -1),
    ]
    a_y = [copy(acc.at[:, pl.ds(24, 16)], ry.at[0], "gy", 1), copy(acc.at[:, pl.ds(0, 16)], ry.at[1], "gy", -1)]
    a_z = [copy(selves.at[1], rz.at[0], "gz", -1), copy(selves.at[2], rz.at[1], "gz", 1)]
    a_x = [
        copy(xs.at[pl.ds(1, 2)], rx1.at[0], "gx", 1), copy(xs.at[pl.ds(0, 2)], rx1.at[1], "gx", -1),
        copy(xs.at[2], rx2.at[0], "gx", 2), copy(xs.at[0], rx2.at[1], "gx", -2),
    ]
    l_y = [copy(loads.at[three], loads.at[low3], "gy", 1), copy(loads.at[three], loads.at[high3], "gy", -1)]
    e_z = [copy(pack.at[0], rim.at[1], "gz", -1), copy(pack.at[1], rim.at[0], "gz", 1)]

    def start(copies):
        for c in copies:
            c.start()

    def arrived(copies):
        for c in copies:
            c.wait_recv()

    for c in inputs:
        c.wait()
    flags = alive[...].astype(F32)
    rows = [cell[c].astype(F32) for c in range(3)] + [offset[c] for c in range(3)] + [radius[...], flags]
    for r, v in enumerate(rows):
        for h in range(4):
            s[4, h, r:r + 1, 0:128] = v[2 * h:2 * h + 1]
            s[4, h, r:r + 1, 128:256] = v[2 * h + 1:2 * h + 2]
    for h in range(4):
        scale[1, h:h + 1, :] = envelope_scale(s, 4, h)
    for h in range(4):
        for k in range(2):
            row = slice(2 * h + k, 2 * h + k + 1)
            thick[4, row, :] = visc[row, :] * flags[row] * scale[1, h:h + 1, k * 128:(k + 1) * 128]
    pl.semaphore_wait(barrier, len(greeted))
    start(s_x)
    start(s_z)
    start(q_z)

    bx[26:28] = jnp.zeros((2, CY, CZ), F32)
    hot_rows(q, hot_p, hot_a, 0)
    find_mine(s.at[4], q, mine, 0)
    arrived(s_z)
    arrived(q_z)
    hot_rows(q, hot_p, hot_a, 1)
    find_mine(zs.at[0], q, mine, 1)
    arrived(s_x)
    start(s_y)
    hot_rows(q, hot_p, hot_a, 2)
    find_mine(zs.at[1], q, mine, 2)
    find_others(s, q, hot_p, tab, other, (3, 4, 5), True)
    arrived(s_y)
    start(b_x)

    find_others(s, q, hot_p, tab, other, (0, 1, 2, 6, 7, 8), False)
    push_forces(q, mine, other, push, keys)
    sum_others(push, keys, hot_p, acc)
    start(a_y)
    sum_mine(push, keys, hot_a, selves, 1)
    sum_mine(push, keys, hot_a, selves, 2)
    start(a_z)
    sum_mine(push, keys, hot_a, selves, 0)

    long_tables(s, 4, 0, 3, 20, ph0, pw0, zt.at[0])

    def side_tables(it, carry):
        long_tables(s, 3 + 2 * it, 2 * it - 1, it * 19, 7, ph1.at[it], pw1.at[it], zt.at[1 + it])
        return carry

    arrived(a_y)
    arrived(a_z)
    xs[...] = jnp.zeros_like(xs)
    for c in range(3):
        middle = acc[c, 12:24] + ry[0, c, 0:12] + ry[1, c, 0:12]
        f = force[c]
        f = jnp.concatenate(
            [jnp.concatenate([f[2 * h:2 * h + 1], f[2 * h + 1:2 * h + 2]], axis=1) for h in range(4)], axis=0
        )
        at = slice(c * 8, c * 8 + 4)
        f = f + selves[0, at] + rz[0, at] + rz[1, at]
        xs[0, c * 4:c * 4 + 4] = middle[0:4]
        xs[1, c * 4:c * 4 + 4] = middle[4:8] + f
        xs[2, c * 4:c * 4 + 4] = middle[8:12]
    start(a_x)

    def thickness(b):
        return jnp.concatenate([thick[b, t:t + 1, :] for t in range(8)], axis=1)

    def forces(b):
        return {c: line_of(loads, b, c) for c in range(3)}

    def long_all(load, parts):
        long_brick(ph0, pw0, zt.at[0], load(4), parts, main, edge, 3, 20)

        def side(it, carry):
            long_brick(ph1.at[it], pw1.at[it], zt.at[1 + it], load(3 + 2 * it), parts, main, edge, it * 19, 7)
            return carry

        lax.fori_loop(0, 2, side, 0)

    lax.fori_loop(0, 2, side_tables, 0)
    for h in range(4):
        for n in (0, 2):
            scale[n, h:h + 1, :] = envelope_scale(s, 3 + n, h)
    for n, dy in enumerate((-1, 1)):
        short_tables(s, 3 * (dy + 1) + 1, 0, dy, 3, 20, pfy.at[n], zh.at[n * 3], zl.at[n * 3])

        def corner(it, carry):
            k = n * 3 + 1 + it
            short_tables(s, 3 * (dy + 1) + 2 * it, 2 * it - 1, dy, it * 19, 7, pfd.at[n * 2 + it], zh.at[k], zl.at[k])
            return carry

        lax.fori_loop(0, 2, corner, 0)
    main[...] = jnp.zeros_like(main)
    edge[...] = jnp.zeros_like(edge)
    arrived(a_x)
    for n in range(3):
        if n == 0:
            total = rx1[0, 0] + rx2[0] + xs[0]
        elif n == 1:
            total = xs[1] + rx1[0, 1] + rx1[1, 0]
        else:
            total = rx1[1, 1] + rx2[1] + xs[2]
        for h in range(4):
            on = s[3 + n, h, 7:8, :] * scale[n, h:h + 1, :]
            for c in range(3):
                loads[3 + n, c * 4 + h:c * 4 + h + 1, :] = on * total[c * 4 + h:c * 4 + h + 1]
        loads[3 + n, 12:16] = jnp.zeros((4, 256), F32)
    start(l_y)
    arrived(b_x)
    start(b_y)

    long_all(lambda b: {3: thickness(b)}, (3, None))
    long_all(forces, (2, None))
    arrived(l_y)
    for n, dy in enumerate((-1, 1)):
        k = n * 3
        b = 3 * (dy + 1) + 1
        short_brick(pfy[n], zh.at[k], zl.at[k], {**forces(b), 3: thickness(b)}, main, edge, 3, 20, R0[dy + 1])

        def corner(it, carry):
            k = n * 3 + 1 + it
            b = 3 * (dy + 1) + 2 * it
            load = {**forces(b), 3: thickness(b)}
            short_brick(pfd[n * 2 + it], zh.at[k], zl.at[k], load, main, edge, it * 19, 7, R0[dy + 1])
            return carry

        lax.fori_loop(0, 2, corner, 0, unroll=True)
    arrived(b_y)
    wrap_rims(bx, by, edge, pack)
    start(e_z)
    long_all(forces, (0, 1))
    add_base(bx, by, main)
    arrived(e_z)

    first_sweep(main, edge, rim, ua, ha, inv, hvisco, hinv)
    rest = (main, edge, inv, hvisco, hinv)
    sweep(ua, ub, ha, hb, *rest, 1, 48)
    sweep(ub, ua, hb, ha, *rest, 2, 40)
    sweep(ua, ub, ha, hb, *rest, 3, 40)

    def finish(x, carry):
        for c in range(3):
            ua[c, x, 0:CY] = ub[c, x + REACH, ROW0:ROW0 + CY, :]
        return carry

    lax.fori_loop(0, CX, finish, 0)
    outputs = [pltpu.make_async_copy(ua.at[:, pl.ds(0, CX), pl.ds(0, CY)], field_out, out_sem.at[0])]
    outputs[0].start()
    interpolate(ub, hb, ph0, pw0, zt.at[0], s, scale, uh, ul, vel)
    outputs.append(pltpu.make_async_copy(vel, vel_out, out_sem.at[1]))
    outputs[1].start()
    for group in (s_x, s_y, s_z, q_z, b_x, b_y, a_y, a_z, a_x, l_y, e_z):
        for c in group:
            c.wait_send()
    for c in outputs:
        c.wait()


def scratch():
    f = lambda *shape: pltpu.VMEM(shape, F32)
    i = lambda *shape: pltpu.VMEM(shape, jnp.int32)
    b = lambda *shape: pltpu.VMEM(shape, BF)
    grid = lambda *lead: pltpu.VMEM(lead + (PLANES, ROWS, 128), F32)
    sem = pltpu.SemaphoreType.DMA
    return [
        i(3, 8, 128), f(3, 8, 128), f(8, 128), f(3, 8, 128), f(8, 128), i(8, 128),
        f(9, 4, 8, 256), f(9, 8, 128), f(3, 8, 256), f(2, 4, 8, 256), i(3, 4, 32, 128),
        b(3, 256, PAIRS), b(3, 256, PAIRS), b(192, 512),
        f(TILES, 8, 128), f(TILES, 8, 128), f(6, TILES, 128), i(2, TILES, 128),
        f(3, 40, 256), f(3, 24, 256),
        f(2, 3, 16, 256), f(2, 24, 256), f(3, 16, 256), f(2, 2, 16, 256), f(2, 16, 256), f(9, 16, 256),
        b(800, SLOTS), b(800, SLOTS), b(2, 280, SLOTS), b(2, 280, SLOTS), f(3, 256, SLOTS),
        f(2, 160, SLOTS), f(4, 56, SLOTS), b(6, 256, SLOTS), b(6, 256, SLOTS),
        f(PLANES, CY, CZ), f(2, PLANES, 8, CZ), grid(4), grid(), f(2, PLANES // 4, ROWS, 128), f(2, PLANES // 4, ROWS, 128),
        grid(3), grid(3), grid(), grid(), grid(), grid(), grid(), b(800, 512), b(800, 512), f(3, 8, 128),
        sem((11,)), sem((28,)), sem((28,)), sem((2,)),
    ]


def body(
    cell_index, cell_offset, radius, forcing, viscosity, occupied, base_viscosity,
    pair_local, pair_owner, pair_partner, pair_slot_mask,
):
    args = [a.reshape(3, 8, 128) if a.shape[0] == 3 else a.reshape(8, 128) for a in (
        cell_index, cell_offset, radius, forcing, viscosity, occupied
    )]
    args += [base_viscosity]
    args += [a.reshape(32, 128) for a in (pair_local, pair_owner, pair_partner, pair_slot_mask)]
    field, velocity = pl.pallas_call(
        step_kernel,
        out_shape=(
            jax.ShapeDtypeStruct((3, CX, CY, CZ), F32),
            jax.ShapeDtypeStruct((3, 8, 128), F32),
        ),
        in_specs=[pl.BlockSpec(memory_space=pltpu.HBM)] * 11,
        out_specs=(pl.BlockSpec(memory_space=pltpu.HBM),) * 2,
        scratch_shapes=scratch(),
        compiler_params=pltpu.CompilerParams(
            collective_id=0, has_side_effects=True, vmem_limit_bytes=62 * 2**20
        ),
        name="coupling",
    )(*args)
    return field, velocity.reshape(3, 1, 1, 1, SLOTS)


def solution(mesh):
    line = P("gx", "gy", "gz", None)
    wide = P(None, "gx", "gy", "gz", None)
    placed = (wide, wide, line, wide, line, line, P("gx", "gy", "gz"), line, line, line, line)
    return jax.shard_map(
        body,
        mesh=mesh,
        in_specs=placed,
        out_specs=(P(None, "gx", "gy", "gz"), wide),
        check_vma=False,
    )
```

```python
import functools
import jax
import jax.numpy as jnp
from jax import lax
from jax.experimental import pallas as pl
from jax.experimental.pallas import tpu as pltpu
from jax.sharding import PartitionSpec as P

spread_sigma = 0.8
damping = 0.5
lubrication_strength = 8.0
minimum_gap = 4.0
sharpness = 1.0 / (2.0 * spread_sigma * spread_sigma)

CX, CY, CZ = 16, 32, 128
SLOTS = 1024
PAIRS = 4096
TILES = 3 * PAIRS // 128
QB = 1024
REACH = 5
PLANES = 28
ROWS = 48
ROW0 = 5
BF = jnp.bfloat16
F32 = jnp.float32
NT = (((1,), (1,)), ((), ()))
NN = (((1,), (0,)), ((), ()))
TN = (((0,), (0,)), ((), ()))


def halves(value):
    high = value.astype(BF)
    return high, (value - high.astype(F32)).astype(BF)


def dot(a, b, dims):
    return lax.dot_general(a, b, dims, preferred_element_type=F32)


def dot3(a, b, dims):
    return dot(a[0], b[0], dims) + dot(a[1], b[0], dims) + dot(a[0], b[1], dims)


def iota(shape, dim):
    return lax.broadcasted_iota(jnp.int32, shape, dim)


def roll(value, shift, axis):
    shift = shift % value.shape[axis]
    return pltpu.roll(value, shift, axis) if shift else value


def lanes(value, index):
    index = jnp.broadcast_to(index, value.shape)
    return jnp.take_along_axis(value, index, axis=1, mode="promise_in_bounds")


def gauss(shift, offset):
    t = shift + 0.5 - offset
    return jnp.exp(-(t * t) * sharpness)


def norm(offset):
    total = gauss(-2.0, offset)
    for k in range(-1, 3):
        total = total + gauss(float(k), offset)
    return total


def window(cells, target, offset):
    shift = target.astype(F32) - cells
    return jnp.where(jnp.abs(shift) <= 2.0, gauss(shift, offset), 0.0)


def hot_rows(q, hot_p, hot_a, l):
    rows = iota((256, 128), 0)

    def tile(t, carry):
        for j in range(4):
            n = t * 4 + j
            at = pl.multiple_of(n * 128, 128)
            par = q[l, 2, pl.ds(n, 1), :] & 255
            loc = q[l, 0, pl.ds(n, 1), :] & 255
            hot_p[l, :, pl.ds(at, 128)] = jnp.where(rows == par, 1.0, 0.0).astype(BF)
            hot_a[l, :, pl.ds(at, 128)] = jnp.where(rows == loc, 1.0, 0.0).astype(BF)
        return carry

    lax.fori_loop(0, PAIRS // 512, tile, 0)


def row_of(q, l, j, ch):
    n = QB // 128
    return jnp.concatenate([q[l, j, pl.ds(ch * n + t, 1), :] for t in range(n)], axis=1)


def pick(found, slab, slabs, out):
    wide = jnp.broadcast_to(slab, (8, QB))
    for n, k in enumerate(slabs):
        out = jnp.where(wide == k, found[n * 8:(n + 1) * 8], out)
    return out


def find_mine(src, q, mine, l):
    def step(t, carry):
        for j in range(4):
            n = t * 4 + j
            loc = jnp.broadcast_to(q[l, 0, pl.ds(n, 1), :], (8, 128))
            index, block = loc & 127, loc >> 7
            out = jnp.zeros((8, 128), F32)
            for k in range(8):
                out = jnp.where(block == k, lanes(src[k // 2, :, k % 2 * 128:k % 2 * 128 + 128], index), out)
            mine[l * (PAIRS // 128) + n] = out
        return carry

    lax.fori_loop(0, PAIRS // 512, step, 0, unroll=4)


def codes(own):
    one = lambda c: jnp.where(c, 1, 0)
    dx = one(own >= 9) + one(own >= 18)
    rest = own - 9 * dx
    dy = one(rest >= 3) + one(rest >= 6)
    return dx, dy, rest - 3 * dy


def find_others(s, q, hot_p, tab, tab_low, other, bricks, first):
    count = len(bricks)
    for n, brick in enumerate(bricks):
        v = jnp.concatenate([s[brick, h] for h in range(4)], axis=0)
        high = v.astype(BF)
        rest = v - high.astype(F32)
        tab[n * 32:(n + 1) * 32] = high
        tab_low[n * 16:(n + 1) * 16] = jnp.concatenate([rest[h * 8:h * 8 + 4] for h in range(4)], axis=0).astype(BF)
    slabs = [b * 4 + h for b in bricks for h in range(4)]
    tiles = QB // 128

    def step(it, carry):
        l = it // (PAIRS // QB)
        ch = it % (PAIRS // QB)
        hot = hot_p[l, :, pl.ds(pl.multiple_of(ch * QB, QB), QB)]
        dx, dy, _ = codes(row_of(q, l, 1, ch))
        slab = (dy * 3 + dx) * 4 + (row_of(q, l, 2, ch) >> 8)
        if first:
            out = jnp.zeros((8, QB), F32)
        else:
            out = jnp.concatenate([other[it * tiles + t] for t in range(tiles)], axis=1)
        out = pick(dot(tab[0:count * 32], hot, NN), slab, slabs, out)
        low = pick(dot(tab_low[0:count * 16], hot, NN), slab >> 1, [k // 2 for k in slabs[::2]], jnp.zeros((8, QB), F32))
        low = jnp.where(slab & 1 == 1, low[4:8], low[0:4])
        out = out + jnp.concatenate([low, jnp.zeros((4, QB), F32)], axis=0)
        for t in range(tiles):
            other[it * tiles + t] = out[:, t * 128:(t + 1) * 128]
        return carry

    lax.fori_loop(0, 3 * PAIRS // QB, step, 0, unroll=4)


def push_forces(q, mine, other, push, keys):
    for l in range(3):
        at = slice(l * (PAIRS // 128), (l + 1) * (PAIRS // 128))
        loc, own, par, live = (q[l, j] for j in range(4))
        dx, dy, dz = codes(own)
        m = [mine[at, r, :] for r in range(8)]
        o = [other[at, r, :] for r in range(8)]
        r = [
            (o[4 + c] - m[4 + c]) + (o[c] - m[c]) + (code - 1).astype(F32) * float(side)
            for c, (code, side) in enumerate(((dx, CX), (dy, CY), (dz, CZ)))
        ]
        spacing = jnp.sqrt(r[0] * r[0] + r[1] * r[1] + r[2] * r[2])
        clearance = spacing - m[3] - o[3]
        want = (1, 2, 0)[l]
        weight = (
            jnp.where(dz == want, live, 0).astype(F32) * m[7] * o[7] * lubrication_strength
            / (jnp.maximum(spacing, 1.0) * jnp.maximum(clearance, minimum_gap))
        )
        for c in range(3):
            v = r[c] * weight
            high = v.astype(BF).astype(F32)
            push[c, at] = high
            push[3 + c, at] = v - high
        keys[0, at] = (dy * 3 + dx) * 4 + (par >> 8)
        keys[1, at] = loc >> 8


def spread_rows(push, keys, it, count):
    cols = []
    for t in range(QB // 128):
        k = it * (QB // 128) + t
        hit = iota((count, 128), 0) == keys[pl.ds(k, 1), :]
        rows = [jnp.where(hit, push[p, pl.ds(k, 1), :], 0.0) for p in range(6)]
        cols.append(jnp.concatenate(rows, axis=0).astype(BF))
    return jnp.concatenate(cols, axis=1)


def sum_others(push, keys, hot_p, acc):
    acc[...] = jnp.zeros_like(acc)

    def step(it, carry):
        l = it // (PAIRS // QB)
        at = pl.multiple_of(it % (PAIRS // QB) * QB, QB)
        sums = dot(spread_rows(push, keys.at[0], it, 40), hot_p[l, :, pl.ds(at, QB)], NT)
        acc[...] -= (sums[0:120] + sums[120:240]).reshape(3, 40, 256)
        return carry

    lax.fori_loop(0, 3 * PAIRS // QB, step, 0, unroll=4)


def sum_mine(push, keys, hot_a, selves, l):
    selves[l] = jnp.zeros((24, 256), F32)

    def step(ch, carry):
        it = l * (PAIRS // QB) + ch
        sums = dot(spread_rows(push, keys.at[1], it, 8), hot_a[l, :, pl.ds(pl.multiple_of(ch * QB, QB), QB)], NT)
        selves[l] += sums[0:24] + sums[24:48]
        return carry

    lax.fori_loop(0, PAIRS // QB, step, 0, unroll=2)


X0 = (0, 3, 19)
NXS = (7, 20, 7)
R0 = (0, 0, 34)


def edge_rows():
    line = iota((128, 1), 0)
    k = line % 8
    low = line // 32 % 2 == 0
    kept = jnp.where(low, -5 + k, 125 + k)
    sent = jnp.where(low, -3 + k, 123 + k)
    return jnp.where(line < 64, kept, sent), line // 8 % 4


def axis_tables(s, b, kc, dx, dy, x0, nx, r0, ny):
    v = s[b, kc]
    offs = [v[c:c + 1] for c in range(3)]
    cells = [v[4 + c:5 + c] for c in range(3)]
    dx_cells = jnp.asarray(dx * CX, jnp.int32).astype(F32)
    wx = window(cells[0] + dx_cells, iota((nx, 256), 0) + (x0 - REACH), offs[0])
    wy = window(cells[1] + float(dy * CY), iota((ny, 256), 0) + (r0 - ROW0), offs[1])
    wz = window(cells[2], iota((128, 256), 0), offs[2])
    eight = iota((8, 256), 0)
    wedge = [window(cells[2], eight + z, offs[2]) for z in (-5, 125, -3, 123)]
    return wx, wy, wz, [w for w in wedge for c in range(4)]


def long_tables(s, b, dx, x0, nx, ph, pw, zt):
    def chunk(kc, carry):
        wx, wy, wz, wedge = axis_tables(s, b, kc, dx, 0, x0, nx, 0, 40)
        at = pl.ds(pl.multiple_of(kc * 256, 256), 256)
        for x in range(nx):
            high, low = halves(wx[x:x + 1] * wy)
            ph[x * 40:(x + 1) * 40, at] = high
            pw[x * 40:(x + 1) * 40, at] = low
        zt[0:128, at] = wz
        zt[128:256, at] = jnp.concatenate(wedge, axis=0)
        return carry

    lax.fori_loop(0, 4, chunk, 0)


def short_tables(s, b, dx, dy, x0, nx, pf, zh, zl):
    def chunk(kc, carry):
        wx, wy, wz, wedge = axis_tables(s, b, kc, dx, dy, x0, nx, R0[dy + 1], 8)
        at = pl.ds(pl.multiple_of(kc * 256, 256), 256)
        for x in range(nx):
            pf[x * 8:(x + 1) * 8, at] = wx[x:x + 1] * wy
        high, low = halves(wz)
        zh[0:128, at] = high
        zl[0:128, at] = low
        pairs = [jnp.concatenate(wedge[n:n + 2], axis=0) for n in (0, 4, 8, 12)]
        for n, (high, low) in enumerate(halves(p) for p in pairs):
            for k in range(2):
                rows = slice(128 + n * 32 + k * 16, 128 + n * 32 + k * 16 + 16)
                zh[rows, at] = high
                zl[rows, at] = low
        return carry

    lax.fori_loop(0, 4, chunk, 0)


def envelope_scale(s, b, h):
    total = norm(s[b, h])
    return 1.0 / (total[0:1] * total[1:2] * total[2:3])


def line_of(ref, b, c):
    return jnp.concatenate([ref[b, c * 4 + h:c * 4 + h + 1, :] for h in range(4)], axis=1)


def long_brick(ph, pw, zt, load, main, x0, nx):
    d = halves(jnp.concatenate([zt[0:128, :] * v for v in load.values()], axis=0))
    res = dot3((ph[...], pw[...]), d, NT).reshape(nx, 40, 256)
    for n, c in enumerate(load):
        main[c, pl.ds(x0, nx), 0:40, :] += res[:, :, n * 128:(n + 1) * 128]


def long_edge(ph, pw, zt, load, edge, x0, nx):
    comp = edge_rows()[1]
    v = jnp.zeros((128, SLOTS), F32)
    for c, value in load.items():
        v = jnp.where(comp == c, value, v)
    high, low = halves(zt[128:256, :] * v)
    res = dot(ph[...], jnp.concatenate([high, low], axis=0), NT)
    res = res[:, 0:128] + res[:, 128:256] + dot(pw[...], high, NT)
    edge[pl.ds(x0, nx), 0:40, :] += res.reshape(nx, 40, 128)


def short_brick(pf, zh, zl, load, main, edge, x0, nx, r0):
    lane = iota((nx, 8, 128), 2)
    value = jnp.concatenate([pf[...] * v for v in load.values()], axis=0)
    res = dot3(halves(value), (zh[...], zl[...]), NT).reshape(len(load), nx, 8, 256)
    rim = jnp.zeros((nx, 8, 128), F32)
    for n, c in enumerate(load):
        main[c, pl.ds(x0, nx), r0:r0 + 8, :] += res[n, :, :, 0:128]
        rim = jnp.where(lane // 8 % 4 == c, res[n, :, :, 128:256], rim)
    edge[pl.ds(x0, nx), r0:r0 + 8, :] += rim


def assemble_base(bx, by, i):
    rows = jnp.concatenate([by[0, i], bx[i], by[1, i]], axis=0)
    return roll(rows, ROW0 - 8, 0)


def wrap_rims(bx, by, edge, pack):
    lane = iota((ROWS, 128), 1)
    within = [(29, 32, 0), (56, 59, 125), (91, 96, 0), (120, 125, 123)]
    index = lane
    mask = lane < 0
    for first, last, z in within:
        inside = (lane >= first) & (lane < last)
        index = jnp.where(inside, lane - first + z, index)
        mask = mask | inside

    def wrap(g, carry):
        tiles = []
        for j in range(4):
            i = g * 4 + j
            b = assemble_base(bx, by, i)
            t = edge[i] + jnp.where(mask, lanes(b, index), 0.0)
            edge[i] = t
            tiles.append(t)
        for side in range(2):
            out = jnp.zeros((ROWS, 128), F32)
            for j in range(4):
                out = jnp.where(lane // 32 == j, roll(tiles[j], 32 * j - 64 - 32 * side, 1), out)
            pack[side, g] = out
        return carry

    lax.fori_loop(0, PLANES // 4, wrap, 0)


def add_base(bx, by, main):
    def plane(g, carry):
        for j in range(4):
            i = g * 4 + j
            main[3, i] += assemble_base(bx, by, i)
        return carry

    lax.fori_loop(0, PLANES // 4, plane, 0)


def first_sweep(main, edge, rim, ua, ha, inv, hvisco, hinv, got_high, got_low):
    lane = iota((ROWS, 128), 1)
    thick = lane // 32 * 32 + 24 + lane % 8

    def unpack(g, carry):
        from_low, from_high = rim[0, g], rim[1, g]
        for j in range(4):
            i = g * 4 + j
            got = jnp.where(lane < 32, roll(from_low, -32 * j, 1), 0.0)
            got = jnp.where(lane // 32 == 1, roll(from_high, 32 - 32 * j, 1), got)
            high, low = halves(got)
            at = pl.ds(pl.multiple_of(i * ROWS, ROWS), ROWS)
            got_high[at] = high
            got_low[at] = low
            total = jnp.where(lane < 64, edge[i], 0.0) + got
            v = lanes(total, thick)
            r = 1.0 / (damping + 6.0 * v)
            hvisco[i] = v
            hinv[i] = r
            edge[i] = total
            ha[i] = total * r
        return carry

    lax.fori_loop(0, PLANES // 4, unpack, 0)

    source, col = iota((128, 256), 0), iota((128, 256), 1)
    z = col & 127
    for c in (0, 2):
        wanted = jnp.where(z < 2, z + 5, z + (33 - 126)) + (c + (col >> 7)) * 8
        ones = jnp.where((source == wanted) & ((z < 2) | (z >= 126)), 1.0, 0.0).astype(BF)
        near = dot(got_high[...], ones, NN) + dot(got_low[...], ones, NN)
        near = near.reshape(PLANES, ROWS, 256)
        main[c] += near[:, :, 0:128]
        main[c + 1] += near[:, :, 128:256]

    def start(i, carry):
        r = 1.0 / (damping + 6.0 * main[3, i])
        inv[i] = r
        for c in range(3):
            ua[c, i] = main[c, i] * r
        return carry

    lax.fori_loop(0, PLANES, start, 0, unroll=4)


def sweep(src, dst, hsrc, hdst, main, edge, inv, hvisco, hinv, first, rows):
    lane = iota((rows, 128), 1)
    at = slice(0, rows)

    def next_row(value, ref, *lead):
        return ref[(*lead, slice(1, rows + 1))] if rows < ROWS else roll(value, -1, 0)

    def plane(i, carry):
        h = hsrc[i, at]
        beside = hsrc[i - 1, at] + hsrc[i + 1, at] + roll(h, 1, 0) + next_row(h, hsrc, i) + roll(h, 1, 1) + roll(h, -1, 1)
        hdst[i, at] = (edge[i, at] + hvisco[i, at] * beside) * hinv[i, at]
        v, r = main[3, i, at], inv[i, at]
        for c in range(3):
            u = src[c, i, at]
            rim = lanes(h, jnp.where(lane == 0, c * 8 + 4, 35 + c * 8))
            before = jnp.where(lane == 0, rim, roll(u, 1, 1))
            after = jnp.where(lane == 127, rim, roll(u, -1, 1))
            beside = src[c, i - 1, at] + src[c, i + 1, at] + roll(u, 1, 0) + next_row(u, src, c, i) + before + after
            dst[c, i, at] = (main[c, i, at] + v * beside) * r
        return carry

    lax.fori_loop(first, 26 - first, plane, 0, unroll=True)


def interpolate(ub, hb, ph, pw, zt, s, scale, uh, ul, out):
    for x in range(20):
        row = jnp.concatenate([ub[0, x + 3, 0:40], ub[1, x + 3, 0:40], ub[2, x + 3, 0:40], hb[x + 3, 0:40]], axis=1)
        high, low = halves(row)
        uh[x * 40:(x + 1) * 40] = high
        ul[x * 40:(x + 1) * 40] = low
    field = uh[...].T[0:448], ul[...].T[0:448]
    z, comp = (v[0:64] for v in edge_rows())
    outside = (z < 0) | (z >= CZ)
    for pc in range(4):
        at = slice(pc * 256, (pc + 1) * 256)
        res = dot3(field, (ph[:, at], pw[:, at]), NN)
        wz = zt[0:128, at]
        rim = jnp.where(outside, zt[128:192, at] * res[384:448], 0.0)
        factor = s[4, pc, 7:8, :] * scale[1, pc:pc + 1, :]
        for c in range(3):
            value = jnp.sum(res[c * 128:(c + 1) * 128] * wz, axis=0, keepdims=True)
            value = (value + jnp.sum(jnp.where(comp == c, rim, 0.0), axis=0, keepdims=True)) * factor
            out[c, 2 * pc:2 * pc + 1, :] = value[:, 0:128]
            out[c, 2 * pc + 1:2 * pc + 2, :] = value[:, 128:256]


def step_kernel(
    cell_in, offset_in, radius_in, force_in, visc_in, live_in, base_in,
    local_in, owner_in, partner_in, mask_in,
    field_out, vel_out,
    cell, offset, radius, force, visc, alive,
    s, thick, scale, zs, q, hot_p, hot_a, tab, tab_low, mine, other, push, keys, acc, selves,
    ry, rz, xs, rx1, rx2, loads,
    ph0, pw0, ph1, pw1, zt, pfy, pfd, zh, zl,
    bx, by, main, edge, pack, rim,
    ua, ub, ha, hb, inv, hvisco, hinv, got_high, got_low, uh, ul, vel,
    in_sem, send_sem, recv_sem, out_sem,
):
    me = {a: lax.axis_index(a) for a in ("gx", "gy", "gz")}

    def near(axis, step):
        n = lax.axis_size(axis)
        return {axis: lax.rem(me[axis] + step + n, n)}

    inputs = [
        (cell_in, cell), (offset_in, offset), (radius_in, radius), (force_in, force), (visc_in, visc),
        (live_in, alive), (base_in, bx.at[pl.ds(REACH, CX)]), (local_in, q.at[0, 0]), (owner_in, q.at[0, 1]),
        (partner_in, q.at[0, 2]), (mask_in, q.at[0, 3]),
    ]
    inputs = [pltpu.make_async_copy(a, b, in_sem.at[n]) for n, (a, b) in enumerate(inputs)]
    for c in inputs:
        c.start()

    barrier = pltpu.get_barrier_semaphore()
    greeted = [("gx", 1), ("gx", -1), ("gx", 2), ("gx", -2), ("gy", 1), ("gy", -1), ("gz", 1), ("gz", -1)]
    for axis, step in greeted:
        pl.semaphore_signal(barrier, inc=1, device_id=near(axis, step), device_id_type=pl.DeviceIdType.MESH)

    count = [0]

    def copy(src, dst, axis, step):
        n = count[0]
        count[0] += 1
        return pltpu.make_async_remote_copy(
            src_ref=src, dst_ref=dst, send_sem=send_sem.at[n], recv_sem=recv_sem.at[n],
            device_id=near(axis, step), device_id_type=pl.DeviceIdType.MESH,
        )

    three, low3, high3 = pl.ds(3, 3), pl.ds(0, 3), pl.ds(6, 3)
    s_x = [copy(s.at[4], s.at[3], "gx", 1), copy(s.at[4], s.at[5], "gx", -1)]
    s_x += [copy(thick.at[4], thick.at[3], "gx", 1), copy(thick.at[4], thick.at[5], "gx", -1)]
    s_y = [copy(s.at[three], s.at[low3], "gy", 1), copy(s.at[three], s.at[high3], "gy", -1)]
    s_y += [copy(thick.at[three], thick.at[low3], "gy", 1), copy(thick.at[three], thick.at[high3], "gy", -1)]
    s_z = [copy(s.at[4], zs.at[0], "gz", 1), copy(s.at[4], zs.at[1], "gz", -1)]
    q_z = [copy(q.at[0], q.at[1], "gz", 1), copy(q.at[0], q.at[2], "gz", -1)]
    b_x = [
        copy(bx.at[pl.ds(CX, REACH)], bx.at[pl.ds(0, REACH)], "gx", 1),
        copy(bx.at[pl.ds(REACH, REACH)], bx.at[pl.ds(CX + REACH, REACH)], "gx", -1),
    ]
    b_y = [
        copy(bx.at[:, pl.ds(CY - 8, 8)], by.at[0], "gy", 1),
        copy(bx.at[:, pl.ds(0, 8)], by.at[1], "gy", -1),
    ]
    a_y = [copy(acc.at[:, pl.ds(24, 16)], ry.at[0], "gy", 1), copy(acc.at[:, pl.ds(0, 16)], ry.at[1], "gy", -1)]
    a_z = [copy(selves.at[1], rz.at[0], "gz", -1), copy(selves.at[2], rz.at[1], "gz", 1)]
    a_x = [
        copy(xs.at[pl.ds(1, 2)], rx1.at[0], "gx", 1), copy(xs.at[pl.ds(0, 2)], rx1.at[1], "gx", -1),
        copy(xs.at[2], rx2.at[0], "gx", 2), copy(xs.at[0], rx2.at[1], "gx", -2),
    ]
    l_y = [copy(loads.at[three], loads.at[low3], "gy", 1), copy(loads.at[three], loads.at[high3], "gy", -1)]
    e_z = [copy(pack.at[0], rim.at[1], "gz", -1), copy(pack.at[1], rim.at[0], "gz", 1)]

    def start(copies):
        for c in copies:
            c.start()

    def arrived(copies):
        for c in copies:
            c.wait_recv()

    for c in inputs:
        c.wait()
    flags = alive[...].astype(F32)
    rows = [offset[c] for c in range(3)] + [radius[...]] + [cell[c].astype(F32) for c in range(3)] + [flags]
    for r, v in enumerate(rows):
        for h in range(4):
            s[4, h, r:r + 1, 0:128] = v[2 * h:2 * h + 1]
            s[4, h, r:r + 1, 128:256] = v[2 * h + 1:2 * h + 2]
    for h in range(4):
        scale[1, h:h + 1, :] = envelope_scale(s, 4, h)
    for h in range(4):
        for k in range(2):
            row = slice(2 * h + k, 2 * h + k + 1)
            thick[4, row, :] = visc[row, :] * flags[row] * scale[1, h:h + 1, k * 128:(k + 1) * 128]
    pl.semaphore_wait(barrier, len(greeted))
    start(s_x)
    start(s_z)
    start(q_z)

    bx[26:28] = jnp.zeros((2, CY, CZ), F32)
    hot_rows(q, hot_p, hot_a, 0)
    find_mine(s.at[4], q, mine, 0)
    arrived(s_z)
    arrived(q_z)
    hot_rows(q, hot_p, hot_a, 1)
    find_mine(zs.at[0], q, mine, 1)
    hot_rows(q, hot_p, hot_a, 2)
    find_mine(zs.at[1], q, mine, 2)
    arrived(s_x)
    start(s_y)
    find_others(s, q, hot_p, tab, tab_low, other, (3, 4, 5), True)
    arrived(s_y)
    start(b_x)

    find_others(s, q, hot_p, tab, tab_low, other, (0, 1, 2, 6, 7, 8), False)
    push_forces(q, mine, other, push, keys)
    sum_others(push, keys, hot_p, acc)
    start(a_y)
    sum_mine(push, keys, hot_a, selves, 1)
    sum_mine(push, keys, hot_a, selves, 2)
    start(a_z)
    sum_mine(push, keys, hot_a, selves, 0)

    long_tables(s, 4, 0, 3, 20, ph0, pw0, zt.at[0])

    def side_tables(it, carry):
        long_tables(s, 3 + 2 * it, 2 * it - 1, it * 19, 7, ph1.at[it], pw1.at[it], zt.at[1 + it])
        return carry

    arrived(a_y)
    arrived(a_z)
    xs[...] = jnp.zeros_like(xs)
    for c in range(3):
        middle = acc[c, 12:24] + ry[0, c, 0:12] + ry[1, c, 0:12]
        f = force[c]
        f = jnp.concatenate(
            [jnp.concatenate([f[2 * h:2 * h + 1], f[2 * h + 1:2 * h + 2]], axis=1) for h in range(4)], axis=0
        )
        at = slice(c * 8, c * 8 + 4)
        f = f + selves[0, at] + rz[0, at] + rz[1, at]
        xs[0, c * 4:c * 4 + 4] = middle[0:4]
        xs[1, c * 4:c * 4 + 4] = middle[4:8] + f
        xs[2, c * 4:c * 4 + 4] = middle[8:12]
    start(a_x)

    def thickness(b):
        return jnp.concatenate([thick[b, t:t + 1, :] for t in range(8)], axis=1)

    def forces(b):
        return {c: line_of(loads, b, c) for c in range(3)}

    def everything(b):
        return {**forces(b), 3: thickness(b)}

    def long_all(comps, what, *out):
        def part(b):
            load = everything(b)
            return {c: load[c] for c in comps}

        what(ph0, pw0, zt.at[0], part(4), *out, 3, 20)

        def side(it, carry):
            what(ph1.at[it], pw1.at[it], zt.at[1 + it], part(3 + 2 * it), *out, it * 19, 7)
            return carry

        lax.fori_loop(0, 2, side, 0, unroll=True)

    lax.fori_loop(0, 2, side_tables, 0)
    for h in range(4):
        for n in (0, 2):
            scale[n, h:h + 1, :] = envelope_scale(s, 3 + n, h)
    for n, dy in enumerate((-1, 1)):
        short_tables(s, 3 * (dy + 1) + 1, 0, dy, 3, 20, pfy.at[n], zh.at[n * 3], zl.at[n * 3])

        def corner(it, carry):
            k = n * 3 + 1 + it
            short_tables(s, 3 * (dy + 1) + 2 * it, 2 * it - 1, dy, it * 19, 7, pfd.at[n * 2 + it], zh.at[k], zl.at[k])
            return carry

        lax.fori_loop(0, 2, corner, 0)
    main[...] = jnp.zeros_like(main)
    edge[...] = jnp.zeros_like(edge)
    arrived(a_x)
    for n in range(3):
        if n == 0:
            total = rx1[0, 0] + rx2[0] + xs[0]
        elif n == 1:
            total = xs[1] + rx1[0, 1] + rx1[1, 0]
        else:
            total = rx1[1, 1] + rx2[1] + xs[2]
        for h in range(4):
            on = s[3 + n, h, 7:8, :] * scale[n, h:h + 1, :]
            for c in range(3):
                loads[3 + n, c * 4 + h:c * 4 + h + 1, :] = on * total[c * 4 + h:c * 4 + h + 1]
        loads[3 + n, 12:16] = jnp.zeros((4, 256), F32)
    start(l_y)
    arrived(b_x)
    start(b_y)

    long_all(range(4), long_edge, edge)
    arrived(l_y)
    for n, dy in enumerate((-1, 1)):
        k = n * 3
        b = 3 * (dy + 1) + 1
        short_brick(pfy[n], zh.at[k], zl.at[k], everything(b), main, edge, 3, 20, R0[dy + 1])

        def corner(it, carry):
            k = n * 3 + 1 + it
            b = 3 * (dy + 1) + 2 * it
            load = everything(b)
            short_brick(pfd[n * 2 + it], zh.at[k], zl.at[k], load, main, edge, it * 19, 7, R0[dy + 1])
            return carry

        lax.fori_loop(0, 2, corner, 0, unroll=True)
    arrived(b_y)
    wrap_rims(bx, by, edge, pack)
    start(e_z)
    long_all((0, 1), long_brick, main)
    long_all((2, 3), long_brick, main)
    add_base(bx, by, main)
    arrived(e_z)

    first_sweep(main, edge, rim, ua, ha, inv, hvisco, hinv, got_high, got_low)
    rest = (main, edge, inv, hvisco, hinv)
    sweep(ua, ub, ha, hb, *rest, 1, 48)
    sweep(ub, ua, hb, ha, *rest, 2, 40)
    sweep(ua, ub, ha, hb, *rest, 3, 40)

    def finish(x, carry):
        for c in range(3):
            ua[c, x, 0:CY] = ub[c, x + REACH, ROW0:ROW0 + CY, :]
        return carry

    lax.fori_loop(0, CX, finish, 0)
    outputs = [pltpu.make_async_copy(ua.at[:, pl.ds(0, CX), pl.ds(0, CY)], field_out, out_sem.at[0])]
    outputs[0].start()
    interpolate(ub, hb, ph0, pw0, zt.at[0], s, scale, uh, ul, vel)
    outputs.append(pltpu.make_async_copy(vel, vel_out, out_sem.at[1]))
    outputs[1].start()
    for group in (s_x, s_y, s_z, q_z, b_x, b_y, a_y, a_z, a_x, l_y, e_z):
        for c in group:
            c.wait_send()
    for c in outputs:
        c.wait()


def hand_over(field, velocity, field_out, velocity_out, sem):
    copies = [pltpu.make_async_copy(velocity, velocity_out, sem.at[12])]
    for n in range(12):
        at = (n // 4, pl.ds(n % 4 * 4, 4))
        copies.append(pltpu.make_async_copy(field.at[at], field_out.at[at], sem.at[n]))
    for c in copies:
        c.start()
    for c in copies:
        c.wait()


def scratch():
    f = lambda *shape: pltpu.VMEM(shape, F32)
    i = lambda *shape: pltpu.VMEM(shape, jnp.int32)
    b = lambda *shape: pltpu.VMEM(shape, BF)
    grid = lambda *lead: pltpu.VMEM(lead + (PLANES, ROWS, 128), F32)
    sem = pltpu.SemaphoreType.DMA
    return [
        i(3, 8, 128), f(3, 8, 128), f(8, 128), f(3, 8, 128), f(8, 128), i(8, 128),
        f(9, 4, 8, 256), f(9, 8, 128), f(3, 8, 256), f(2, 4, 8, 256), i(3, 4, 32, 128),
        b(3, 256, PAIRS), b(3, 256, PAIRS), b(192, 256), b(96, 256),
        f(TILES, 8, 128), f(TILES, 8, 128), f(6, TILES, 128), i(2, TILES, 128),
        f(3, 40, 256), f(3, 24, 256),
        f(2, 3, 16, 256), f(2, 24, 256), f(3, 16, 256), f(2, 2, 16, 256), f(2, 16, 256), f(9, 16, 256),
        b(800, SLOTS), b(800, SLOTS), b(2, 280, SLOTS), b(2, 280, SLOTS), f(3, 256, SLOTS),
        f(2, 160, SLOTS), f(4, 56, SLOTS), b(6, 256, SLOTS), b(6, 256, SLOTS),
        f(PLANES, CY, CZ), f(2, PLANES, 8, CZ), grid(4), grid(), f(2, PLANES // 4, ROWS, 128), f(2, PLANES // 4, ROWS, 128),
        grid(3), grid(3), grid(), grid(), grid(), grid(), grid(), b(PLANES * ROWS, 128), b(PLANES * ROWS, 128), b(800, 512), b(800, 512), f(3, 8, 128),
        sem((11,)), sem((28,)), sem((28,)), sem((2,)),
    ]


def body(
    cell_index, cell_offset, radius, forcing, viscosity, occupied, base_viscosity,
    pair_local, pair_owner, pair_partner, pair_slot_mask,
):
    args = [a.reshape(3, 8, 128) if a.shape[0] == 3 else a.reshape(8, 128) for a in (
        cell_index, cell_offset, radius, forcing, viscosity, occupied
    )]
    args += [base_viscosity]
    args += [a.reshape(32, 128) for a in (pair_local, pair_owner, pair_partner, pair_slot_mask)]
    hbm = pl.BlockSpec(memory_space=pltpu.HBM)
    results = (
        jax.ShapeDtypeStruct((3, CX, CY, CZ), F32),
        jax.ShapeDtypeStruct((3, 8, 128), F32),
    )
    results = pl.pallas_call(
        step_kernel,
        out_shape=results,
        in_specs=[hbm] * 11,
        out_specs=(hbm,) * 2,
        scratch_shapes=scratch(),
        compiler_params=pltpu.CompilerParams(
            collective_id=0, has_side_effects=True, vmem_limit_bytes=62 * 2**20
        ),
        name="coupling",
    )(*args)
    field, velocity = pl.pallas_call(
        hand_over,
        out_shape=(
            jax.ShapeDtypeStruct((3, CX, CY, CZ), F32),
            jax.ShapeDtypeStruct((3, 8, 128), F32),
        ),
        in_specs=[hbm] * 2,
        out_specs=(hbm,) * 2,
        scratch_shapes=[pltpu.SemaphoreType.DMA((13,))],
        compiler_params=pltpu.CompilerParams(vmem_limit_bytes=62 * 2**20),
        name="hand_over",
    )(*results)
    return field, velocity.reshape(3, 1, 1, 1, SLOTS)


def solution(mesh):
    line = P("gx", "gy", "gz", None)
    wide = P(None, "gx", "gy", "gz", None)
    placed = (wide, wide, line, wide, line, line, P("gx", "gy", "gz"), line, line, line, line)
    return jax.shard_map(
        body,
        mesh=mesh,
        in_specs=placed,
        out_specs=(P(None, "gx", "gy", "gz"), wide),
        check_vma=False,
    )
```

```python
import functools
import jax
import jax.numpy as jnp
from jax import lax
from jax.experimental import pallas as pl
from jax.experimental.pallas import tpu as pltpu
from jax.sharding import PartitionSpec as P

spread_sigma = 0.8
damping = 0.5
lubrication_strength = 8.0
minimum_gap = 4.0
sharpness = 1.0 / (2.0 * spread_sigma * spread_sigma)

CX, CY, CZ = 16, 32, 128
SLOTS = 1024
PAIRS = 4096
TILES = 3 * PAIRS // 128
QB = 1024
REACH = 5
PLANES = 28
ROWS = 48
ROW0 = 5
BF = jnp.bfloat16
F32 = jnp.float32
NT = (((1,), (1,)), ((), ()))
NN = (((1,), (0,)), ((), ()))
TN = (((0,), (0,)), ((), ()))


def halves(value):
    high = value.astype(BF)
    return high, (value - high.astype(F32)).astype(BF)


def dot(a, b, dims):
    return lax.dot_general(a, b, dims, preferred_element_type=F32)


def dot3(a, b, dims):
    return dot(a[0], b[0], dims) + dot(a[1], b[0], dims) + dot(a[0], b[1], dims)


def iota(shape, dim):
    return lax.broadcasted_iota(jnp.int32, shape, dim)


def roll(value, shift, axis):
    shift = shift % value.shape[axis]
    return pltpu.roll(value, shift, axis) if shift else value


def lanes(value, index):
    index = jnp.broadcast_to(index, value.shape)
    return jnp.take_along_axis(value, index, axis=1, mode="promise_in_bounds")


def gauss(shift, offset):
    t = shift + 0.5 - offset
    return jnp.exp(-(t * t) * sharpness)


def norm(offset):
    total = gauss(-2.0, offset)
    for k in range(-1, 3):
        total = total + gauss(float(k), offset)
    return total


def window(cells, target, offset):
    shift = target.astype(F32) - cells
    return jnp.where(jnp.abs(shift) <= 2.0, gauss(shift, offset), 0.0)


def hot_rows(q, hot_p, hot_a, l):
    rows = iota((256, 128), 0)

    def tile(t, carry):
        for j in range(4):
            n = t * 4 + j
            at = pl.multiple_of(n * 128, 128)
            par = q[l, 2, pl.ds(n, 1), :] & 255
            loc = q[l, 0, pl.ds(n, 1), :] & 255
            hot_p[l, :, pl.ds(at, 128)] = jnp.where(rows == par, 1.0, 0.0).astype(BF)
            hot_a[l, :, pl.ds(at, 128)] = jnp.where(rows == loc, 1.0, 0.0).astype(BF)
        return carry

    lax.fori_loop(0, PAIRS // 512, tile, 0)


def row_of(q, l, j, ch):
    n = QB // 128
    return jnp.concatenate([q[l, j, pl.ds(ch * n + t, 1), :] for t in range(n)], axis=1)


def pick(found, slab, slabs, out):
    wide = jnp.broadcast_to(slab, (8, QB))
    for n, k in enumerate(slabs):
        out = jnp.where(wide == k, found[n * 8:(n + 1) * 8], out)
    return out


def find_mine(src, q, mine, l):
    def step(t, carry):
        for j in range(4):
            n = t * 4 + j
            loc = jnp.broadcast_to(q[l, 0, pl.ds(n, 1), :], (8, 128))
            index, block = loc & 127, loc >> 7
            out = jnp.zeros((8, 128), F32)
            for k in range(8):
                out = jnp.where(block == k, lanes(src[k // 2, :, k % 2 * 128:k % 2 * 128 + 128], index), out)
            mine[l * (PAIRS // 128) + n] = out
        return carry

    lax.fori_loop(0, PAIRS // 512, step, 0, unroll=4)


def codes(own):
    one = lambda c: jnp.where(c, 1, 0)
    dx = one(own >= 9) + one(own >= 18)
    rest = own - 9 * dx
    dy = one(rest >= 3) + one(rest >= 6)
    return dx, dy, rest - 3 * dy


def find_others(s, q, hot_p, tab, tab_low, other, bricks, first):
    count = len(bricks)
    for n, brick in enumerate(bricks):
        v = jnp.concatenate([s[brick, h] for h in range(4)], axis=0)
        high = v.astype(BF)
        rest = v - high.astype(F32)
        tab[n * 32:(n + 1) * 32] = high
        tab_low[n * 16:(n + 1) * 16] = jnp.concatenate([rest[h * 8:h * 8 + 4] for h in range(4)], axis=0).astype(BF)
    slabs = [b * 4 + h for b in bricks for h in range(4)]
    tiles = QB // 128

    def step(it, carry):
        l = it // (PAIRS // QB)
        ch = it % (PAIRS // QB)
        hot = hot_p[l, :, pl.ds(pl.multiple_of(ch * QB, QB), QB)]
        dx, dy, _ = codes(row_of(q, l, 1, ch))
        slab = (dy * 3 + dx) * 4 + (row_of(q, l, 2, ch) >> 8)
        if first:
            out = jnp.zeros((8, QB), F32)
        else:
            out = jnp.concatenate([other[it * tiles + t] for t in range(tiles)], axis=1)
        out = pick(dot(tab[0:count * 32], hot, NN), slab, slabs, out)
        low = pick(dot(tab_low[0:count * 16], hot, NN), slab >> 1, [k // 2 for k in slabs[::2]], jnp.zeros((8, QB), F32))
        low = jnp.where(slab & 1 == 1, low[4:8], low[0:4])
        out = out + jnp.concatenate([low, jnp.zeros((4, QB), F32)], axis=0)
        for t in range(tiles):
            other[it * tiles + t] = out[:, t * 128:(t + 1) * 128]
        return carry

    lax.fori_loop(0, 3 * PAIRS // QB, step, 0, unroll=4)


def push_forces(q, mine, other, push, keys):
    for l in range(3):
        at = slice(l * (PAIRS // 128), (l + 1) * (PAIRS // 128))
        loc, own, par, live = (q[l, j] for j in range(4))
        dx, dy, dz = codes(own)
        m = [mine[at, r, :] for r in range(8)]
        o = [other[at, r, :] for r in range(8)]
        r = [
            (o[4 + c] - m[4 + c]) + (o[c] - m[c]) + (code - 1).astype(F32) * float(side)
            for c, (code, side) in enumerate(((dx, CX), (dy, CY), (dz, CZ)))
        ]
        spacing = jnp.sqrt(r[0] * r[0] + r[1] * r[1] + r[2] * r[2])
        clearance = spacing - m[3] - o[3]
        want = (1, 2, 0)[l]
        weight = (
            jnp.where(dz == want, live, 0).astype(F32) * m[7] * o[7] * lubrication_strength
            / (jnp.maximum(spacing, 1.0) * jnp.maximum(clearance, minimum_gap))
        )
        for c in range(3):
            v = r[c] * weight
            high = v.astype(BF).astype(F32)
            push[c, at] = high
            push[3 + c, at] = v - high
        keys[0, at] = (dy * 3 + dx) * 4 + (par >> 8)
        keys[1, at] = loc >> 8


def spread_rows(push, keys, it, count):
    cols = []
    for t in range(QB // 128):
        k = it * (QB // 128) + t
        hit = iota((count, 128), 0) == keys[pl.ds(k, 1), :]
        rows = [jnp.where(hit, push[p, pl.ds(k, 1), :], 0.0) for p in range(6)]
        cols.append(jnp.concatenate(rows, axis=0).astype(BF))
    return jnp.concatenate(cols, axis=1)


def sum_others(push, keys, hot_p, acc):
    acc[...] = jnp.zeros_like(acc)

    def step(it, carry):
        l = it // (PAIRS // QB)
        at = pl.multiple_of(it % (PAIRS // QB) * QB, QB)
        sums = dot(spread_rows(push, keys.at[0], it, 40), hot_p[l, :, pl.ds(at, QB)], NT)
        acc[...] -= (sums[0:120] + sums[120:240]).reshape(3, 40, 256)
        return carry

    lax.fori_loop(0, 3 * PAIRS // QB, step, 0, unroll=4)


def sum_mine(push, keys, hot_a, selves, l):
    selves[l] = jnp.zeros((24, 256), F32)

    def step(ch, carry):
        it = l * (PAIRS // QB) + ch
        sums = dot(spread_rows(push, keys.at[1], it, 8), hot_a[l, :, pl.ds(pl.multiple_of(ch * QB, QB), QB)], NT)
        selves[l] += sums[0:24] + sums[24:48]
        return carry

    lax.fori_loop(0, PAIRS // QB, step, 0, unroll=2)


X0 = (0, 3, 19)
NXS = (7, 20, 7)
R0 = (0, 0, 34)


def edge_rows():
    line = iota((128, 1), 0)
    k = line % 8
    low = line // 32 % 2 == 0
    kept = jnp.where(low, -5 + k, 125 + k)
    sent = jnp.where(low, -3 + k, 123 + k)
    return jnp.where(line < 64, kept, sent), line // 8 % 4


def axis_tables(s, b, kc, dx, dy, x0, nx, r0, ny):
    v = s[b, kc]
    offs = [v[c:c + 1] for c in range(3)]
    cells = [v[4 + c:5 + c] for c in range(3)]
    dx_cells = jnp.asarray(dx * CX, jnp.int32).astype(F32)
    wx = window(cells[0] + dx_cells, iota((nx, 256), 0) + (x0 - REACH), offs[0])
    wy = window(cells[1] + float(dy * CY), iota((ny, 256), 0) + (r0 - ROW0), offs[1])
    wz = window(cells[2], iota((128, 256), 0), offs[2])
    eight = iota((8, 256), 0)
    wedge = [window(cells[2], eight + z, offs[2]) for z in (-5, 125, -3, 123)]
    return wx, wy, wz, [w for w in wedge for c in range(4)]


def long_tables(s, b, dx, x0, nx, ph, pw, zt):
    def chunk(kc, carry):
        wx, wy, wz, wedge = axis_tables(s, b, kc, dx, 0, x0, nx, 0, 40)
        at = pl.ds(pl.multiple_of(kc * 256, 256), 256)
        for x in range(nx):
            high, low = halves(wx[x:x + 1] * wy)
            ph[x * 40:(x + 1) * 40, at] = high
            pw[x * 40:(x + 1) * 40, at] = low
        zt[0:128, at] = wz
        zt[128:256, at] = jnp.concatenate(wedge, axis=0)
        return carry

    lax.fori_loop(0, 4, chunk, 0)


def short_tables(s, b, dx, dy, x0, nx, pf, zh, zl):
    def chunk(kc, carry):
        wx, wy, wz, wedge = axis_tables(s, b, kc, dx, dy, x0, nx, R0[dy + 1], 8)
        at = pl.ds(pl.multiple_of(kc * 256, 256), 256)
        for x in range(nx):
            pf[x * 8:(x + 1) * 8, at] = wx[x:x + 1] * wy
        high, low = halves(wz)
        zh[0:128, at] = high
        zl[0:128, at] = low
        pairs = [jnp.concatenate(wedge[n:n + 2], axis=0) for n in (0, 4, 8, 12)]
        for n, (high, low) in enumerate(halves(p) for p in pairs):
            for k in range(2):
                rows = slice(128 + n * 32 + k * 16, 128 + n * 32 + k * 16 + 16)
                zh[rows, at] = high
                zl[rows, at] = low
        return carry

    lax.fori_loop(0, 4, chunk, 0)


def envelope_scale(s, b, h):
    total = norm(s[b, h])
    return 1.0 / (total[0:1] * total[1:2] * total[2:3])


def line_of(ref, b, c):
    return jnp.concatenate([ref[b, c * 4 + h:c * 4 + h + 1, :] for h in range(4)], axis=1)


def long_brick(ph, pw, zt, load, main, x0, nx):
    d = halves(jnp.concatenate([zt[0:128, :] * v for v in load.values()], axis=0))
    res = dot3((ph[...], pw[...]), d, NT).reshape(nx, 40, 256)
    for n, c in enumerate(load):
        main[c, pl.ds(x0, nx), 0:40, :] += res[:, :, n * 128:(n + 1) * 128]


def narrow(ph, pw, d, nx):
    high, low = halves(d)
    res = dot(ph[...], jnp.concatenate([high, low], axis=0), NT)
    res = res[:, 0:128] + res[:, 128:256] + dot(pw[...], high, NT)
    return res.reshape(nx, 40, 128)


def long_one(ph, pw, zt, load, main, x0, nx):
    (c, v), = load.items()
    main[c, pl.ds(x0, nx), 0:40, :] += narrow(ph, pw, zt[0:128, :] * v, nx)


def long_edge(ph, pw, zt, load, edge, x0, nx):
    comp = edge_rows()[1]
    v = jnp.zeros((128, SLOTS), F32)
    for c, value in load.items():
        v = jnp.where(comp == c, value, v)
    edge[pl.ds(x0, nx), 0:40, :] += narrow(ph, pw, zt[128:256, :] * v, nx)


def short_brick(pf, zh, zl, load, main, edge, x0, nx, r0):
    lane = iota((nx, 8, 128), 2)
    value = jnp.concatenate([pf[...] * v for v in load.values()], axis=0)
    res = dot3(halves(value), (zh[...], zl[...]), NT).reshape(len(load), nx, 8, 256)
    rim = jnp.zeros((nx, 8, 128), F32)
    for n, c in enumerate(load):
        main[c, pl.ds(x0, nx), r0:r0 + 8, :] += res[n, :, :, 0:128]
        rim = jnp.where(lane // 8 % 4 == c, res[n, :, :, 128:256], rim)
    edge[pl.ds(x0, nx), r0:r0 + 8, :] += rim


def assemble_base(bx, by, i):
    rows = jnp.concatenate([by[0, i], bx[i], by[1, i]], axis=0)
    return roll(rows, ROW0 - 8, 0)


def wrap_rims(bx, by, edge, pack):
    lane = iota((ROWS, 128), 1)
    within = [(29, 32, 0), (56, 59, 125), (91, 96, 0), (120, 125, 123)]
    index = lane
    mask = lane < 0
    for first, last, z in within:
        inside = (lane >= first) & (lane < last)
        index = jnp.where(inside, lane - first + z, index)
        mask = mask | inside

    def wrap(g, carry):
        tiles = []
        for j in range(4):
            i = g * 4 + j
            b = assemble_base(bx, by, i)
            t = edge[i] + jnp.where(mask, lanes(b, index), 0.0)
            edge[i] = t
            tiles.append(t)
        for side in range(2):
            out = jnp.zeros((ROWS, 128), F32)
            for j in range(4):
                out = jnp.where(lane // 32 == j, roll(tiles[j], 32 * j - 64 - 32 * side, 1), out)
            pack[side, g] = out
        return carry

    lax.fori_loop(0, PLANES // 4, wrap, 0)


def add_base(bx, by, main):
    def plane(g, carry):
        for j in range(4):
            i = g * 4 + j
            main[3, i] += assemble_base(bx, by, i)
        return carry

    lax.fori_loop(0, PLANES // 4, plane, 0)


def first_sweep(main, edge, rim, ua, ha, inv, hvisco, hinv, got_high, got_low):
    lane = iota((ROWS, 128), 1)
    thick = lane // 32 * 32 + 24 + lane % 8

    def unpack(g, carry):
        from_low, from_high = rim[0, g], rim[1, g]
        for j in range(4):
            i = g * 4 + j
            got = jnp.where(lane < 32, roll(from_low, -32 * j, 1), 0.0)
            got = jnp.where(lane // 32 == 1, roll(from_high, 32 - 32 * j, 1), got)
            high, low = halves(got)
            at = pl.ds(pl.multiple_of(i * ROWS, ROWS), ROWS)
            got_high[at] = high
            got_low[at] = low
            total = jnp.where(lane < 64, edge[i], 0.0) + got
            v = lanes(total, thick)
            r = 1.0 / (damping + 6.0 * v)
            hvisco[i] = v
            hinv[i] = r
            edge[i] = total
            ha[i] = total * r
        return carry

    lax.fori_loop(0, PLANES // 4, unpack, 0)

    source, col = iota((128, 256), 0), iota((128, 256), 1)
    z = col & 127
    for c in (0, 2):
        wanted = jnp.where(z < 2, z + 5, z + (33 - 126)) + (c + (col >> 7)) * 8
        ones = jnp.where((source == wanted) & ((z < 2) | (z >= 126)), 1.0, 0.0).astype(BF)
        near = dot(got_high[...], ones, NN) + dot(got_low[...], ones, NN)
        near = near.reshape(PLANES, ROWS, 256)
        main[c] += near[:, :, 0:128]
        main[c + 1] += near[:, :, 128:256]

    def start(i, carry):
        r = 1.0 / (damping + 6.0 * main[3, i])
        inv[i] = r
        for c in range(3):
            ua[c, i] = main[c, i] * r
        return carry

    lax.fori_loop(0, PLANES, start, 0, unroll=4)


def sweep(src, dst, hsrc, hdst, main, edge, inv, hvisco, hinv, first, rows):
    lane = iota((rows, 128), 1)
    at = slice(0, rows)

    def next_row(value, ref, *lead):
        return ref[(*lead, slice(1, rows + 1))] if rows < ROWS else roll(value, -1, 0)

    def plane(i, carry):
        h = hsrc[i, at]
        beside = hsrc[i - 1, at] + hsrc[i + 1, at] + roll(h, 1, 0) + next_row(h, hsrc, i) + roll(h, 1, 1) + roll(h, -1, 1)
        hdst[i, at] = (edge[i, at] + hvisco[i, at] * beside) * hinv[i, at]
        v, r = main[3, i, at], inv[i, at]
        for c in range(3):
            u = src[c, i, at]
            rim = lanes(h, jnp.where(lane == 0, c * 8 + 4, 35 + c * 8))
            before = jnp.where(lane == 0, rim, roll(u, 1, 1))
            after = jnp.where(lane == 127, rim, roll(u, -1, 1))
            beside = src[c, i - 1, at] + src[c, i + 1, at] + roll(u, 1, 0) + next_row(u, src, c, i) + before + after
            dst[c, i, at] = (main[c, i, at] + v * beside) * r
        return carry

    lax.fori_loop(first, 26 - first, plane, 0, unroll=True)


def interpolate(ub, hb, ph, pw, zt, s, scale, uh, ul, out):
    for x in range(20):
        row = jnp.concatenate([ub[0, x + 3, 0:40], ub[1, x + 3, 0:40], ub[2, x + 3, 0:40], hb[x + 3, 0:40]], axis=1)
        high, low = halves(row)
        uh[x * 40:(x + 1) * 40] = high
        ul[x * 40:(x + 1) * 40] = low
    field = uh[...].T[0:448], ul[...].T[0:448]
    z, comp = (v[0:64] for v in edge_rows())
    outside = (z < 0) | (z >= CZ)
    for pc in range(4):
        at = slice(pc * 256, (pc + 1) * 256)
        res = dot3(field, (ph[:, at], pw[:, at]), NN)
        wz = zt[0:128, at]
        rim = jnp.where(outside, zt[128:192, at] * res[384:448], 0.0)
        factor = s[4, pc, 7:8, :] * scale[1, pc:pc + 1, :]
        for c in range(3):
            value = jnp.sum(res[c * 128:(c + 1) * 128] * wz, axis=0, keepdims=True)
            value = (value + jnp.sum(jnp.where(comp == c, rim, 0.0), axis=0, keepdims=True)) * factor
            out[c, 2 * pc:2 * pc + 1, :] = value[:, 0:128]
            out[c, 2 * pc + 1:2 * pc + 2, :] = value[:, 128:256]


def step_kernel(
    cell_in, offset_in, radius_in, force_in, visc_in, live_in, base_in,
    local_in, owner_in, partner_in, mask_in,
    field_out, vel_out,
    cell, offset, radius, force, visc, alive,
    s, thick, scale, zs, q, hot_p, hot_a, tab, tab_low, mine, other, push, keys, acc, selves,
    ry, rz, xs, rx1, rx2, loads,
    ph0, pw0, ph1, pw1, zt, pfy, pfd, zh, zl,
    bx, by, main, edge, pack, rim,
    ua, ub, ha, hb, inv, hvisco, hinv, got_high, got_low, uh, ul, vel,
    in_sem, send_sem, recv_sem, out_sem,
):
    me = {a: lax.axis_index(a) for a in ("gx", "gy", "gz")}

    def near(axis, step):
        n = lax.axis_size(axis)
        return {axis: lax.rem(me[axis] + step + n, n)}

    inputs = [
        (cell_in, cell), (offset_in, offset), (radius_in, radius), (force_in, force), (visc_in, visc),
        (live_in, alive), (base_in, bx.at[pl.ds(REACH, CX)]), (local_in, q.at[0, 0]), (owner_in, q.at[0, 1]),
        (partner_in, q.at[0, 2]), (mask_in, q.at[0, 3]),
    ]
    inputs = [pltpu.make_async_copy(a, b, in_sem.at[n]) for n, (a, b) in enumerate(inputs)]
    for c in inputs:
        c.start()

    barrier = pltpu.get_barrier_semaphore()
    greeted = [("gx", 1), ("gx", -1), ("gx", 2), ("gx", -2), ("gy", 1), ("gy", -1), ("gz", 1), ("gz", -1)]
    for axis, step in greeted:
        pl.semaphore_signal(barrier, inc=1, device_id=near(axis, step), device_id_type=pl.DeviceIdType.MESH)

    count = [0]

    def copy(src, dst, axis, step):
        n = count[0]
        count[0] += 1
        return pltpu.make_async_remote_copy(
            src_ref=src, dst_ref=dst, send_sem=send_sem.at[n], recv_sem=recv_sem.at[n],
            device_id=near(axis, step), device_id_type=pl.DeviceIdType.MESH,
        )

    three, low3, high3 = pl.ds(3, 3), pl.ds(0, 3), pl.ds(6, 3)
    s_x = [copy(s.at[4], s.at[3], "gx", 1), copy(s.at[4], s.at[5], "gx", -1)]
    s_x += [copy(thick.at[4], thick.at[3], "gx", 1), copy(thick.at[4], thick.at[5], "gx", -1)]
    s_y = [copy(s.at[three], s.at[low3], "gy", 1), copy(s.at[three], s.at[high3], "gy", -1)]
    s_y += [copy(thick.at[three], thick.at[low3], "gy", 1), copy(thick.at[three], thick.at[high3], "gy", -1)]
    s_z = [copy(s.at[4], zs.at[0], "gz", 1), copy(s.at[4], zs.at[1], "gz", -1)]
    q_z = [copy(q.at[0], q.at[1], "gz", 1), copy(q.at[0], q.at[2], "gz", -1)]
    b_x = [
        copy(bx.at[pl.ds(CX, REACH)], bx.at[pl.ds(0, REACH)], "gx", 1),
        copy(bx.at[pl.ds(REACH, REACH)], bx.at[pl.ds(CX + REACH, REACH)], "gx", -1),
    ]
    b_y = [
        copy(bx.at[:, pl.ds(CY - 8, 8)], by.at[0], "gy", 1),
        copy(bx.at[:, pl.ds(0, 8)], by.at[1], "gy", -1),
    ]
    a_y = [copy(acc.at[:, pl.ds(24, 16)], ry.at[0], "gy", 1), copy(acc.at[:, pl.ds(0, 16)], ry.at[1], "gy", -1)]
    a_z = [copy(selves.at[1], rz.at[0], "gz", -1), copy(selves.at[2], rz.at[1], "gz", 1)]
    a_x = [
        copy(xs.at[pl.ds(1, 2)], rx1.at[0], "gx", 1), copy(xs.at[pl.ds(0, 2)], rx1.at[1], "gx", -1),
        copy(xs.at[2], rx2.at[0], "gx", 2), copy(xs.at[0], rx2.at[1], "gx", -2),
    ]
    l_y = [copy(loads.at[three], loads.at[low3], "gy", 1), copy(loads.at[three], loads.at[high3], "gy", -1)]
    e_z = [copy(pack.at[0], rim.at[1], "gz", -1), copy(pack.at[1], rim.at[0], "gz", 1)]

    def start(copies):
        for c in copies:
            c.start()

    def arrived(copies):
        for c in copies:
            c.wait_recv()

    for c in inputs:
        c.wait()
    flags = alive[...].astype(F32)
    rows = [offset[c] for c in range(3)] + [radius[...]] + [cell[c].astype(F32) for c in range(3)] + [flags]
    for r, v in enumerate(rows):
        for h in range(4):
            s[4, h, r:r + 1, 0:128] = v[2 * h:2 * h + 1]
            s[4, h, r:r + 1, 128:256] = v[2 * h + 1:2 * h + 2]
    for h in range(4):
        scale[1, h:h + 1, :] = envelope_scale(s, 4, h)
    for h in range(4):
        for k in range(2):
            row = slice(2 * h + k, 2 * h + k + 1)
            thick[4, row, :] = visc[row, :] * flags[row] * scale[1, h:h + 1, k * 128:(k + 1) * 128]
    pl.semaphore_wait(barrier, len(greeted))
    start(s_x)
    start(s_z)
    start(q_z)

    bx[26:28] = jnp.zeros((2, CY, CZ), F32)
    hot_rows(q, hot_p, hot_a, 0)
    find_mine(s.at[4], q, mine, 0)
    arrived(s_z)
    arrived(q_z)
    hot_rows(q, hot_p, hot_a, 1)
    find_mine(zs.at[0], q, mine, 1)
    hot_rows(q, hot_p, hot_a, 2)
    find_mine(zs.at[1], q, mine, 2)
    arrived(s_x)
    start(s_y)
    start(b_x)
    find_others(s, q, hot_p, tab, tab_low, other, (3, 4, 5), True)
    long_tables(s, 4, 0, 3, 20, ph0, pw0, zt.at[0])
    main[...] = jnp.zeros_like(main)
    edge[...] = jnp.zeros_like(edge)
    arrived(s_y)

    find_others(s, q, hot_p, tab, tab_low, other, (0, 1, 2, 6, 7, 8), False)
    push_forces(q, mine, other, push, keys)
    sum_others(push, keys, hot_p, acc)
    start(a_y)
    sum_mine(push, keys, hot_a, selves, 1)
    sum_mine(push, keys, hot_a, selves, 2)
    start(a_z)
    sum_mine(push, keys, hot_a, selves, 0)

    def side_tables(it, carry):
        long_tables(s, 3 + 2 * it, 2 * it - 1, it * 19, 7, ph1.at[it], pw1.at[it], zt.at[1 + it])
        return carry

    lax.fori_loop(0, 2, side_tables, 0)
    arrived(a_y)
    arrived(a_z)
    xs[...] = jnp.zeros_like(xs)
    for c in range(3):
        middle = acc[c, 12:24] + ry[0, c, 0:12] + ry[1, c, 0:12]
        f = force[c]
        f = jnp.concatenate(
            [jnp.concatenate([f[2 * h:2 * h + 1], f[2 * h + 1:2 * h + 2]], axis=1) for h in range(4)], axis=0
        )
        at = slice(c * 8, c * 8 + 4)
        f = f + selves[0, at] + rz[0, at] + rz[1, at]
        xs[0, c * 4:c * 4 + 4] = middle[0:4]
        xs[1, c * 4:c * 4 + 4] = middle[4:8] + f
        xs[2, c * 4:c * 4 + 4] = middle[8:12]
    start(a_x)

    def thickness(b):
        return jnp.concatenate([thick[b, t:t + 1, :] for t in range(8)], axis=1)

    def forces(b):
        return {c: line_of(loads, b, c) for c in range(3)}

    def everything(b):
        return {**forces(b), 3: thickness(b)}

    def long_all(comps, what, *out):
        def part(b):
            return {c: thickness(b) if c == 3 else line_of(loads, b, c) for c in comps}

        what(ph0, pw0, zt.at[0], part(4), *out, 3, 20)

        def side(it, carry):
            what(ph1.at[it], pw1.at[it], zt.at[1 + it], part(3 + 2 * it), *out, it * 19, 7)
            return carry

        lax.fori_loop(0, 2, side, 0, unroll=True)

    for h in range(4):
        for n in (0, 2):
            scale[n, h:h + 1, :] = envelope_scale(s, 3 + n, h)
    for n, dy in enumerate((-1, 1)):
        short_tables(s, 3 * (dy + 1) + 1, 0, dy, 3, 20, pfy.at[n], zh.at[n * 3], zl.at[n * 3])

        def corner(it, carry):
            k = n * 3 + 1 + it
            short_tables(s, 3 * (dy + 1) + 2 * it, 2 * it - 1, dy, it * 19, 7, pfd.at[n * 2 + it], zh.at[k], zl.at[k])
            return carry

        lax.fori_loop(0, 2, corner, 0)
    long_all((3,), long_one, main)
    arrived(a_x)
    for n in range(3):
        if n == 0:
            total = rx1[0, 0] + rx2[0] + xs[0]
        elif n == 1:
            total = xs[1] + rx1[0, 1] + rx1[1, 0]
        else:
            total = rx1[1, 1] + rx2[1] + xs[2]
        for h in range(4):
            on = s[3 + n, h, 7:8, :] * scale[n, h:h + 1, :]
            for c in range(3):
                loads[3 + n, c * 4 + h:c * 4 + h + 1, :] = on * total[c * 4 + h:c * 4 + h + 1]
        loads[3 + n, 12:16] = jnp.zeros((4, 256), F32)
    start(l_y)
    arrived(b_x)
    start(b_y)

    long_all(range(4), long_edge, edge)
    arrived(l_y)
    for n, dy in enumerate((-1, 1)):
        k = n * 3
        b = 3 * (dy + 1) + 1
        short_brick(pfy[n], zh.at[k], zl.at[k], everything(b), main, edge, 3, 20, R0[dy + 1])

        def corner(it, carry):
            k = n * 3 + 1 + it
            b = 3 * (dy + 1) + 2 * it
            load = everything(b)
            short_brick(pfd[n * 2 + it], zh.at[k], zl.at[k], load, main, edge, it * 19, 7, R0[dy + 1])
            return carry

        lax.fori_loop(0, 2, corner, 0, unroll=True)
    arrived(b_y)
    wrap_rims(bx, by, edge, pack)
    start(e_z)
    long_all((0, 1), long_brick, main)
    long_all((2,), long_one, main)
    add_base(bx, by, main)
    arrived(e_z)

    first_sweep(main, edge, rim, ua, ha, inv, hvisco, hinv, got_high, got_low)
    rest = (main, edge, inv, hvisco, hinv)
    sweep(ua, ub, ha, hb, *rest, 1, 48)
    sweep(ub, ua, hb, ha, *rest, 2, 40)
    sweep(ua, ub, ha, hb, *rest, 3, 40)

    def finish(x, carry):
        for c in range(3):
            ua[c, x, 0:CY] = ub[c, x + REACH, ROW0:ROW0 + CY, :]
        return carry

    lax.fori_loop(0, CX, finish, 0)
    outputs = [pltpu.make_async_copy(ua.at[:, pl.ds(0, CX), pl.ds(0, CY)], field_out, out_sem.at[0])]
    outputs[0].start()
    interpolate(ub, hb, ph0, pw0, zt.at[0], s, scale, uh, ul, vel)
    outputs.append(pltpu.make_async_copy(vel, vel_out, out_sem.at[1]))
    outputs[1].start()
    for group in (s_x, s_y, s_z, q_z, b_x, b_y, a_y, a_z, a_x, l_y, e_z):
        for c in group:
            c.wait_send()
    for c in outputs:
        c.wait()


def hand_over(field, velocity, field_out, velocity_out, here, there, sem):
    halves_of = [(c, pl.ds(n * 8, 8)) for c in range(3) for n in range(2)]
    ways = [(velocity, there, velocity_out)] + [(field.at[at], here.at[at], field_out.at[at]) for at in halves_of]
    arrive = [pltpu.make_async_copy(a, b, sem.at[0, n]) for n, (a, b, _) in enumerate(ways)]
    leave = [pltpu.make_async_copy(b, c, sem.at[1, n]) for n, (_, b, c) in enumerate(ways)]
    for c in arrive:
        c.start()
    for a, b in zip(arrive, leave):
        a.wait()
        b.start()
    for c in leave:
        c.wait()


def scratch():
    f = lambda *shape: pltpu.VMEM(shape, F32)
    i = lambda *shape: pltpu.VMEM(shape, jnp.int32)
    b = lambda *shape: pltpu.VMEM(shape, BF)
    grid = lambda *lead: pltpu.VMEM(lead + (PLANES, ROWS, 128), F32)
    sem = pltpu.SemaphoreType.DMA
    return [
        i(3, 8, 128), f(3, 8, 128), f(8, 128), f(3, 8, 128), f(8, 128), i(8, 128),
        f(9, 4, 8, 256), f(9, 8, 128), f(3, 8, 256), f(2, 4, 8, 256), i(3, 4, 32, 128),
        b(3, 256, PAIRS), b(3, 256, PAIRS), b(192, 256), b(96, 256),
        f(TILES, 8, 128), f(TILES, 8, 128), f(6, TILES, 128), i(2, TILES, 128),
        f(3, 40, 256), f(3, 24, 256),
        f(2, 3, 16, 256), f(2, 24, 256), f(3, 16, 256), f(2, 2, 16, 256), f(2, 16, 256), f(9, 16, 256),
        b(800, SLOTS), b(800, SLOTS), b(2, 280, SLOTS), b(2, 280, SLOTS), f(3, 256, SLOTS),
        f(2, 160, SLOTS), f(4, 56, SLOTS), b(6, 256, SLOTS), b(6, 256, SLOTS),
        f(PLANES, CY, CZ), f(2, PLANES, 8, CZ), grid(4), grid(), f(2, PLANES // 4, ROWS, 128), f(2, PLANES // 4, ROWS, 128),
        grid(3), grid(3), grid(), grid(), grid(), grid(), grid(), b(PLANES * ROWS, 128), b(PLANES * ROWS, 128), b(800, 512), b(800, 512), f(3, 8, 128),
        sem((11,)), sem((28,)), sem((28,)), sem((2,)),
    ]


def body(
    cell_index, cell_offset, radius, forcing, viscosity, occupied, base_viscosity,
    pair_local, pair_owner, pair_partner, pair_slot_mask,
):
    args = [a.reshape(3, 8, 128) if a.shape[0] == 3 else a.reshape(8, 128) for a in (
        cell_index, cell_offset, radius, forcing, viscosity, occupied
    )]
    args += [base_viscosity]
    args += [a.reshape(32, 128) for a in (pair_local, pair_owner, pair_partner, pair_slot_mask)]
    hbm = pl.BlockSpec(memory_space=pltpu.HBM)
    results = (
        jax.ShapeDtypeStruct((3, CX, CY, CZ), F32),
        jax.ShapeDtypeStruct((3, 8, 128), F32),
    )
    results = pl.pallas_call(
        step_kernel,
        out_shape=results,
        in_specs=[hbm] * 11,
        out_specs=(hbm,) * 2,
        scratch_shapes=scratch(),
        compiler_params=pltpu.CompilerParams(
            collective_id=0, has_side_effects=True, vmem_limit_bytes=62 * 2**20
        ),
        name="coupling",
    )(*args)
    field, velocity = pl.pallas_call(
        hand_over,
        out_shape=(
            jax.ShapeDtypeStruct((3, CX, CY, CZ), F32),
            jax.ShapeDtypeStruct((3, 8, 128), F32),
        ),
        in_specs=[hbm] * 2,
        out_specs=(hbm,) * 2,
        scratch_shapes=[
            pltpu.VMEM((3, CX, CY, CZ), F32), pltpu.VMEM((3, 8, 128), F32), pltpu.SemaphoreType.DMA((2, 7)),
        ],
        compiler_params=pltpu.CompilerParams(vmem_limit_bytes=62 * 2**20),
        name="hand_over",
    )(*results)
    return field, velocity.reshape(3, 1, 1, 1, SLOTS)


def solution(mesh):
    line = P("gx", "gy", "gz", None)
    wide = P(None, "gx", "gy", "gz", None)
    placed = (wide, wide, line, wide, line, line, P("gx", "gy", "gz"), line, line, line, line)
    return jax.shard_map(
        body,
        mesh=mesh,
        in_specs=placed,
        out_specs=(P(None, "gx", "gy", "gz"), wide),
        check_vma=False,
    )
```

```python
import functools
import jax
import jax.numpy as jnp
from jax import lax
from jax.experimental import pallas as pl
from jax.experimental.pallas import tpu as pltpu
from jax.sharding import PartitionSpec as P

spread_sigma = 0.8
damping = 0.5
lubrication_strength = 8.0
minimum_gap = 4.0
sharpness = 1.0 / (2.0 * spread_sigma * spread_sigma)

CX, CY, CZ = 16, 32, 128
SLOTS = 1024
PAIRS = 4096
TILES = 3 * PAIRS // 128
QB = 1024
REACH = 5
PLANES = 28
ROWS = 48
ROW0 = 5
BF = jnp.bfloat16
F32 = jnp.float32
NT = (((1,), (1,)), ((), ()))
NN = (((1,), (0,)), ((), ()))
TN = (((0,), (0,)), ((), ()))


def halves(value):
    high = value.astype(BF)
    return high, (value - high.astype(F32)).astype(BF)


def dot(a, b, dims):
    return lax.dot_general(a, b, dims, preferred_element_type=F32)


def dot3(a, b, dims):
    return dot(a[0], b[0], dims) + dot(a[1], b[0], dims) + dot(a[0], b[1], dims)


def iota(shape, dim):
    return lax.broadcasted_iota(jnp.int32, shape, dim)


def roll(value, shift, axis):
    shift = shift % value.shape[axis]
    return pltpu.roll(value, shift, axis) if shift else value


def lanes(value, index):
    index = jnp.broadcast_to(index, value.shape)
    return jnp.take_along_axis(value, index, axis=1, mode="promise_in_bounds")


def gauss(shift, offset):
    t = shift + 0.5 - offset
    return jnp.exp(-(t * t) * sharpness)


def norm(offset):
    total = gauss(-2.0, offset)
    for k in range(-1, 3):
        total = total + gauss(float(k), offset)
    return total


def window(cells, target, offset):
    shift = target.astype(F32) - cells
    return jnp.where(jnp.abs(shift) <= 2.0, gauss(shift, offset), 0.0)


def hot_rows(q, hot_p, hot_a, l):
    rows = iota((256, 128), 0)

    def tile(t, carry):
        for j in range(4):
            n = t * 4 + j
            at = pl.multiple_of(n * 128, 128)
            par = q[l, 2, pl.ds(n, 1), :] & 255
            loc = q[l, 0, pl.ds(n, 1), :] & 255
            hot_p[l, :, pl.ds(at, 128)] = jnp.where(rows == par, 1.0, 0.0).astype(BF)
            hot_a[l, :, pl.ds(at, 128)] = jnp.where(rows == loc, 1.0, 0.0).astype(BF)
        return carry

    lax.fori_loop(0, PAIRS // 512, tile, 0)


def row_of(q, l, j, ch):
    n = QB // 128
    return jnp.concatenate([q[l, j, pl.ds(ch * n + t, 1), :] for t in range(n)], axis=1)


def pick(found, slab, slabs, out):
    wide = jnp.broadcast_to(slab, (8, QB))
    for n, k in enumerate(slabs):
        out = jnp.where(wide == k, found[n * 8:(n + 1) * 8], out)
    return out


def find_mine(src, q, mine, l):
    def step(t, carry):
        for j in range(4):
            n = t * 4 + j
            loc = jnp.broadcast_to(q[l, 0, pl.ds(n, 1), :], (8, 128))
            index, block = loc & 127, loc >> 7
            out = jnp.zeros((8, 128), F32)
            for k in range(8):
                out = jnp.where(block == k, lanes(src[k // 2, :, k % 2 * 128:k % 2 * 128 + 128], index), out)
            mine[l * (PAIRS // 128) + n] = out
        return carry

    lax.fori_loop(0, PAIRS // 512, step, 0, unroll=4)


def codes(own):
    one = lambda c: jnp.where(c, 1, 0)
    dx = one(own >= 9) + one(own >= 18)
    rest = own - 9 * dx
    dy = one(rest >= 3) + one(rest >= 6)
    return dx, dy, rest - 3 * dy


def find_others(s, q, hot_p, tab, tab_low, other, bricks, first):
    count = len(bricks)
    for n, brick in enumerate(bricks):
        v = jnp.concatenate([s[brick, h] for h in range(4)], axis=0)
        high = v.astype(BF)
        rest = v - high.astype(F32)
        tab[n * 32:(n + 1) * 32] = high
        tab_low[n * 16:(n + 1) * 16] = jnp.concatenate([rest[h * 8:h * 8 + 4] for h in range(4)], axis=0).astype(BF)
    slabs = [b * 4 + h for b in bricks for h in range(4)]
    tiles = QB // 128

    def step(it, carry):
        l = it // (PAIRS // QB)
        ch = it % (PAIRS // QB)
        hot = hot_p[l, :, pl.ds(pl.multiple_of(ch * QB, QB), QB)]
        dx, dy, _ = codes(row_of(q, l, 1, ch))
        slab = (dy * 3 + dx) * 4 + (row_of(q, l, 2, ch) >> 8)
        if first:
            out = jnp.zeros((8, QB), F32)
        else:
            out = jnp.concatenate([other[it * tiles + t] for t in range(tiles)], axis=1)
        out = pick(dot(tab[0:count * 32], hot, NN), slab, slabs, out)
        low = pick(dot(tab_low[0:count * 16], hot, NN), slab >> 1, [k // 2 for k in slabs[::2]], jnp.zeros((8, QB), F32))
        low = jnp.where(slab & 1 == 1, low[4:8], low[0:4])
        out = out + jnp.concatenate([low, jnp.zeros((4, QB), F32)], axis=0)
        for t in range(tiles):
            other[it * tiles + t] = out[:, t * 128:(t + 1) * 128]
        return carry

    lax.fori_loop(0, 3 * PAIRS // QB, step, 0, unroll=4)


def push_forces(q, mine, other, push, keys):
    for l in range(3):
        at = slice(l * (PAIRS // 128), (l + 1) * (PAIRS // 128))
        loc, own, par, live = (q[l, j] for j in range(4))
        dx, dy, dz = codes(own)
        m = [mine[at, r, :] for r in range(8)]
        o = [other[at, r, :] for r in range(8)]
        r = [
            (o[4 + c] - m[4 + c]) + (o[c] - m[c]) + (code - 1).astype(F32) * float(side)
            for c, (code, side) in enumerate(((dx, CX), (dy, CY), (dz, CZ)))
        ]
        spacing = jnp.sqrt(r[0] * r[0] + r[1] * r[1] + r[2] * r[2])
        clearance = spacing - m[3] - o[3]
        want = (1, 2, 0)[l]
        weight = (
            jnp.where(dz == want, live, 0).astype(F32) * m[7] * o[7] * lubrication_strength
            / (jnp.maximum(spacing, 1.0) * jnp.maximum(clearance, minimum_gap))
        )
        for c in range(3):
            v = r[c] * weight
            high = v.astype(BF).astype(F32)
            push[c, at] = high
            push[3 + c, at] = v - high
        keys[0, at] = (dy * 3 + dx) * 4 + (par >> 8)
        keys[1, at] = loc >> 8


def spread_rows(push, keys, it, count):
    cols = []
    for t in range(QB // 128):
        k = it * (QB // 128) + t
        hit = iota((count, 128), 0) == keys[pl.ds(k, 1), :]
        rows = [jnp.where(hit, push[p, pl.ds(k, 1), :], 0.0) for p in range(6)]
        cols.append(jnp.concatenate(rows, axis=0).astype(BF))
    return jnp.concatenate(cols, axis=1)


def sum_others(push, keys, hot_p, acc):
    acc[...] = jnp.zeros_like(acc)

    def step(it, carry):
        l = it // (PAIRS // QB)
        at = pl.multiple_of(it % (PAIRS // QB) * QB, QB)
        sums = dot(spread_rows(push, keys.at[0], it, 40), hot_p[l, :, pl.ds(at, QB)], NT)
        acc[...] -= (sums[0:120] + sums[120:240]).reshape(3, 40, 256)
        return carry

    lax.fori_loop(0, 3 * PAIRS // QB, step, 0, unroll=4)


def sum_mine(push, keys, hot_a, selves, l):
    selves[l] = jnp.zeros((24, 256), F32)

    def step(ch, carry):
        it = l * (PAIRS // QB) + ch
        sums = dot(spread_rows(push, keys.at[1], it, 8), hot_a[l, :, pl.ds(pl.multiple_of(ch * QB, QB), QB)], NT)
        selves[l] += sums[0:24] + sums[24:48]
        return carry

    lax.fori_loop(0, PAIRS // QB, step, 0, unroll=2)


X0 = (0, 3, 19)
NXS = (7, 20, 7)
R0 = (0, 0, 34)


def edge_rows():
    line = iota((128, 1), 0)
    k = line % 8
    low = line // 32 % 2 == 0
    kept = jnp.where(low, -5 + k, 125 + k)
    sent = jnp.where(low, -3 + k, 123 + k)
    return jnp.where(line < 64, kept, sent), line // 8 % 4


def axis_tables(s, b, kc, dx, dy, x0, nx, r0, ny):
    v = s[b, kc]
    offs = [v[c:c + 1] for c in range(3)]
    cells = [v[4 + c:5 + c] for c in range(3)]
    dx_cells = jnp.asarray(dx * CX, jnp.int32).astype(F32)
    wx = window(cells[0] + dx_cells, iota((nx, 256), 0) + (x0 - REACH), offs[0])
    wy = window(cells[1] + float(dy * CY), iota((ny, 256), 0) + (r0 - ROW0), offs[1])
    wz = window(cells[2], iota((128, 256), 0), offs[2])
    eight = iota((8, 256), 0)
    wedge = [window(cells[2], eight + z, offs[2]) for z in (-5, 125, -3, 123)]
    return wx, wy, wz, [w for w in wedge for c in range(4)]


def long_tables(s, b, dx, x0, nx, ph, pw, zt):
    def chunk(kc, carry):
        wx, wy, wz, wedge = axis_tables(s, b, kc, dx, 0, x0, nx, 0, 40)
        at = pl.ds(pl.multiple_of(kc * 256, 256), 256)
        for x in range(nx):
            high, low = halves(wx[x:x + 1] * wy)
            ph[x * 40:(x + 1) * 40, at] = high
            pw[x * 40:(x + 1) * 40, at] = low
        zt[0:128, at] = wz
        zt[128:256, at] = jnp.concatenate(wedge, axis=0)
        return carry

    lax.fori_loop(0, 4, chunk, 0)


def short_tables(s, b, dx, dy, x0, nx, pf, zh, zl):
    def chunk(kc, carry):
        wx, wy, wz, wedge = axis_tables(s, b, kc, dx, dy, x0, nx, R0[dy + 1], 8)
        at = pl.ds(pl.multiple_of(kc * 256, 256), 256)
        for x in range(nx):
            pf[x * 8:(x + 1) * 8, at] = wx[x:x + 1] * wy
        high, low = halves(wz)
        zh[0:128, at] = high
        zl[0:128, at] = low
        pairs = [jnp.concatenate(wedge[n:n + 2], axis=0) for n in (0, 4, 8, 12)]
        for n, (high, low) in enumerate(halves(p) for p in pairs):
            for k in range(2):
                rows = slice(128 + n * 32 + k * 16, 128 + n * 32 + k * 16 + 16)
                zh[rows, at] = high
                zl[rows, at] = low
        return carry

    lax.fori_loop(0, 4, chunk, 0)


def envelope_scale(s, b, h):
    total = norm(s[b, h])
    return 1.0 / (total[0:1] * total[1:2] * total[2:3])


def line_of(ref, b, c):
    return jnp.concatenate([ref[b, c * 4 + h:c * 4 + h + 1, :] for h in range(4)], axis=1)


def long_brick(ph, pw, zt, load, main, x0, nx):
    d = halves(jnp.concatenate([zt[0:128, :] * v for v in load.values()], axis=0))
    res = dot3((ph[...], pw[...]), d, NT).reshape(nx, 40, 256)
    for n, c in enumerate(load):
        main[c, pl.ds(x0, nx), 0:40, :] += res[:, :, n * 128:(n + 1) * 128]


def narrow(ph, pw, d, nx):
    high, low = halves(d)
    res = dot(ph[...], jnp.concatenate([high, low], axis=0), NT)
    res = res[:, 0:128] + res[:, 128:256] + dot(pw[...], high, NT)
    return res.reshape(nx, 40, 128)


def long_one(ph, pw, zt, load, main, x0, nx):
    (c, v), = load.items()
    main[c, pl.ds(x0, nx), 0:40, :] += narrow(ph, pw, zt[0:128, :] * v, nx)


def long_edge(ph, pw, zt, load, edge, x0, nx):
    comp = edge_rows()[1]
    v = jnp.zeros((128, SLOTS), F32)
    for c, value in load.items():
        v = jnp.where(comp == c, value, v)
    edge[pl.ds(x0, nx), 0:40, :] += narrow(ph, pw, zt[128:256, :] * v, nx)


def short_brick(pf, zh, zl, load, main, edge, x0, nx, r0):
    lane = iota((nx, 8, 128), 2)
    value = jnp.concatenate([pf[...] * v for v in load.values()], axis=0)
    res = dot3(halves(value), (zh[...], zl[...]), NT).reshape(len(load), nx, 8, 256)
    rim = jnp.zeros((nx, 8, 128), F32)
    for n, c in enumerate(load):
        main[c, pl.ds(x0, nx), r0:r0 + 8, :] += res[n, :, :, 0:128]
        rim = jnp.where(lane // 8 % 4 == c, res[n, :, :, 128:256], rim)
    edge[pl.ds(x0, nx), r0:r0 + 8, :] += rim


def assemble_base(bx, by, i):
    rows = jnp.concatenate([by[0, i], bx[i], by[1, i]], axis=0)
    return roll(rows, ROW0 - 8, 0)


def wrap_rims(bx, by, edge, pack):
    lane = iota((ROWS, 128), 1)
    within = [(29, 32, 0), (56, 59, 125), (91, 96, 0), (120, 125, 123)]
    index = lane
    mask = lane < 0
    for first, last, z in within:
        inside = (lane >= first) & (lane < last)
        index = jnp.where(inside, lane - first + z, index)
        mask = mask | inside

    def wrap(g, carry):
        tiles = []
        for j in range(4):
            i = g * 4 + j
            b = assemble_base(bx, by, i)
            t = edge[i] + jnp.where(mask, lanes(b, index), 0.0)
            edge[i] = t
            tiles.append(t)
        for side in range(2):
            out = jnp.zeros((ROWS, 128), F32)
            for j in range(4):
                out = jnp.where(lane // 32 == j, roll(tiles[j], 32 * j - 64 - 32 * side, 1), out)
            pack[side, g] = out
        return carry

    lax.fori_loop(0, PLANES // 4, wrap, 0)


def add_base(bx, by, main):
    def plane(g, carry):
        for j in range(4):
            i = g * 4 + j
            main[3, i] += assemble_base(bx, by, i)
        return carry

    lax.fori_loop(0, PLANES // 4, plane, 0)


def first_sweep(main, edge, rim, ua, ha, inv, hvisco, hinv, got_high, got_low):
    lane = iota((ROWS, 128), 1)
    thick = lane // 32 * 32 + 24 + lane % 8

    def unpack(g, carry):
        from_low, from_high = rim[0, g], rim[1, g]
        for j in range(4):
            i = g * 4 + j
            got = jnp.where(lane < 32, roll(from_low, -32 * j, 1), 0.0)
            got = jnp.where(lane // 32 == 1, roll(from_high, 32 - 32 * j, 1), got)
            high, low = halves(got)
            at = pl.ds(pl.multiple_of(i * ROWS, ROWS), ROWS)
            got_high[at] = high
            got_low[at] = low
            total = jnp.where(lane < 64, edge[i], 0.0) + got
            v = lanes(total, thick)
            r = 1.0 / (damping + 6.0 * v)
            hvisco[i] = v
            hinv[i] = r
            edge[i] = total
            ha[i] = total * r
        return carry

    lax.fori_loop(0, PLANES // 4, unpack, 0)

    source, col = iota((128, 256), 0), iota((128, 256), 1)
    z = col & 127
    for c in (0, 2):
        wanted = jnp.where(z < 2, z + 5, z + (33 - 126)) + (c + (col >> 7)) * 8
        ones = jnp.where((source == wanted) & ((z < 2) | (z >= 126)), 1.0, 0.0).astype(BF)
        near = dot(got_high[...], ones, NN) + dot(got_low[...], ones, NN)
        near = near.reshape(PLANES, ROWS, 256)
        main[c] += near[:, :, 0:128]
        main[c + 1] += near[:, :, 128:256]

    def start(i, carry):
        r = 1.0 / (damping + 6.0 * main[3, i])
        inv[i] = r
        for c in range(3):
            ua[c, i] = main[c, i] * r
        return carry

    lax.fori_loop(0, PLANES, start, 0, unroll=4)


def sweep(src, dst, hsrc, hdst, main, edge, inv, hvisco, hinv, first, rows):
    lane = iota((rows, 128), 1)
    at = slice(0, rows)

    def next_row(value, ref, *lead):
        return ref[(*lead, slice(1, rows + 1))] if rows < ROWS else roll(value, -1, 0)

    def plane(i, carry):
        h = hsrc[i, at]
        beside = hsrc[i - 1, at] + hsrc[i + 1, at] + roll(h, 1, 0) + next_row(h, hsrc, i) + roll(h, 1, 1) + roll(h, -1, 1)
        hdst[i, at] = (edge[i, at] + hvisco[i, at] * beside) * hinv[i, at]
        v, r = main[3, i, at], inv[i, at]
        for c in range(3):
            u = src[c, i, at]
            rim = lanes(h, jnp.where(lane == 0, c * 8 + 4, 35 + c * 8))
            before = jnp.where(lane == 0, rim, roll(u, 1, 1))
            after = jnp.where(lane == 127, rim, roll(u, -1, 1))
            beside = src[c, i - 1, at] + src[c, i + 1, at] + roll(u, 1, 0) + next_row(u, src, c, i) + before + after
            dst[c, i, at] = (main[c, i, at] + v * beside) * r
        return carry

    lax.fori_loop(first, 26 - first, plane, 0, unroll=True)


def interpolate(ub, hb, ph, pw, zt, s, scale, uh, ul, out):
    for x in range(20):
        row = jnp.concatenate([ub[0, x + 3, 0:40], ub[1, x + 3, 0:40], ub[2, x + 3, 0:40], hb[x + 3, 0:40]], axis=1)
        high, low = halves(row)
        uh[x * 40:(x + 1) * 40] = high
        ul[x * 40:(x + 1) * 40] = low
    field = uh[...].T[0:448], ul[...].T[0:448]
    z, comp = (v[0:64] for v in edge_rows())
    outside = (z < 0) | (z >= CZ)
    for pc in range(4):
        at = slice(pc * 256, (pc + 1) * 256)
        res = dot3(field, (ph[:, at], pw[:, at]), NN)
        wz = zt[0:128, at]
        rim = jnp.where(outside, zt[128:192, at] * res[384:448], 0.0)
        factor = s[4, pc, 7:8, :] * scale[1, pc:pc + 1, :]
        for c in range(3):
            value = jnp.sum(res[c * 128:(c + 1) * 128] * wz, axis=0, keepdims=True)
            value = (value + jnp.sum(jnp.where(comp == c, rim, 0.0), axis=0, keepdims=True)) * factor
            out[c, 2 * pc:2 * pc + 1, :] = value[:, 0:128]
            out[c, 2 * pc + 1:2 * pc + 2, :] = value[:, 128:256]


def step_kernel(
    cell_in, offset_in, radius_in, force_in, visc_in, live_in, base_in,
    local_in, owner_in, partner_in, mask_in,
    field_out, vel_out,
    cell, offset, radius, force, visc, alive,
    s, thick, scale, zs, q, hot_p, hot_a, tab, tab_low, mine, other, push, keys, acc, selves,
    ry, rz, xs, rx1, rx2, loads,
    ph0, pw0, ph1, pw1, zt, pfy, pfd, zh, zl,
    bx, by, main, edge, pack, rim,
    ua, ub, ha, hb, inv, hvisco, hinv, got_high, got_low, uh, ul, vel,
    in_sem, send_sem, recv_sem, out_sem,
):
    me = {a: lax.axis_index(a) for a in ("gx", "gy", "gz")}

    def near(axis, step):
        n = lax.axis_size(axis)
        return {axis: lax.rem(me[axis] + step + n, n)}

    inputs = [
        (cell_in, cell), (offset_in, offset), (radius_in, radius), (force_in, force), (visc_in, visc),
        (live_in, alive), (base_in, bx.at[pl.ds(REACH, CX)]), (local_in, q.at[0, 0]), (owner_in, q.at[0, 1]),
        (partner_in, q.at[0, 2]), (mask_in, q.at[0, 3]),
    ]
    inputs = [pltpu.make_async_copy(a, b, in_sem.at[n]) for n, (a, b) in enumerate(inputs)]
    for c in inputs:
        c.start()

    barrier = pltpu.get_barrier_semaphore()
    greeted = [("gx", 1), ("gx", -1), ("gx", 2), ("gx", -2), ("gy", 1), ("gy", -1), ("gz", 1), ("gz", -1)]
    for axis, step in greeted:
        pl.semaphore_signal(barrier, inc=1, device_id=near(axis, step), device_id_type=pl.DeviceIdType.MESH)

    count = [0]

    def copy(src, dst, axis, step):
        n = count[0]
        count[0] += 1
        return pltpu.make_async_remote_copy(
            src_ref=src, dst_ref=dst, send_sem=send_sem.at[n], recv_sem=recv_sem.at[n],
            device_id=near(axis, step), device_id_type=pl.DeviceIdType.MESH,
        )

    three, low3, high3 = pl.ds(3, 3), pl.ds(0, 3), pl.ds(6, 3)
    s_x = [copy(s.at[4], s.at[3], "gx", 1), copy(s.at[4], s.at[5], "gx", -1)]
    s_x += [copy(thick.at[4], thick.at[3], "gx", 1), copy(thick.at[4], thick.at[5], "gx", -1)]
    s_y = [copy(s.at[three], s.at[low3], "gy", 1), copy(s.at[three], s.at[high3], "gy", -1)]
    s_y += [copy(thick.at[three], thick.at[low3], "gy", 1), copy(thick.at[three], thick.at[high3], "gy", -1)]
    s_z = [copy(s.at[4], zs.at[0], "gz", 1), copy(s.at[4], zs.at[1], "gz", -1)]
    q_z = [copy(q.at[0], q.at[1], "gz", 1), copy(q.at[0], q.at[2], "gz", -1)]
    b_x = [
        copy(bx.at[pl.ds(CX, REACH)], bx.at[pl.ds(0, REACH)], "gx", 1),
        copy(bx.at[pl.ds(REACH, REACH)], bx.at[pl.ds(CX + REACH, REACH)], "gx", -1),
    ]
    def base_rows(planes):
        return [
            copy(bx.at[planes, pl.ds(CY - 8, 8)], by.at[0, planes], "gy", 1),
            copy(bx.at[planes, pl.ds(0, 8)], by.at[1, planes], "gy", -1),
        ]

    b_own = base_rows(pl.ds(REACH, CX))
    b_far = base_rows(pl.ds(0, REACH)) + base_rows(pl.ds(REACH + CX, PLANES - REACH - CX))
    a_y = [copy(acc.at[:, pl.ds(24, 16)], ry.at[0], "gy", 1), copy(acc.at[:, pl.ds(0, 16)], ry.at[1], "gy", -1)]
    a_z = [copy(selves.at[1], rz.at[0], "gz", -1), copy(selves.at[2], rz.at[1], "gz", 1)]
    a_x = [
        copy(xs.at[pl.ds(1, 2)], rx1.at[0], "gx", 1), copy(xs.at[pl.ds(0, 2)], rx1.at[1], "gx", -1),
        copy(xs.at[2], rx2.at[0], "gx", 2), copy(xs.at[0], rx2.at[1], "gx", -2),
    ]
    l_y = [copy(loads.at[three], loads.at[low3], "gy", 1), copy(loads.at[three], loads.at[high3], "gy", -1)]
    e_z = [copy(pack.at[0], rim.at[1], "gz", -1), copy(pack.at[1], rim.at[0], "gz", 1)]

    def start(copies):
        for c in copies:
            c.start()

    def arrived(copies):
        for c in copies:
            c.wait_recv()

    for c in inputs:
        c.wait()
    flags = alive[...].astype(F32)
    rows = [offset[c] for c in range(3)] + [radius[...]] + [cell[c].astype(F32) for c in range(3)] + [flags]
    for r, v in enumerate(rows):
        for h in range(4):
            s[4, h, r:r + 1, 0:128] = v[2 * h:2 * h + 1]
            s[4, h, r:r + 1, 128:256] = v[2 * h + 1:2 * h + 2]
    for h in range(4):
        scale[1, h:h + 1, :] = envelope_scale(s, 4, h)
    for h in range(4):
        for k in range(2):
            row = slice(2 * h + k, 2 * h + k + 1)
            thick[4, row, :] = visc[row, :] * flags[row] * scale[1, h:h + 1, k * 128:(k + 1) * 128]
    pl.semaphore_wait(barrier, len(greeted))
    start(s_x)
    start(s_z)
    start(q_z)
    start(b_own)

    bx[26:28] = jnp.zeros((2, CY, CZ), F32)
    hot_rows(q, hot_p, hot_a, 0)
    find_mine(s.at[4], q, mine, 0)
    arrived(s_z)
    arrived(q_z)
    hot_rows(q, hot_p, hot_a, 1)
    find_mine(zs.at[0], q, mine, 1)
    hot_rows(q, hot_p, hot_a, 2)
    find_mine(zs.at[1], q, mine, 2)
    arrived(s_x)
    start(s_y)
    find_others(s, q, hot_p, tab, tab_low, other, (3, 4, 5), True)
    long_tables(s, 4, 0, 3, 20, ph0, pw0, zt.at[0])
    main[...] = jnp.zeros_like(main)
    edge[...] = jnp.zeros_like(edge)
    arrived(s_y)
    start(b_x)

    find_others(s, q, hot_p, tab, tab_low, other, (0, 1, 2, 6, 7, 8), False)
    push_forces(q, mine, other, push, keys)
    sum_others(push, keys, hot_p, acc)
    start(a_y)
    sum_mine(push, keys, hot_a, selves, 1)
    sum_mine(push, keys, hot_a, selves, 2)
    start(a_z)
    sum_mine(push, keys, hot_a, selves, 0)

    def side_tables(it, carry):
        long_tables(s, 3 + 2 * it, 2 * it - 1, it * 19, 7, ph1.at[it], pw1.at[it], zt.at[1 + it])
        return carry

    lax.fori_loop(0, 2, side_tables, 0)
    arrived(a_y)
    arrived(a_z)
    xs[...] = jnp.zeros_like(xs)
    for c in range(3):
        middle = acc[c, 12:24] + ry[0, c, 0:12] + ry[1, c, 0:12]
        f = force[c]
        f = jnp.concatenate(
            [jnp.concatenate([f[2 * h:2 * h + 1], f[2 * h + 1:2 * h + 2]], axis=1) for h in range(4)], axis=0
        )
        at = slice(c * 8, c * 8 + 4)
        f = f + selves[0, at] + rz[0, at] + rz[1, at]
        xs[0, c * 4:c * 4 + 4] = middle[0:4]
        xs[1, c * 4:c * 4 + 4] = middle[4:8] + f
        xs[2, c * 4:c * 4 + 4] = middle[8:12]
    start(a_x)

    def thickness(b):
        return jnp.concatenate([thick[b, t:t + 1, :] for t in range(8)], axis=1)

    def forces(b):
        return {c: line_of(loads, b, c) for c in range(3)}

    def everything(b):
        return {**forces(b), 3: thickness(b)}

    def long_all(comps, what, *out):
        def part(b):
            return {c: thickness(b) if c == 3 else line_of(loads, b, c) for c in comps}

        what(ph0, pw0, zt.at[0], part(4), *out, 3, 20)

        def side(it, carry):
            what(ph1.at[it], pw1.at[it], zt.at[1 + it], part(3 + 2 * it), *out, it * 19, 7)
            return carry

        lax.fori_loop(0, 2, side, 0, unroll=True)

    for h in range(4):
        for n in (0, 2):
            scale[n, h:h + 1, :] = envelope_scale(s, 3 + n, h)
    for n, dy in enumerate((-1, 1)):
        short_tables(s, 3 * (dy + 1) + 1, 0, dy, 3, 20, pfy.at[n], zh.at[n * 3], zl.at[n * 3])

        def corner(it, carry):
            k = n * 3 + 1 + it
            short_tables(s, 3 * (dy + 1) + 2 * it, 2 * it - 1, dy, it * 19, 7, pfd.at[n * 2 + it], zh.at[k], zl.at[k])
            return carry

        lax.fori_loop(0, 2, corner, 0)
    long_all((3,), long_one, main)
    arrived(a_x)
    for n in range(3):
        if n == 0:
            total = rx1[0, 0] + rx2[0] + xs[0]
        elif n == 1:
            total = xs[1] + rx1[0, 1] + rx1[1, 0]
        else:
            total = rx1[1, 1] + rx2[1] + xs[2]
        for h in range(4):
            on = s[3 + n, h, 7:8, :] * scale[n, h:h + 1, :]
            for c in range(3):
                loads[3 + n, c * 4 + h:c * 4 + h + 1, :] = on * total[c * 4 + h:c * 4 + h + 1]
        loads[3 + n, 12:16] = jnp.zeros((4, 256), F32)
    start(l_y)
    arrived(b_x)
    start(b_far)

    long_all(range(4), long_edge, edge)
    arrived(l_y)
    for n, dy in enumerate((-1, 1)):
        k = n * 3
        b = 3 * (dy + 1) + 1
        short_brick(pfy[n], zh.at[k], zl.at[k], everything(b), main, edge, 3, 20, R0[dy + 1])

        def corner(it, carry):
            k = n * 3 + 1 + it
            b = 3 * (dy + 1) + 2 * it
            load = everything(b)
            short_brick(pfd[n * 2 + it], zh.at[k], zl.at[k], load, main, edge, it * 19, 7, R0[dy + 1])
            return carry

        lax.fori_loop(0, 2, corner, 0, unroll=True)
    arrived(b_own)
    arrived(b_far)
    wrap_rims(bx, by, edge, pack)
    start(e_z)
    long_all((0, 1), long_brick, main)
    long_all((2,), long_one, main)
    add_base(bx, by, main)
    arrived(e_z)

    first_sweep(main, edge, rim, ua, ha, inv, hvisco, hinv, got_high, got_low)
    rest = (main, edge, inv, hvisco, hinv)
    sweep(ua, ub, ha, hb, *rest, 1, 48)
    sweep(ub, ua, hb, ha, *rest, 2, 40)
    sweep(ua, ub, ha, hb, *rest, 3, 40)

    def finish(x, carry):
        for c in range(3):
            ua[c, x, 0:CY] = ub[c, x + REACH, ROW0:ROW0 + CY, :]
        return carry

    lax.fori_loop(0, CX, finish, 0)
    outputs = [pltpu.make_async_copy(ua.at[:, pl.ds(0, CX), pl.ds(0, CY)], field_out, out_sem.at[0])]
    outputs[0].start()
    interpolate(ub, hb, ph0, pw0, zt.at[0], s, scale, uh, ul, vel)
    outputs.append(pltpu.make_async_copy(vel, vel_out, out_sem.at[1]))
    outputs[1].start()
    for group in (s_x, s_y, s_z, q_z, b_x, b_own, b_far, a_y, a_z, a_x, l_y, e_z):
        for c in group:
            c.wait_send()
    for c in outputs:
        c.wait()


def hand_over(field, velocity, field_out, velocity_out, here, there, sem):
    halves_of = [(c, pl.ds(n * 8, 8)) for c in range(3) for n in range(2)]
    ways = [(velocity, there, velocity_out)] + [(field.at[at], here.at[at], field_out.at[at]) for at in halves_of]
    arrive = [pltpu.make_async_copy(a, b, sem.at[0, n]) for n, (a, b, _) in enumerate(ways)]
    leave = [pltpu.make_async_copy(b, c, sem.at[1, n]) for n, (_, b, c) in enumerate(ways)]
    for c in arrive:
        c.start()
    for a, b in zip(arrive, leave):
        a.wait()
        b.start()
    for c in leave:
        c.wait()


def scratch():
    f = lambda *shape: pltpu.VMEM(shape, F32)
    i = lambda *shape: pltpu.VMEM(shape, jnp.int32)
    b = lambda *shape: pltpu.VMEM(shape, BF)
    grid = lambda *lead: pltpu.VMEM(lead + (PLANES, ROWS, 128), F32)
    sem = pltpu.SemaphoreType.DMA
    return [
        i(3, 8, 128), f(3, 8, 128), f(8, 128), f(3, 8, 128), f(8, 128), i(8, 128),
        f(9, 4, 8, 256), f(9, 8, 128), f(3, 8, 256), f(2, 4, 8, 256), i(3, 4, 32, 128),
        b(3, 256, PAIRS), b(3, 256, PAIRS), b(192, 256), b(96, 256),
        f(TILES, 8, 128), f(TILES, 8, 128), f(6, TILES, 128), i(2, TILES, 128),
        f(3, 40, 256), f(3, 24, 256),
        f(2, 3, 16, 256), f(2, 24, 256), f(3, 16, 256), f(2, 2, 16, 256), f(2, 16, 256), f(9, 16, 256),
        b(800, SLOTS), b(800, SLOTS), b(2, 280, SLOTS), b(2, 280, SLOTS), f(3, 256, SLOTS),
        f(2, 160, SLOTS), f(4, 56, SLOTS), b(6, 256, SLOTS), b(6, 256, SLOTS),
        f(PLANES, CY, CZ), f(2, PLANES, 8, CZ), grid(4), grid(), f(2, PLANES // 4, ROWS, 128), f(2, PLANES // 4, ROWS, 128),
        grid(3), grid(3), grid(), grid(), grid(), grid(), grid(), b(PLANES * ROWS, 128), b(PLANES * ROWS, 128), b(800, 512), b(800, 512), f(3, 8, 128),
        sem((11,)), sem((32,)), sem((32,)), sem((2,)),
    ]


def body(
    cell_index, cell_offset, radius, forcing, viscosity, occupied, base_viscosity,
    pair_local, pair_owner, pair_partner, pair_slot_mask,
):
    args = [a.reshape(3, 8, 128) if a.shape[0] == 3 else a.reshape(8, 128) for a in (
        cell_index, cell_offset, radius, forcing, viscosity, occupied
    )]
    args += [base_viscosity]
    args += [a.reshape(32, 128) for a in (pair_local, pair_owner, pair_partner, pair_slot_mask)]
    hbm = pl.BlockSpec(memory_space=pltpu.HBM)
    results = (
        jax.ShapeDtypeStruct((3, CX, CY, CZ), F32),
        jax.ShapeDtypeStruct((3, 8, 128), F32),
    )
    results = pl.pallas_call(
        step_kernel,
        out_shape=results,
        in_specs=[hbm] * 11,
        out_specs=(hbm,) * 2,
        scratch_shapes=scratch(),
        compiler_params=pltpu.CompilerParams(
            collective_id=0, has_side_effects=True, vmem_limit_bytes=62 * 2**20
        ),
        name="coupling",
    )(*args)
    field, velocity = pl.pallas_call(
        hand_over,
        out_shape=(
            jax.ShapeDtypeStruct((3, CX, CY, CZ), F32),
            jax.ShapeDtypeStruct((3, 8, 128), F32),
        ),
        in_specs=[hbm] * 2,
        out_specs=(hbm,) * 2,
        scratch_shapes=[
            pltpu.VMEM((3, CX, CY, CZ), F32), pltpu.VMEM((3, 8, 128), F32), pltpu.SemaphoreType.DMA((2, 7)),
        ],
        compiler_params=pltpu.CompilerParams(vmem_limit_bytes=62 * 2**20),
        name="hand_over",
    )(*results)
    return field, velocity.reshape(3, 1, 1, 1, SLOTS)


def solution(mesh):
    line = P("gx", "gy", "gz", None)
    wide = P(None, "gx", "gy", "gz", None)
    placed = (wide, wide, line, wide, line, line, P("gx", "gy", "gz"), line, line, line, line)
    return jax.shard_map(
        body,
        mesh=mesh,
        in_specs=placed,
        out_specs=(P(None, "gx", "gy", "gz"), wide),
        check_vma=False,
    )
```
